32 devices in a mesh: ctx: 2 (over x), tp: 4 (over z), dp: 4 (over y, core).
Axes of the slice: x: 2, y: 2, z: 4, core: 2. Of those that a mesh axis runs over, the one named last changes fastest.
Arguments:
- trailing_questions: bfloat16 [1024, 8192], P(('dp', 'ctx'), 'tp'), parts along dimension 0, may hold values from -6 to 6
- output_gradient: bfloat16 [1024, 8192], P(('dp', 'ctx'), 'tp'), parts along dimension 0, may hold values from -6 to 6
- tail_row_key: bfloat16 [1024, 1024], P(('dp', 'ctx'), 'tp'), parts along dimension 0, may hold values from -6 to 6
- tail_row_value: bfloat16 [1024, 1024], P(('dp', 'ctx'), 'tp'), parts along dimension 0, may hold values from -6 to 6
- passage_key_cache: bfloat16 [2048, 1024], P(('dp', 'ctx'), 'tp'), parts along dimension 0, may hold values from -6 to 6
- passage_value_cache: bfloat16 [2048, 1024], P(('dp', 'ctx'), 'tp'), parts along dimension 0, may hold values from -6 to 6
- row_list: int32 [1024], P(('dp', 'ctx')), parts along dimension 0, may hold values from 0 to 1, as said below
- read_owner: int32 [8, 24], P(('dp', 'ctx')), parts along dimension 0, may hold values from 0 to 1, as said below
- read_tile: int32 [8, 24], P(('dp', 'ctx')), parts along dimension 0, may hold values from 0 to 1
- read_list: int32 [8, 24], P(('dp', 'ctx')), parts along dimension 0, may hold values from 0 to 1
- read_count: int32 [8], P(('dp', 'ctx')), parts along dimension 0, may hold values from 12 to 24, as said below
Outputs:
- grad_query: bfloat16 [1024, 8192], P(('dp', 'ctx'), 'tp'), parts along dimension 0
- grad_tail_key: bfloat16 [1024, 1024], P(('dp', 'ctx'), 'tp'), parts along dimension 0
- grad_tail_value: bfloat16 [1024, 1024], P(('dp', 'ctx'), 'tp'), parts along dimension 0
- grad_key_cache: float32 [2048, 1024], P(('dp', 'ctx'), 'tp'), parts along dimension 0
- grad_value_cache: float32 [2048, 1024], P(('dp', 'ctx'), 'tp'), parts along dimension 0
The draws below stay inside these ranges and needn't reach their ends.
There are 4 independent parts, one for each index of `dp`. The reference program is written for one: setup_inputs(seed, part) draws one part's arguments, and reference() takes and returns one part's arrays. A program takes and returns all parts, laid end to end along the dimension named above; each array names one. Nothing has to cross between parts.
Inputs may be any that keep to these rules, and one draw needn't show every extreme that they name: `row_list`: on each reader's 128 rows the list number is 0 on a first run and 1 on the rest; both runs are nonempty. `read_owner`: a reader names one owner at most 12 times, and every reader names some owner exactly 12 times. `read_count`: some reader has all 24 reads live.
All inputs are finite; a program needn't handle non-finite values.
Results may differ from the reference program's by a relative error of at most 0.012.
Values may be sent and summed in bfloat16 or wider, within the bound.
No kernel may reach another device: no remote copies, remote signals or barrier semaphores. Data moves between devices by JAX's collectives and lax.ppermute only.
A program may use at most 64 MiB of HBM per device.

```python
import math
import jax
import jax.numpy as jnp
from jax import lax

QUERY_HEADS = 64
MEMORY_CHANNELS = 8
ATTN_WIDTH = 128
SUFFIX_LINES = 128
SEGMENT_FETCHES = 24
OWNED_TILES = 2
SEGMENT_LENGTH = 128
LISTS = 2
TAIL_ROWS = 256
CACHED_TOKENS = 512
N_CTX = 2


def draw_trailing_questions(key, part):
    query_group_size = QUERY_HEADS // MEMORY_CHANNELS
    complete_shape = (TAIL_ROWS, MEMORY_CHANNELS, query_group_size, ATTN_WIDTH)
    offset_start = jnp.clip(jax.random.normal(jax.random.fold_in(key, 1), complete_shape, jnp.float32), -6.0, 6.0)
    return offset_start.reshape(TAIL_ROWS, QUERY_HEADS * ATTN_WIDTH).astype(jnp.bfloat16)


def draw_tail_row_key(key, part):
    complete_shape = (TAIL_ROWS, MEMORY_CHANNELS, ATTN_WIDTH)
    offset_start = jnp.clip(jax.random.normal(jax.random.fold_in(key, 2), complete_shape, jnp.float32), -6.0, 6.0)
    return offset_start.reshape(TAIL_ROWS, MEMORY_CHANNELS * ATTN_WIDTH).astype(jnp.bfloat16)


def draw_row_list(key, part):
    cut_rows = jax.random.randint(jax.random.fold_in(key, 3), (N_CTX, 1), 1, SUFFIX_LINES)
    local_rows = jnp.arange(SUFFIX_LINES)[None, :]
    return (local_rows >= cut_rows).astype(jnp.int32).reshape(TAIL_ROWS)


def one_order(subkey):
    owner_order = jax.random.permutation(jax.random.fold_in(subkey, 1), N_CTX)
    column_order = jax.random.permutation(jax.random.fold_in(subkey, 2), SEGMENT_FETCHES)
    return owner_order[column_order % N_CTX]


def draw_read_owner(key, part):
    subkeys = jax.random.split(jax.random.fold_in(key, 4), N_CTX)
    return jax.vmap(one_order)(subkeys).astype(jnp.int32)


def draw_read_count(key, part):
    counts = jax.random.randint(jax.random.fold_in(key, 5), (N_CTX,), SEGMENT_FETCHES // 2, SEGMENT_FETCHES + 1)
    return jnp.where(jnp.arange(N_CTX) == 0, SEGMENT_FETCHES, counts).astype(jnp.int32)


def place_ends(array, key, smallest, largest):
    extent = array.shape
    spot = [jax.random.randint(jax.random.fold_in(key, axis), (), 0, extent[axis]) for axis in range(len(extent))]
    array = array.at[tuple(spot)].set(smallest)
    longest = extent.index(max(extent))
    spot[longest] = (spot[longest] + 1) % extent[longest]
    return array.at[tuple(spot)].set(largest)


def block_levels(stream_key, extent, shards, smallest, largest):
    level = 1.0
    for axis_at, shards_of in shards:
        steps = jax.random.uniform(jax.random.fold_in(jax.random.fold_in(stream_key, 6), axis_at), (shards_of,), jnp.float32, smallest / len(shards), largest / len(shards))
        level = level * jnp.repeat(jnp.exp(steps), extent[axis_at] // shards_of).reshape((-1,) + (1,) * (len(extent) - 1 - axis_at))
    return level


def bell_draw(key, shape, spread, reach, shards=(), dtype=jnp.bfloat16):
    array = jax.random.normal(key, shape, jnp.float32) * spread
    if len(shards) > 0:
        array = block_levels(key, shape, shards, -0.22, 0.18) * array
    return jnp.clip(array, min=-reach, max=reach).astype(dtype)


def setup_inputs(seed: int = 0, part: int = 0) -> dict:
    arg_keys = jax.random.split(jax.random.key(seed), 12)
    part_splits = jax.random.split(jax.random.fold_in(arg_keys[11], part), 12)
    trailing_questions = draw_trailing_questions(jax.random.fold_in(jax.random.fold_in(arg_keys[11], part), 71), part)
    output_gradient = bell_draw(part_splits[1], (TAIL_ROWS, QUERY_HEADS * ATTN_WIDTH), 1.0, 6.0, ((0, 2), (1, 4)))
    tail_row_key = draw_tail_row_key(jax.random.fold_in(jax.random.fold_in(arg_keys[11], part), 71), part)
    tail_row_value = bell_draw(part_splits[3], (TAIL_ROWS, MEMORY_CHANNELS * ATTN_WIDTH), 1.0, 6.0, ((0, 2), (1, 4)))
    passage_key_cache = bell_draw(part_splits[4], (CACHED_TOKENS, MEMORY_CHANNELS * ATTN_WIDTH), 1.0, 6.0, ((0, 2), (1, 4)))
    passage_value_cache = bell_draw(part_splits[5], (CACHED_TOKENS, MEMORY_CHANNELS * ATTN_WIDTH), 1.0, 6.0, ((0, 2), (1, 4)))
    row_list = draw_row_list(jax.random.fold_in(jax.random.fold_in(arg_keys[11], part), 71), part)
    read_owner = draw_read_owner(jax.random.fold_in(jax.random.fold_in(arg_keys[11], part), 71), part)
    read_tile = place_ends(jax.random.randint(part_splits[8], (N_CTX, SEGMENT_FETCHES), 0, OWNED_TILES), jax.random.fold_in(part_splits[8], 1), 0, OWNED_TILES - 1).astype(jnp.int32)
    read_list = place_ends(jax.random.randint(part_splits[9], (N_CTX, SEGMENT_FETCHES), 0, LISTS), jax.random.fold_in(part_splits[9], 1), 0, LISTS - 1).astype(jnp.int32)
    read_count = draw_read_count(jax.random.fold_in(jax.random.fold_in(arg_keys[11], part), 71), part)
    return {"trailing_questions": trailing_questions, "output_gradient": output_gradient, "tail_row_key": tail_row_key, "tail_row_value": tail_row_value, "passage_key_cache": passage_key_cache, "passage_value_cache": passage_value_cache, "row_list": row_list, "read_owner": read_owner, "read_tile": read_tile, "read_list": read_list, "read_count": read_count}


NEG_FILL = -1e+30

def reference(trailing_questions, output_gradient, tail_row_key, tail_row_value, passage_key_cache, passage_value_cache, row_list, read_owner, read_tile, read_list, read_count):
    query_group_size = QUERY_HEADS // MEMORY_CHANNELS
    sharpness_scale = 1.0 / math.sqrt(ATTN_WIDTH)
    stored_keys = passage_key_cache.reshape(N_CTX * OWNED_TILES, SEGMENT_LENGTH, MEMORY_CHANNELS, ATTN_WIDTH)
    stored_values = passage_value_cache.reshape(N_CTX * OWNED_TILES, SEGMENT_LENGTH, MEMORY_CHANNELS, ATTN_WIDTH)

    def one_reader(loop_accumulator, reader):
        running_keys, running_values = loop_accumulator
        begin_index = (reader * SUFFIX_LINES).astype(jnp.int32)
        asking_matrix = lax.dynamic_slice_in_dim(trailing_questions, begin_index, SUFFIX_LINES, 0).reshape(SUFFIX_LINES, MEMORY_CHANNELS, query_group_size, ATTN_WIDTH).astype(jnp.float32)
        result_cotangents = lax.dynamic_slice_in_dim(output_gradient, begin_index, SUFFIX_LINES, 0).reshape(SUFFIX_LINES, MEMORY_CHANNELS, query_group_size, ATTN_WIDTH).astype(jnp.float32)
        ending_keys = lax.dynamic_slice_in_dim(tail_row_key, begin_index, SUFFIX_LINES, 0).reshape(SUFFIX_LINES, MEMORY_CHANNELS, ATTN_WIDTH)
        ending_values = lax.dynamic_slice_in_dim(tail_row_value, begin_index, SUFFIX_LINES, 0).reshape(SUFFIX_LINES, MEMORY_CHANNELS, ATTN_WIDTH)
        own_list = lax.dynamic_slice_in_dim(row_list, begin_index, SUFFIX_LINES, 0)
        overall_tile = (read_owner[reader] * OWNED_TILES + read_tile[reader]).astype(jnp.int32)
        remote_keys = jnp.take(stored_keys, overall_tile, axis=0).reshape(SEGMENT_FETCHES * SEGMENT_LENGTH, MEMORY_CHANNELS, ATTN_WIDTH)
        remote_values = jnp.take(stored_values, overall_tile, axis=0).reshape(SEGMENT_FETCHES * SEGMENT_LENGTH, MEMORY_CHANNELS, ATTN_WIDTH)
        every_address_vector = jnp.concatenate([ending_keys, remote_keys], axis=0).astype(jnp.float32)
        all_values = jnp.concatenate([ending_values, remote_values], axis=0).astype(jnp.float32)
        positions = jnp.arange(SUFFIX_LINES)
        tail_allowed = (own_list[:, None] == own_list[None, :]) & (positions[None, :] <= positions[:, None])
        key_lists = jnp.repeat(read_list[reader], SEGMENT_LENGTH)
        key_live = jnp.repeat(jnp.arange(SEGMENT_FETCHES) < read_count[reader], SEGMENT_LENGTH)
        far_allowed = (own_list[:, None] == key_lists[None, :]) & key_live[None, :]
        permitted_mask = jnp.concatenate([tail_allowed, far_allowed], axis=1)
        similarity_matrix = jnp.einsum('sjvf,ijf->jvsi', asking_matrix, every_address_vector) * sharpness_scale
        similarity_matrix = jnp.where(permitted_mask[None, None], similarity_matrix, NEG_FILL)
        row_max = lax.optimization_barrier(jnp.max(similarity_matrix, axis=-1, keepdims=True))
        log_norm = row_max + jnp.log(lax.optimization_barrier(jnp.sum(jnp.exp(similarity_matrix - row_max), axis=-1, keepdims=True)))
        attn_prob = jnp.exp(similarity_matrix - log_norm)
        dprob = jnp.einsum('sjvf,ijf->jvsi', result_cotangents, all_values)
        delta = lax.optimization_barrier(jnp.sum(attn_prob * dprob, axis=-1, keepdims=True))
        dscore = attn_prob * (dprob - delta)
        softmax_weights_lowp = lax.optimization_barrier(attn_prob.astype(jnp.bfloat16)).astype(jnp.float32)
        score_adjoint_halfprec = lax.optimization_barrier(dscore.astype(jnp.bfloat16)).astype(jnp.float32)
        derivative_lines_matrix = (jnp.einsum('ctba,aci->bcti', score_adjoint_halfprec, every_address_vector) * sharpness_scale).astype(jnp.bfloat16)
        retrieval_shares = (jnp.einsum('frjc,jfrx->cfx', score_adjoint_halfprec, asking_matrix) * sharpness_scale).astype(jnp.bfloat16)
        content_contributions = jnp.einsum('frjc,jfrx->cfx', softmax_weights_lowp, result_cotangents).astype(jnp.bfloat16)
        final_lookup_cotangent = retrieval_shares[:SUFFIX_LINES].reshape(SUFFIX_LINES, MEMORY_CHANNELS * ATTN_WIDTH)
        final_content_cotangent = content_contributions[:SUFFIX_LINES].reshape(SUFFIX_LINES, MEMORY_CHANNELS * ATTN_WIDTH)
        distant_lookup_cotangent = retrieval_shares[SUFFIX_LINES:].reshape(SEGMENT_FETCHES, SEGMENT_LENGTH, MEMORY_CHANNELS, ATTN_WIDTH).astype(jnp.float32)
        distant_content_cotangent = content_contributions[SUFFIX_LINES:].reshape(SEGMENT_FETCHES, SEGMENT_LENGTH, MEMORY_CHANNELS, ATTN_WIDTH).astype(jnp.float32)
        read_index = jnp.arange(SEGMENT_FETCHES)
        same_tile = overall_tile[:, None] == overall_tile[None, :]
        earlier = read_index[None, :] < read_index[:, None]
        first_read = jnp.logical_not(jnp.any(same_tile & earlier, axis=1)).astype(jnp.float32)
        same_float = same_tile.astype(jnp.float32)
        summed_k = jnp.einsum('st,tkhd->skhd', same_float, distant_lookup_cotangent).astype(jnp.bfloat16).astype(jnp.float32)
        summed_v = jnp.einsum('st,tkhd->skhd', same_float, distant_content_cotangent).astype(jnp.bfloat16).astype(jnp.float32)
        summed_k = summed_k * first_read[:, None, None, None]
        summed_v = summed_v * first_read[:, None, None, None]
        running_keys = running_keys.at[overall_tile].add(summed_k)
        running_values = running_values.at[overall_tile].add(summed_v)
        return ((running_keys, running_values), (derivative_lines_matrix.reshape(SUFFIX_LINES, QUERY_HEADS * ATTN_WIDTH), final_lookup_cotangent, final_content_cotangent))
    initial_zeros = jnp.zeros((N_CTX * OWNED_TILES, SEGMENT_LENGTH, MEMORY_CHANNELS, ATTN_WIDTH), jnp.float32)
    (running_keys, running_values), (derivative_lines_matrix, final_lookup_cotangent, final_content_cotangent) = lax.scan(one_reader, (initial_zeros, initial_zeros), jnp.arange(N_CTX).astype(jnp.int32))
    return (derivative_lines_matrix.reshape(TAIL_ROWS, QUERY_HEADS * ATTN_WIDTH), final_lookup_cotangent.reshape(TAIL_ROWS, MEMORY_CHANNELS * ATTN_WIDTH), final_content_cotangent.reshape(TAIL_ROWS, MEMORY_CHANNELS * ATTN_WIDTH), running_keys.reshape(CACHED_TOKENS, MEMORY_CHANNELS * ATTN_WIDTH), running_values.reshape(CACHED_TOKENS, MEMORY_CHANNELS * ATTN_WIDTH))
```

```python
import functools
import math

import jax
import jax.numpy as jnp
from jax import lax
from jax.experimental import pallas as pl
from jax.experimental.pallas import tpu as pltpu
from jax.sharding import PartitionSpec as P

WIDTH = 128
TILE = 128
PAIR = 2 * WIDTH
NEG = -1e30
SCALE = 1.0 / math.sqrt(WIDTH)
SCALE2 = SCALE * math.log2(math.e)
F32 = jnp.float32
BF16 = jnp.bfloat16


def dot_nt(a, b):
    return lax.dot_general(a, b, (((1,), (1,)), ((), ())), preferred_element_type=F32)


def dot_nn(a, b):
    return lax.dot_general(a, b, (((1,), (0,)), ((), ())), preferred_element_type=F32)


def dot_tn(a, b):
    return lax.dot_general(a, b, (((0,), (0,)), ((), ())), preferred_element_type=F32)


def repeat(steps, unroll, step):
    if unroll:
        for i in range(steps):
            step(i)
    else:

        def one(i, carry):
            step(i)
            return carry

        lax.fori_loop(0, steps, one, 0)


def columns(i, width):
    if isinstance(i, int):
        return pl.ds(i * width, width)
    return pl.ds(pl.multiple_of(i * width, width), width)


def pair_rows(ref, i):
    block = ref[:, columns(i, PAIR)]
    return jnp.concatenate([block[:, :WIDTH], block[:, WIDTH:]], axis=0)


def stacked_rows(ref, head, group):
    first = head * group
    return jnp.concatenate(
        [ref[:, (first + g) * WIDTH : (first + g + 1) * WIDTH] for g in range(group)], axis=0
    )


def twice(row):
    return jnp.concatenate([row, row], axis=1)


def tile_bias(table, first, tiles):
    return [twice(table[first + t : first + t + 1, :]) for t in range(tiles)]


def add_tiles(scores, biases):
    parts = [
        scores[t * TILE : (t + 1) * TILE, :] * SCALE2 + bias for t, bias in enumerate(biases)
    ]
    return parts[0] if len(parts) == 1 else jnp.concatenate(parts, axis=0)


def tail_bias(row_list):
    rows = row_list.shape[1]
    cut = jnp.sum((row_list == 0).astype(jnp.int32), axis=1, keepdims=True)
    key_at = lax.broadcasted_iota(jnp.int32, (rows, rows), 0)
    row_at = lax.broadcasted_iota(jnp.int32, (rows, rows), 1)
    allowed = ((key_at < cut) == (row_at < cut)) & (key_at <= row_at)
    return twice(jnp.where(allowed, 0.0, NEG).astype(F32))


def near_kernel(
    ctx, q_ref, g_ref, tk_ref, tv_ref, ok_ref, ov_ref, rl_ref, ro_ref, rt_ref, rs_ref, rc_ref,
    stats_ref, table_ref,
):
    own = ok_ref.shape[0] // TILE
    heads = tk_ref.shape[1] // WIDTH
    pairs = q_ref.shape[1] // PAIR
    reads = ro_ref.shape[1]
    slots = table_ref.shape[0]
    row_list = rl_ref[...]
    owner = ro_ref[...] - lax.axis_index("ctx")
    owner = jnp.where(owner < 0, owner + ctx, owner)
    wanted = owner * own + rt_ref[...]
    live = lax.broadcasted_iota(jnp.int32, (1, reads), 1) < rc_ref[...]
    wanted = jnp.where(live, wanted, -1)
    hit = lax.broadcasted_iota(jnp.int32, (slots, reads), 0) == wanted
    first = rs_ref[...] == 0
    count0 = jnp.sum(jnp.where(hit & first, 1.0, 0.0), axis=1, keepdims=True)
    count1 = jnp.sum(jnp.where(hit & jnp.logical_not(first), 1.0, 0.0), axis=1, keepdims=True)
    count = jnp.where(row_list == 0, count0, count1)
    table = jnp.where(count > 0.5, jnp.log2(jnp.maximum(count, 1.0)), NEG)
    table_ref[...] = table
    biases = [tail_bias(row_list)] + tile_bias(table, 0, own)
    for head in range(heads):
        cols = slice(head * WIDTH, (head + 1) * WIDTH)
        keys = jnp.concatenate([tk_ref[:, cols], ok_ref[:, cols]], axis=0)
        values = jnp.concatenate([tv_ref[:, cols], ov_ref[:, cols]], axis=0)
        for pair in range(head * pairs // heads, (head + 1) * pairs // heads):
            s = add_tiles(dot_nt(keys, pair_rows(q_ref, pair)), biases)
            top = jnp.max(s, axis=0, keepdims=True)
            p = jnp.exp2(s - top)
            d = dot_nt(values, pair_rows(g_ref, pair))
            at = slice(pair * PAIR, (pair + 1) * PAIR)
            stats_ref[0:1, at] = top
            stats_ref[1:2, at] = jnp.sum(p, axis=0, keepdims=True)
            stats_ref[2:3, at] = jnp.sum(p * d, axis=0, keepdims=True)


def far_kernel(
    unroll, q_ref, g_ref, k_ref, v_ref, stats_ref, table_ref, back_ref, ds_ref, fin_ref, p_ref
):
    near_tiles, far_tiles = table_tiles(back_ref)
    heads = k_ref.shape[1] // WIDTH
    pairs = q_ref.shape[1] // PAIR
    per_head = pairs // heads
    shifts, _, own_keys, _ = back_ref.shape
    table = table_ref[...]
    biases = tile_bias(table, near_tiles, far_tiles)
    for head in range(heads):
        cols = slice(head * WIDTH, (head + 1) * WIDTH)

        def step(i):
            pair = head * per_head + i
            at = columns(pair, PAIR)
            s = add_tiles(dot_nt(k_ref[:, cols], pair_rows(q_ref, pair)), biases)
            d = dot_nt(v_ref[:, cols], pair_rows(g_ref, pair))
            near_top = stats_ref[0:1, at]
            top = jnp.maximum(near_top, jnp.max(s, axis=0, keepdims=True))
            p = jnp.exp2(s - top)
            fade = jnp.exp2(near_top - top)
            total = stats_ref[1:2, at] * fade + jnp.sum(p, axis=0, keepdims=True)
            cross = stats_ref[2:3, at] * fade + jnp.sum(p * d, axis=0, keepdims=True)
            inverse = 1.0 / total
            delta = cross * inverse
            fin_ref[0:1, at] = top + jnp.log2(total)
            fin_ref[1:2, at] = delta
            p = p * inverse
            here = columns(i, PAIR)
            p_ref[:, here] = p.astype(BF16)
            ds_ref[head, :, here] = (p * (d - delta)).astype(BF16)

        repeat(per_head, unroll, step)
        dk = (dot_nn(ds_ref[head], stacked_rows(q_ref, head, 2 * per_head)) * SCALE).astype(BF16)
        dv = dot_nn(p_ref[...], stacked_rows(g_ref, head, 2 * per_head)).astype(BF16)
        for shift in range(shifts):
            rows = slice(shift * own_keys, (shift + 1) * own_keys)
            back_ref[shift, 0, :, cols] = dk[rows]
            back_ref[shift, 1, :, cols] = dv[rows]


def table_tiles(back_ref):
    own = back_ref.shape[2] // TILE
    return own, back_ref.shape[0] * own


def last_kernel(
    unroll, q_ref, g_ref, tk_ref, tv_ref, ok_ref, ov_ref, rl_ref, table_ref, fin_ref, fk_ref, fds_ref,
    dq_ref, dtk_ref, dtv_ref, dok_ref, dov_ref, p_ref, ds_ref,
):
    own = ok_ref.shape[0] // TILE
    tail = tk_ref.shape[0]
    heads = tk_ref.shape[1] // WIDTH
    pairs = q_ref.shape[1] // PAIR
    per_head = pairs // heads
    biases = [tail_bias(rl_ref[...])] + tile_bias(table_ref[...], 0, own)
    for head in range(heads):
        cols = slice(head * WIDTH, (head + 1) * WIDTH)
        keys = jnp.concatenate([tk_ref[:, cols], ok_ref[:, cols]], axis=0)
        values = jnp.concatenate([tv_ref[:, cols], ov_ref[:, cols]], axis=0)

        def step(i):
            pair = head * per_head + i
            at = columns(pair, PAIR)
            here = columns(i, PAIR)
            s = add_tiles(dot_nt(keys, pair_rows(q_ref, pair)), biases)
            d = dot_nt(values, pair_rows(g_ref, pair))
            p = jnp.exp2(s - fin_ref[0:1, at])
            ds = (p * (d - fin_ref[1:2, at])).astype(BF16)
            p_ref[:, here] = p.astype(BF16)
            ds_ref[:, here] = ds
            dq = dot_tn(keys, ds) + dot_tn(fk_ref[:, cols], fds_ref[head, :, here])
            dq = dq * SCALE
            dq = jnp.concatenate([dq[:, :WIDTH].T, dq[:, WIDTH:].T], axis=1)
            dq_ref[:, at] = dq.astype(BF16)

        repeat(per_head, unroll, step)
        dk = dot_nn(ds_ref[...], stacked_rows(q_ref, head, 2 * per_head)) * SCALE
        dv = dot_nn(p_ref[...], stacked_rows(g_ref, head, 2 * per_head))
        dtk_ref[:, cols] = dk[:tail].astype(BF16)
        dtv_ref[:, cols] = dv[:tail].astype(BF16)
        dok_ref[:, cols] = dk[tail:]
        dov_ref[:, cols] = dv[tail:]


def call(kernel, outs, scratch, flops, mib, *args):
    vmem = pl.BlockSpec(memory_space=pltpu.VMEM)
    moved = sum(a.size * a.dtype.itemsize for a in args) + sum(
        math.prod(o.shape) * o.dtype.itemsize for o in outs
    )
    return pl.pallas_call(
        kernel,
        out_shape=outs,
        in_specs=[vmem] * len(args),
        out_specs=[vmem] * len(outs),
        scratch_shapes=scratch,
        compiler_params=pltpu.CompilerParams(vmem_limit_bytes=mib * 2**20),
        cost_estimate=pl.CostEstimate(flops=flops, bytes_accessed=moved, transcendentals=0),
    )(*args)


def body(q, g, tk, tv, ck, cv, row_list, read_owner, read_tile, read_list, read_count):
    ctx = lax.axis_size("ctx")
    rows, q_width = q.shape
    kv_width = tk.shape[1]
    heads = kv_width // WIDTH
    group_rows = rows * (q_width // kv_width)
    own_keys = ck.shape[0]
    own = own_keys // TILE
    far_keys = (ctx - 1) * own_keys
    near_keys = rows + own_keys
    slots = -(-ctx * own // 8) * 8
    unroll = ctx <= 2
    row_list = row_list.reshape(1, rows)
    read_count = read_count.reshape(1, 1)

    def shifted(x, shift):
        return lax.ppermute(x, "ctx", [(o, (o - shift) % ctx) for o in range(ctx)])

    far_k = [shifted(ck, s) for s in range(1, ctx)]
    far_v = [shifted(cv, s) for s in range(1, ctx)]
    shape = jax.ShapeDtypeStruct
    product = 2 * q_width * rows * WIDTH
    stats, table = call(
        functools.partial(near_kernel, ctx),
        [shape((8, heads * group_rows), F32), shape((slots, rows), F32)],
        [],
        2 * product * near_keys // WIDTH,
        32,
        q, g, tk, tv, ck, cv, row_list, read_owner, read_tile, read_list, read_count,
    )
    far_k = far_k[0] if ctx == 2 else jnp.concatenate(far_k, axis=0)
    far_v = far_v[0] if ctx == 2 else jnp.concatenate(far_v, axis=0)
    back, far_ds, fin = call(
        functools.partial(far_kernel, unroll),
        [
            shape((ctx - 1, 2, own_keys, kv_width), BF16),
            shape((heads, far_keys, group_rows), BF16),
            shape((8, heads * group_rows), F32),
        ],
        [pltpu.VMEM((far_keys, group_rows), BF16)],
        4 * product * far_keys // WIDTH,
        32 if unroll else 60,
        q, g, far_k, far_v, stats, table,
    )
    returned = [shifted(back[s - 1], -s) for s in range(1, ctx)]
    dq, dtk, dtv, dok, dov = call(
        functools.partial(last_kernel, unroll),
        [
            shape(q.shape, BF16),
            shape(tk.shape, BF16),
            shape(tv.shape, BF16),
            shape(ck.shape, F32),
            shape(cv.shape, F32),
        ],
        [pltpu.VMEM((near_keys, group_rows), BF16), pltpu.VMEM((near_keys, group_rows), BF16)],
        product * (5 * near_keys + far_keys) // WIDTH,
        32 if unroll else 60,
        q, g, tk, tv, ck, cv, row_list, table, fin, far_k, far_ds,
    )
    for block in returned:
        dok = dok + block[0].astype(F32)
        dov = dov + block[1].astype(F32)
    return dq, dtk, dtv, dok, dov


def solution(mesh):
    wide = P(("dp", "ctx"), "tp")
    lone = P(("dp", "ctx"))
    flat = P(("dp", "ctx"), None)
    return jax.shard_map(
        body,
        mesh=mesh,
        in_specs=(wide,) * 6 + (lone, flat, flat, flat, lone),
        out_specs=(wide,) * 5,
        check_vma=False,
    )
```

```python
import functools
import math

import jax
import jax.numpy as jnp
from jax import lax
from jax.experimental import pallas as pl
from jax.experimental.pallas import tpu as pltpu
from jax.sharding import PartitionSpec as P

WIDTH = 128
TILE = 128
PAIR = 2 * WIDTH
NEG = -1e30
SCALE = 1.0 / math.sqrt(WIDTH)
SCALE2 = SCALE * math.log2(math.e)
F32 = jnp.float32
BF16 = jnp.bfloat16


def dot_nt(a, b):
    return lax.dot_general(a, b, (((1,), (1,)), ((), ())), preferred_element_type=F32)


def dot_nn(a, b):
    return lax.dot_general(a, b, (((1,), (0,)), ((), ())), preferred_element_type=F32)


def dot_tn(a, b):
    return lax.dot_general(a, b, (((0,), (0,)), ((), ())), preferred_element_type=F32)


def repeat(steps, unroll, step):
    if unroll:
        for i in range(steps):
            step(i)
    else:

        def one(i, carry):
            step(i)
            return carry

        lax.fori_loop(0, steps, one, 0)


def columns(i, width):
    if isinstance(i, int):
        return pl.ds(i * width, width)
    return pl.ds(pl.multiple_of(i * width, width), width)


def pair_rows(ref, i):
    block = ref[:, columns(i, PAIR)]
    return jnp.concatenate([block[:, :WIDTH], block[:, WIDTH:]], axis=0)


def stacked_rows(ref, head, group):
    first = head * group
    return jnp.concatenate(
        [ref[:, (first + g) * WIDTH : (first + g + 1) * WIDTH] for g in range(group)], axis=0
    )


def twice(row):
    return jnp.concatenate([row, row], axis=1)


def tile_bias(table, first, tiles):
    return [twice(table[first + t : first + t + 1, :]) for t in range(tiles)]


def add_tiles(scores, biases):
    parts = [
        scores[t * TILE : (t + 1) * TILE, :] * SCALE2 + bias for t, bias in enumerate(biases)
    ]
    return parts[0] if len(parts) == 1 else jnp.concatenate(parts, axis=0)


def tail_bias(row_list):
    rows = row_list.shape[1]
    cut = jnp.sum((row_list == 0).astype(jnp.int32), axis=1, keepdims=True)
    key_at = lax.broadcasted_iota(jnp.int32, (rows, rows), 0)
    row_at = lax.broadcasted_iota(jnp.int32, (rows, rows), 1)
    allowed = ((key_at < cut) == (row_at < cut)) & (key_at <= row_at)
    return twice(jnp.where(allowed, 0.0, NEG).astype(F32))


def near_kernel(
    ctx, q_in, g_in, tk_in, tv_in, ok_in, ov_in, rl_in, ro_in, rt_in, rs_in, rc_ref,
    q_ref, g_ref, k_ref, v_ref, rl_ref, stats_ref, table_ref,
    ro_ref, rt_ref, rs_ref, sems,
):
    tail = tk_in.shape[0]
    own = ok_in.shape[0] // TILE
    heads = tk_in.shape[1] // WIDTH
    pairs = q_ref.shape[1] // PAIR
    reads = ro_ref.shape[1]
    slots = table_ref.shape[0]
    moves = [
        (rl_in, rl_ref), (ro_in, ro_ref), (rt_in, rt_ref), (rs_in, rs_ref),
        (tk_in, k_ref.at[:tail]), (ok_in, k_ref.at[tail:]), (q_in, q_ref),
        (tv_in, v_ref.at[:tail]), (ov_in, v_ref.at[tail:]), (g_in, g_ref),
    ]
    copies = [pltpu.make_async_copy(a, b, sems.at[i]) for i, (a, b) in enumerate(moves)]
    for copy in copies:
        copy.start()
    for copy in copies[:4]:
        copy.wait()
    row_list = rl_ref[...]
    owner = ro_ref[...] - lax.axis_index("ctx")
    owner = jnp.where(owner < 0, owner + ctx, owner)
    wanted = owner * own + rt_ref[...]
    live = lax.broadcasted_iota(jnp.int32, (1, reads), 1) < rc_ref[0]
    wanted = jnp.where(live, wanted, -1)
    hit = lax.broadcasted_iota(jnp.int32, (slots, reads), 0) == wanted
    first = rs_ref[...] == 0
    count0 = jnp.sum(jnp.where(hit & first, 1.0, 0.0), axis=1, keepdims=True)
    count1 = jnp.sum(jnp.where(hit & jnp.logical_not(first), 1.0, 0.0), axis=1, keepdims=True)
    count = jnp.where(row_list == 0, count0, count1)
    table = jnp.where(count > 0.5, jnp.log2(jnp.maximum(count, 1.0)), NEG)
    table_ref[...] = table
    biases = [tail_bias(row_list)] + tile_bias(table, 0, own)
    for copy in copies[4:]:
        copy.wait()
    for head in range(heads):
        cols = slice(head * WIDTH, (head + 1) * WIDTH)
        for pair in range(head * pairs // heads, (head + 1) * pairs // heads):
            s = add_tiles(dot_nt(k_ref[:, cols], pair_rows(q_ref, pair)), biases)
            top = jnp.max(s, axis=0, keepdims=True)
            p = jnp.exp2(s - top)
            d = dot_nt(v_ref[:, cols], pair_rows(g_ref, pair))
            at = slice(pair * PAIR, (pair + 1) * PAIR)
            stats_ref[0:1, at] = top
            stats_ref[1:2, at] = jnp.sum(p, axis=0, keepdims=True)
            stats_ref[2:3, at] = jnp.sum(p * d, axis=0, keepdims=True)


def far_kernel(
    unroll, q_ref, g_ref, k_ref, v_ref, stats_ref, table_ref, back_ref, ds_ref, fin_ref, p_ref
):
    near_tiles, far_tiles = table_tiles(back_ref)
    heads = k_ref.shape[1] // WIDTH
    pairs = q_ref.shape[1] // PAIR
    per_head = pairs // heads
    shifts, _, own_keys, _ = back_ref.shape
    table = table_ref[...]
    biases = tile_bias(table, near_tiles, far_tiles)
    for head in range(heads):
        cols = slice(head * WIDTH, (head + 1) * WIDTH)

        def step(i):
            pair = head * per_head + i
            at = columns(pair, PAIR)
            s = add_tiles(dot_nt(k_ref[:, cols], pair_rows(q_ref, pair)), biases)
            d = dot_nt(v_ref[:, cols], pair_rows(g_ref, pair))
            near_top = stats_ref[0:1, at]
            top = jnp.maximum(near_top, jnp.max(s, axis=0, keepdims=True))
            p = jnp.exp2(s - top)
            fade = jnp.exp2(near_top - top)
            total = stats_ref[1:2, at] * fade + jnp.sum(p, axis=0, keepdims=True)
            cross = stats_ref[2:3, at] * fade + jnp.sum(p * d, axis=0, keepdims=True)
            inverse = 1.0 / total
            delta = cross * inverse
            fin_ref[0:1, at] = top + jnp.log2(total)
            fin_ref[1:2, at] = delta
            p = p * inverse
            here = columns(i, PAIR)
            p_ref[:, here] = p.astype(BF16)
            ds_ref[head, :, here] = (p * (d - delta)).astype(BF16)

        repeat(per_head, unroll, step)
        dk = (dot_nn(ds_ref[head], stacked_rows(q_ref, head, 2 * per_head)) * SCALE).astype(BF16)
        dv = dot_nn(p_ref[...], stacked_rows(g_ref, head, 2 * per_head)).astype(BF16)
        for shift in range(shifts):
            rows = slice(shift * own_keys, (shift + 1) * own_keys)
            back_ref[shift, 0, :, cols] = dk[rows]
            back_ref[shift, 1, :, cols] = dv[rows]


def table_tiles(back_ref):
    own = back_ref.shape[2] // TILE
    return own, back_ref.shape[0] * own


def last_kernel(
    unroll, q_ref, g_ref, k_ref, v_ref, rl_ref, table_ref, fin_ref, fk_ref, fds_ref,
    dq_ref, dtk_ref, dtv_ref, dok_ref, dov_ref, p_ref, ds_ref,
):
    own = dok_ref.shape[0] // TILE
    tail = dtk_ref.shape[0]
    heads = k_ref.shape[1] // WIDTH
    pairs = q_ref.shape[1] // PAIR
    per_head = pairs // heads
    biases = [tail_bias(rl_ref[...])] + tile_bias(table_ref[...], 0, own)
    for head in range(heads):
        cols = slice(head * WIDTH, (head + 1) * WIDTH)

        def step(i):
            pair = head * per_head + i
            at = columns(pair, PAIR)
            here = columns(i, PAIR)
            s = add_tiles(dot_nt(k_ref[:, cols], pair_rows(q_ref, pair)), biases)
            d = dot_nt(v_ref[:, cols], pair_rows(g_ref, pair))
            p = jnp.exp2(s - fin_ref[0:1, at])
            ds = (p * (d - fin_ref[1:2, at])).astype(BF16)
            p_ref[:, here] = p.astype(BF16)
            ds_ref[:, here] = ds
            dq = dot_tn(k_ref[:, cols], ds) + dot_tn(fk_ref[:, cols], fds_ref[head, :, here])
            dq = dq * SCALE
            dq = jnp.concatenate([dq[:, :WIDTH].T, dq[:, WIDTH:].T], axis=1)
            dq_ref[:, at] = dq.astype(BF16)

        repeat(per_head, unroll, step)
        dk = dot_nn(ds_ref[...], stacked_rows(q_ref, head, 2 * per_head)) * SCALE
        dv = dot_nn(p_ref[...], stacked_rows(g_ref, head, 2 * per_head))
        dtk_ref[:, cols] = dk[:tail].astype(BF16)
        dtv_ref[:, cols] = dv[:tail].astype(BF16)
        dok_ref[:, cols] = dk[tail:]
        dov_ref[:, cols] = dv[tail:]


def call(kernel, spaces, outs, scratch, flops, mib, *args):
    vmem = pl.BlockSpec(memory_space=pltpu.VMEM)
    moved = sum(a.size * a.dtype.itemsize for a in args) + sum(
        math.prod(o.shape) * o.dtype.itemsize for o in outs
    )
    return pl.pallas_call(
        kernel,
        out_shape=outs,
        in_specs=[pl.BlockSpec(memory_space=space) for space in spaces],
        out_specs=[vmem] * len(outs),
        scratch_shapes=scratch,
        compiler_params=pltpu.CompilerParams(vmem_limit_bytes=mib * 2**20),
        cost_estimate=pl.CostEstimate(flops=flops, bytes_accessed=moved, transcendentals=0),
    )(*args)


def body(q, g, tk, tv, ck, cv, row_list, read_owner, read_tile, read_list, read_count):
    ctx = lax.axis_size("ctx")
    rows, q_width = q.shape
    kv_width = tk.shape[1]
    heads = kv_width // WIDTH
    group_rows = rows * (q_width // kv_width)
    own_keys = ck.shape[0]
    own = own_keys // TILE
    far_keys = (ctx - 1) * own_keys
    near_keys = rows + own_keys
    slots = -(-ctx * own // 8) * 8
    unroll = ctx <= 2
    row_list = row_list.reshape(1, rows)

    def shifted(x, shift):
        return lax.ppermute(x, "ctx", [(o, (o - shift) % ctx) for o in range(ctx)])

    far_k = [shifted(ck, s) for s in range(1, ctx)]
    far_v = [shifted(cv, s) for s in range(1, ctx)]
    shape = jax.ShapeDtypeStruct
    product = 2 * q_width * rows * WIDTH
    small = read_owner.shape
    here = [
        pltpu.with_memory_space_constraint(a, pltpu.HBM)
        for a in (q, g, tk, tv, ck, cv, row_list, read_owner, read_tile, read_list)
    ]
    q, g, near_k, near_v, row_list, stats, table = call(
        functools.partial(near_kernel, ctx),
        [pltpu.HBM] * len(here) + [pltpu.SMEM],
        [
            shape(q.shape, BF16),
            shape(g.shape, BF16),
            shape((near_keys, kv_width), BF16),
            shape((near_keys, kv_width), BF16),
            shape(row_list.shape, jnp.int32),
            shape((8, heads * group_rows), F32),
            shape((slots, rows), F32),
        ],
        [pltpu.VMEM(small, jnp.int32)] * 3 + [pltpu.SemaphoreType.DMA((10,))],
        2 * product * near_keys // WIDTH,
        32,
        *here, read_count,
    )
    far_k = far_k[0] if ctx == 2 else jnp.concatenate(far_k, axis=0)
    far_v = far_v[0] if ctx == 2 else jnp.concatenate(far_v, axis=0)
    back, far_ds, fin = call(
        functools.partial(far_kernel, unroll),
        [pltpu.VMEM] * 6,
        [
            shape((ctx - 1, 2, own_keys, kv_width), BF16),
            shape((heads, far_keys, group_rows), BF16),
            shape((8, heads * group_rows), F32),
        ],
        [pltpu.VMEM((far_keys, group_rows), BF16)],
        4 * product * far_keys // WIDTH,
        32 if unroll else 60,
        q, g, far_k, far_v, stats, table,
    )
    returned = [shifted(back[s - 1], -s) for s in range(1, ctx)]
    dq, dtk, dtv, dok, dov = call(
        functools.partial(last_kernel, unroll),
        [pltpu.VMEM] * 9,
        [
            shape(q.shape, BF16),
            shape(tk.shape, BF16),
            shape(tv.shape, BF16),
            shape(ck.shape, F32),
            shape(cv.shape, F32),
        ],
        [pltpu.VMEM((near_keys, group_rows), BF16), pltpu.VMEM((near_keys, group_rows), BF16)],
        product * (5 * near_keys + far_keys) // WIDTH,
        32 if unroll else 60,
        q, g, near_k, near_v, row_list, table, fin, far_k, far_ds,
    )
    for block in returned:
        dok = dok + block[0].astype(F32)
        dov = dov + block[1].astype(F32)
    return dq, dtk, dtv, dok, dov


def solution(mesh):
    wide = P(("dp", "ctx"), "tp")
    lone = P(("dp", "ctx"))
    flat = P(("dp", "ctx"), None)
    return jax.shard_map(
        body,
        mesh=mesh,
        in_specs=(wide,) * 6 + (lone, flat, flat, flat, lone),
        out_specs=(wide,) * 5,
        check_vma=False,
    )
```

```python
import functools
import math

import jax
import jax.numpy as jnp
from jax import lax
from jax.experimental import pallas as pl
from jax.experimental.pallas import tpu as pltpu
from jax.sharding import PartitionSpec as P

WIDTH = 128
TILE = 128
PAIR = 2 * WIDTH
NEG = -1e30
SCALE = 1.0 / math.sqrt(WIDTH)
SCALE2 = SCALE * math.log2(math.e)
F32 = jnp.float32
BF16 = jnp.bfloat16


def dot_nt(a, b):
    return lax.dot_general(a, b, (((1,), (1,)), ((), ())), preferred_element_type=F32)


def dot_nn(a, b):
    return lax.dot_general(a, b, (((1,), (0,)), ((), ())), preferred_element_type=F32)


def dot_tn(a, b):
    return lax.dot_general(a, b, (((0,), (0,)), ((), ())), preferred_element_type=F32)


def repeat(steps, unroll, step):
    if unroll:
        for i in range(steps):
            step(i)
    else:

        def one(i, carry):
            step(i)
            return carry

        lax.fori_loop(0, steps, one, 0)


def columns(i, width):
    if isinstance(i, int):
        return pl.ds(i * width, width)
    return pl.ds(pl.multiple_of(i * width, width), width)


def pair_rows(ref, i):
    block = ref[:, columns(i, PAIR)]
    return jnp.concatenate([block[:, :WIDTH], block[:, WIDTH:]], axis=0)


def stacked_rows(ref, head, group):
    first = head * group
    return jnp.concatenate(
        [ref[:, (first + g) * WIDTH : (first + g + 1) * WIDTH] for g in range(group)], axis=0
    )


def twice(row):
    return jnp.concatenate([row, row], axis=1)


def tile_bias(table, first, tiles):
    return [twice(table[first + t : first + t + 1, :]) for t in range(tiles)]


def add_tiles(scores, biases):
    parts = [
        scores[t * TILE : (t + 1) * TILE, :] * SCALE2 + bias for t, bias in enumerate(biases)
    ]
    return parts[0] if len(parts) == 1 else jnp.concatenate(parts, axis=0)


def tail_bias(row_list):
    rows = row_list.shape[1]
    cut = jnp.sum((row_list == 0).astype(jnp.int32), axis=1, keepdims=True)
    key_at = lax.broadcasted_iota(jnp.int32, (rows, rows), 0)
    row_at = lax.broadcasted_iota(jnp.int32, (rows, rows), 1)
    allowed = ((key_at < cut) == (row_at < cut)) & (key_at <= row_at)
    return twice(jnp.where(allowed, 0.0, NEG).astype(F32))


def near_kernel(
    ctx, q_in, g_in, tk_in, tv_in, ok_in, ov_in, rl_in, ro_in, rt_in, rs_in, rc_ref,
    q_ref, g_ref, k_ref, p_ref, d_ref, stats_ref, table_ref,
    v_ref, rl_ref, ro_ref, rt_ref, rs_ref, sems,
):
    tail = tk_in.shape[0]
    own = ok_in.shape[0] // TILE
    heads = tk_in.shape[1] // WIDTH
    pairs = q_ref.shape[1] // PAIR
    reads = ro_ref.shape[1]
    slots = table_ref.shape[0]
    moves = [
        (rl_in, rl_ref), (ro_in, ro_ref), (rt_in, rt_ref), (rs_in, rs_ref),
        (tk_in, k_ref.at[:tail]), (ok_in, k_ref.at[tail:]), (q_in, q_ref),
        (tv_in, v_ref.at[:tail]), (ov_in, v_ref.at[tail:]), (g_in, g_ref),
    ]
    copies = [pltpu.make_async_copy(a, b, sems.at[i]) for i, (a, b) in enumerate(moves)]
    for copy in copies:
        copy.start()
    for copy in copies[:4]:
        copy.wait()
    row_list = rl_ref[...]
    owner = ro_ref[...] - lax.axis_index("ctx")
    owner = jnp.where(owner < 0, owner + ctx, owner)
    wanted = owner * own + rt_ref[...]
    live = lax.broadcasted_iota(jnp.int32, (1, reads), 1) < rc_ref[0]
    wanted = jnp.where(live, wanted, -1)
    hit = lax.broadcasted_iota(jnp.int32, (slots, reads), 0) == wanted
    first = rs_ref[...] == 0
    count0 = jnp.sum(jnp.where(hit & first, 1.0, 0.0), axis=1, keepdims=True)
    count1 = jnp.sum(jnp.where(hit & jnp.logical_not(first), 1.0, 0.0), axis=1, keepdims=True)
    count = jnp.where(row_list == 0, count0, count1)
    table = jnp.where(count > 0.5, jnp.log2(jnp.maximum(count, 1.0)), NEG)
    table_ref[...] = table
    biases = [tail_bias(row_list)] + tile_bias(table, 0, own)
    for copy in copies[4:]:
        copy.wait()
    for head in range(heads):
        cols = slice(head * WIDTH, (head + 1) * WIDTH)
        for pair in range(head * pairs // heads, (head + 1) * pairs // heads):
            s = add_tiles(dot_nt(k_ref[:, cols], pair_rows(q_ref, pair)), biases)
            top = jnp.max(s, axis=0, keepdims=True)
            p = jnp.exp2(s - top)
            d = dot_nt(v_ref[:, cols], pair_rows(g_ref, pair))
            at = slice(pair * PAIR, (pair + 1) * PAIR)
            here = columns(pair - head * pairs // heads, PAIR)
            p_ref[head, :, here] = p
            d_ref[head, :, here] = d
            stats_ref[0:1, at] = top
            stats_ref[1:2, at] = jnp.sum(p, axis=0, keepdims=True)
            stats_ref[2:3, at] = jnp.sum(p * d, axis=0, keepdims=True)


def far_key_kernel(
    unroll, q_ref, g_ref, k_ref, stats_ref, table_ref, back_ref, p_ref, fin_ref, low_ref
):
    far_tiles = k_ref.shape[0] // TILE
    heads = k_ref.shape[1] // WIDTH
    per_head = q_ref.shape[1] // PAIR // heads
    shifts, own_keys, _ = back_ref.shape
    biases = tile_bias(table_ref[...], own_keys // TILE, far_tiles)
    for head in range(heads):
        cols = slice(head * WIDTH, (head + 1) * WIDTH)

        def step(i):
            pair = head * per_head + i
            at = columns(pair, PAIR)
            here = columns(i, PAIR)
            s = add_tiles(dot_nt(k_ref[:, cols], pair_rows(q_ref, pair)), biases)
            near_top = stats_ref[0:1, at]
            top = jnp.maximum(near_top, jnp.max(s, axis=0, keepdims=True))
            p = jnp.exp2(s - top)
            fade = jnp.exp2(near_top - top)
            inverse = 1.0 / (stats_ref[1:2, at] * fade + jnp.sum(p, axis=0, keepdims=True))
            fade = fade * inverse
            fin_ref[0:1, at] = fade
            fin_ref[1:2, at] = stats_ref[2:3, at] * fade
            p = p * inverse
            p_ref[head, :, here] = p.astype(p_ref.dtype)
            low_ref[:, here] = p.astype(BF16)

        repeat(per_head, unroll, step)
        dv = dot_nn(low_ref[...], stacked_rows(g_ref, head, 2 * per_head)).astype(BF16)
        for shift in range(shifts):
            back_ref[shift, :, cols] = dv[shift * own_keys : (shift + 1) * own_keys]


def far_value_kernel(unroll, q_ref, g_ref, v_ref, p_ref, fin_ref, back_ref, ds_ref, delta_ref):
    heads = v_ref.shape[1] // WIDTH
    per_head = q_ref.shape[1] // PAIR // heads
    shifts, own_keys, _ = back_ref.shape
    for head in range(heads):
        cols = slice(head * WIDTH, (head + 1) * WIDTH)

        def step(i):
            pair = head * per_head + i
            at = columns(pair, PAIR)
            here = columns(i, PAIR)
            d = dot_nt(v_ref[:, cols], pair_rows(g_ref, pair))
            p = p_ref[head, :, here].astype(F32)
            delta = fin_ref[1:2, at] + jnp.sum(p * d, axis=0, keepdims=True)
            delta_ref[0:1, at] = delta
            ds_ref[head, :, here] = (p * (d - delta)).astype(BF16)

        repeat(per_head, unroll, step)
        dk = (dot_nn(ds_ref[head], stacked_rows(q_ref, head, 2 * per_head)) * SCALE).astype(BF16)
        for shift in range(shifts):
            back_ref[shift, :, cols] = dk[shift * own_keys : (shift + 1) * own_keys]


def last_kernel(
    unroll, q_ref, g_ref, k_ref, p_ref, d_ref, fin_ref, delta_ref, fk_ref, fds_ref,
    dq_ref, dtk_ref, dtv_ref, dok_ref, dov_ref, low_ref, ds_ref,
):
    tail = dtk_ref.shape[0]
    heads = k_ref.shape[1] // WIDTH
    per_head = q_ref.shape[1] // PAIR // heads
    for head in range(heads):
        cols = slice(head * WIDTH, (head + 1) * WIDTH)

        def step(i):
            pair = head * per_head + i
            at = columns(pair, PAIR)
            here = columns(i, PAIR)
            p = p_ref[head, :, here] * fin_ref[0:1, at]
            ds = (p * (d_ref[head, :, here] - delta_ref[0:1, at])).astype(BF16)
            low_ref[:, here] = p.astype(BF16)
            ds_ref[:, here] = ds
            dq = dot_tn(k_ref[:, cols], ds) + dot_tn(fk_ref[:, cols], fds_ref[head, :, here])
            dq = dq * SCALE
            dq = jnp.concatenate([dq[:, :WIDTH].T, dq[:, WIDTH:].T], axis=1)
            dq_ref[:, at] = dq.astype(BF16)

        repeat(per_head, unroll, step)
        dk = dot_nn(ds_ref[...], stacked_rows(q_ref, head, 2 * per_head)) * SCALE
        dv = dot_nn(low_ref[...], stacked_rows(g_ref, head, 2 * per_head))
        dtk_ref[:, cols] = dk[:tail].astype(BF16)
        dtv_ref[:, cols] = dv[:tail].astype(BF16)
        dok_ref[:, cols] = dk[tail:]
        dov_ref[:, cols] = dv[tail:]


def call(kernel, spaces, outs, scratch, flops, mib, *args):
    vmem = pl.BlockSpec(memory_space=pltpu.VMEM)
    moved = sum(a.size * a.dtype.itemsize for a in args) + sum(
        math.prod(o.shape) * o.dtype.itemsize for o in outs
    )
    return pl.pallas_call(
        kernel,
        out_shape=outs,
        in_specs=[pl.BlockSpec(memory_space=space) for space in spaces],
        out_specs=[vmem] * len(outs),
        scratch_shapes=scratch,
        compiler_params=pltpu.CompilerParams(vmem_limit_bytes=mib * 2**20),
        cost_estimate=pl.CostEstimate(flops=flops, bytes_accessed=moved, transcendentals=0),
    )(*args)


def body(q, g, tk, tv, ck, cv, row_list, read_owner, read_tile, read_list, read_count):
    ctx = lax.axis_size("ctx")
    rows, q_width = q.shape
    kv_width = tk.shape[1]
    heads = kv_width // WIDTH
    group_rows = rows * (q_width // kv_width)
    own_keys = ck.shape[0]
    own = own_keys // TILE
    far_keys = (ctx - 1) * own_keys
    near_keys = rows + own_keys
    slots = -(-ctx * own // 8) * 8
    unroll = ctx <= 2
    row_list = row_list.reshape(1, rows)

    def shifted(x, shift):
        return lax.ppermute(x, "ctx", [(o, (o - shift) % ctx) for o in range(ctx)])

    far_k = [shifted(ck, s) for s in range(1, ctx)]
    far_v = [shifted(cv, s) for s in range(1, ctx)]
    shape = jax.ShapeDtypeStruct
    product = 2 * q_width * rows * WIDTH
    small = read_owner.shape
    here = [
        pltpu.with_memory_space_constraint(a, pltpu.HBM)
        for a in (q, g, tk, tv, ck, cv, row_list, read_owner, read_tile, read_list)
    ]
    q, g, near_k, near_p, near_d, stats, table = call(
        functools.partial(near_kernel, ctx),
        [pltpu.HBM] * len(here) + [pltpu.SMEM],
        [
            shape(q.shape, BF16),
            shape(g.shape, BF16),
            shape((near_keys, kv_width), BF16),
            shape((heads, near_keys, group_rows), F32),
            shape((heads, near_keys, group_rows), F32),
            shape((8, heads * group_rows), F32),
            shape((slots, rows), F32),
        ],
        [
            pltpu.VMEM((near_keys, kv_width), BF16),
            pltpu.VMEM(row_list.shape, jnp.int32),
            pltpu.VMEM(small, jnp.int32),
            pltpu.VMEM(small, jnp.int32),
            pltpu.VMEM(small, jnp.int32),
            pltpu.SemaphoreType.DMA((10,)),
        ],
        2 * product * near_keys // WIDTH,
        32,
        *here, read_count,
    )
    mib = 32 if unroll else 60
    far_k = far_k[0] if ctx == 2 else jnp.concatenate(far_k, axis=0)
    back_v, far_p, fin = call(
        functools.partial(far_key_kernel, unroll),
        [pltpu.VMEM] * 5,
        [
            shape((ctx - 1, own_keys, kv_width), BF16),
            shape((heads, far_keys, group_rows), F32 if unroll else BF16),
            shape((8, heads * group_rows), F32),
        ],
        [pltpu.VMEM((far_keys, group_rows), BF16)],
        2 * product * far_keys // WIDTH,
        mib,
        q, g, far_k, stats, table,
    )
    returned_v = [shifted(back_v[s - 1], -s) for s in range(1, ctx)]
    far_v = far_v[0] if ctx == 2 else jnp.concatenate(far_v, axis=0)
    back_k, far_ds, delta = call(
        functools.partial(far_value_kernel, unroll),
        [pltpu.VMEM] * 5,
        [
            shape((ctx - 1, own_keys, kv_width), BF16),
            shape((heads, far_keys, group_rows), BF16),
            shape((8, heads * group_rows), F32),
        ],
        [],
        2 * product * far_keys // WIDTH,
        mib,
        q, g, far_v, far_p, fin,
    )
    returned_k = [shifted(back_k[s - 1], -s) for s in range(1, ctx)]
    dq, dtk, dtv, dok, dov = call(
        functools.partial(last_kernel, unroll),
        [pltpu.VMEM] * 9,
        [
            shape(q.shape, BF16),
            shape(tk.shape, BF16),
            shape(tv.shape, BF16),
            shape(ck.shape, F32),
            shape(cv.shape, F32),
        ],
        [pltpu.VMEM((near_keys, group_rows), BF16), pltpu.VMEM((near_keys, group_rows), BF16)],
        product * (3 * near_keys + far_keys) // WIDTH,
        mib,
        q, g, near_k, near_p, near_d, fin, delta, far_k, far_ds,
    )
    for key_block, value_block in zip(returned_k, returned_v):
        dok = dok + key_block.astype(F32)
        dov = dov + value_block.astype(F32)
    return dq, dtk, dtv, dok, dov


def solution(mesh):
    wide = P(("dp", "ctx"), "tp")
    lone = P(("dp", "ctx"))
    flat = P(("dp", "ctx"), None)
    return jax.shard_map(
        body,
        mesh=mesh,
        in_specs=(wide,) * 6 + (lone, flat, flat, flat, lone),
        out_specs=(wide,) * 5,
        check_vma=False,
    )
```

```python
import functools
import math

import jax
import jax.numpy as jnp
from jax import lax
from jax.experimental import pallas as pl
from jax.experimental.pallas import tpu as pltpu
from jax.sharding import PartitionSpec as P

WIDTH = 128
TILE = 128
PAIR = 2 * WIDTH
NEG = -1e30
SCALE = 1.0 / math.sqrt(WIDTH)
SCALE2 = SCALE * math.log2(math.e)
F32 = jnp.float32
BF16 = jnp.bfloat16


def dot_nt(a, b):
    return lax.dot_general(a, b, (((1,), (1,)), ((), ())), preferred_element_type=F32)


def dot_nn(a, b):
    return lax.dot_general(a, b, (((1,), (0,)), ((), ())), preferred_element_type=F32)


def dot_tn(a, b):
    return lax.dot_general(a, b, (((0,), (0,)), ((), ())), preferred_element_type=F32)


def repeat(steps, unroll, step):
    if unroll:
        for i in range(steps):
            step(i)
    else:

        def one(i, carry):
            step(i)
            return carry

        lax.fori_loop(0, steps, one, 0)


def columns(i, width):
    if isinstance(i, int):
        return pl.ds(i * width, width)
    return pl.ds(pl.multiple_of(i * width, width), width)


def pair_rows(ref, i):
    block = ref[:, columns(i, PAIR)]
    return jnp.concatenate([block[:, :WIDTH], block[:, WIDTH:]], axis=0)


def stacked_rows(ref, head, group):
    first = head * group
    return jnp.concatenate(
        [ref[:, (first + g) * WIDTH : (first + g + 1) * WIDTH] for g in range(group)], axis=0
    )


def twice(row):
    return jnp.concatenate([row, row], axis=1)


def tile_bias(table, first, tiles):
    return [twice(table[first + t : first + t + 1, :]) for t in range(tiles)]


def add_tiles(scores, biases):
    parts = [
        scores[t * TILE : (t + 1) * TILE, :] * SCALE2 + bias for t, bias in enumerate(biases)
    ]
    return parts[0] if len(parts) == 1 else jnp.concatenate(parts, axis=0)


def tail_bias(row_list):
    rows = row_list.shape[1]
    cut = jnp.sum((row_list == 0).astype(jnp.int32), axis=1, keepdims=True)
    key_at = lax.broadcasted_iota(jnp.int32, (rows, rows), 0)
    row_at = lax.broadcasted_iota(jnp.int32, (rows, rows), 1)
    allowed = ((key_at < cut) == (row_at < cut)) & (key_at <= row_at)
    return twice(jnp.where(allowed, 0.0, NEG).astype(F32))


def near_key_kernel(
    ctx, q_in, g_in, tk_in, tv_in, ok_in, ov_in, rl_in, ro_in, rt_in, rs_in, rc_ref,
    q_ref, g_ref, k_ref, tv_ref, ov_ref, p_ref, stats_ref, table_ref,
    rl_ref, ro_ref, rt_ref, rs_ref, sems,
):
    tail = tk_in.shape[0]
    own = ok_in.shape[0] // TILE
    heads = tk_in.shape[1] // WIDTH
    per_head = q_ref.shape[1] // PAIR // heads
    reads = ro_ref.shape[1]
    slots = table_ref.shape[0]
    moves = [
        (rl_in, rl_ref), (ro_in, ro_ref), (rt_in, rt_ref), (rs_in, rs_ref),
        (tk_in, k_ref.at[:tail]), (ok_in, k_ref.at[tail:]), (q_in, q_ref),
        (tv_in, tv_ref), (ov_in, ov_ref), (g_in, g_ref),
    ]
    copies = [pltpu.make_async_copy(a, b, sems.at[i]) for i, (a, b) in enumerate(moves)]
    for copy in copies:
        copy.start()
    for copy in copies[:4]:
        copy.wait()
    row_list = rl_ref[...]
    owner = ro_ref[...] - lax.axis_index("ctx")
    owner = jnp.where(owner < 0, owner + ctx, owner)
    wanted = owner * own + rt_ref[...]
    live = lax.broadcasted_iota(jnp.int32, (1, reads), 1) < rc_ref[0]
    wanted = jnp.where(live, wanted, -1)
    hit = lax.broadcasted_iota(jnp.int32, (slots, reads), 0) == wanted
    first = rs_ref[...] == 0
    count0 = jnp.sum(jnp.where(hit & first, 1.0, 0.0), axis=1, keepdims=True)
    count1 = jnp.sum(jnp.where(hit & jnp.logical_not(first), 1.0, 0.0), axis=1, keepdims=True)
    count = jnp.where(row_list == 0, count0, count1)
    table = jnp.where(count > 0.5, jnp.log2(jnp.maximum(count, 1.0)), NEG)
    table_ref[...] = table
    biases = [tail_bias(row_list)] + tile_bias(table, 0, own)
    for copy in copies[4:7]:
        copy.wait()
    for head in range(heads):
        cols = slice(head * WIDTH, (head + 1) * WIDTH)
        for i in range(per_head):
            pair = head * per_head + i
            at = columns(pair, PAIR)
            s = add_tiles(dot_nt(k_ref[:, cols], pair_rows(q_ref, pair)), biases)
            top = jnp.max(s, axis=0, keepdims=True)
            p = jnp.exp2(s - top)
            p_ref[head, :, columns(i, PAIR)] = p
            stats_ref[0:1, at] = top
            stats_ref[1:2, at] = jnp.sum(p, axis=0, keepdims=True)
    for copy in copies[7:]:
        copy.wait()


def near_value_kernel(g_ref, tv_ref, ov_ref, p_ref, d_ref, cross_ref):
    heads = tv_ref.shape[1] // WIDTH
    per_head = g_ref.shape[1] // PAIR // heads
    for head in range(heads):
        cols = slice(head * WIDTH, (head + 1) * WIDTH)
        values = jnp.concatenate([tv_ref[:, cols], ov_ref[:, cols]], axis=0)
        for i in range(per_head):
            pair = head * per_head + i
            here = columns(i, PAIR)
            d = dot_nt(values, pair_rows(g_ref, pair))
            d_ref[head, :, here] = d
            cross = jnp.sum(p_ref[head, :, here] * d, axis=0, keepdims=True)
            cross_ref[0:1, columns(pair, PAIR)] = cross


def far_key_kernel(
    unroll, q_ref, g_ref, k_ref, stats_ref, table_ref, back_ref, p_ref, fin_ref, low_ref
):
    far_tiles = k_ref.shape[0] // TILE
    heads = k_ref.shape[1] // WIDTH
    per_head = q_ref.shape[1] // PAIR // heads
    shifts, own_keys, _ = back_ref.shape
    biases = tile_bias(table_ref[...], own_keys // TILE, far_tiles)
    for head in range(heads):
        cols = slice(head * WIDTH, (head + 1) * WIDTH)

        def step(i):
            pair = head * per_head + i
            at = columns(pair, PAIR)
            here = columns(i, PAIR)
            s = add_tiles(dot_nt(k_ref[:, cols], pair_rows(q_ref, pair)), biases)
            near_top = stats_ref[0:1, at]
            top = jnp.maximum(near_top, jnp.max(s, axis=0, keepdims=True))
            p = jnp.exp2(s - top)
            fade = jnp.exp2(near_top - top)
            inverse = 1.0 / (stats_ref[1:2, at] * fade + jnp.sum(p, axis=0, keepdims=True))
            fin_ref[0:1, at] = fade * inverse
            p = p * inverse
            p_ref[head, :, here] = p.astype(p_ref.dtype)
            low_ref[:, here] = p.astype(BF16)

        repeat(per_head, unroll, step)
        dv = dot_nn(low_ref[...], stacked_rows(g_ref, head, 2 * per_head)).astype(BF16)
        for shift in range(shifts):
            back_ref[shift, :, cols] = dv[shift * own_keys : (shift + 1) * own_keys]


def far_value_kernel(
    unroll, q_ref, g_ref, v_ref, p_ref, fin_ref, cross_ref, back_ref, ds_ref, delta_ref
):
    heads = v_ref.shape[1] // WIDTH
    per_head = q_ref.shape[1] // PAIR // heads
    shifts, own_keys, _ = back_ref.shape
    for head in range(heads):
        cols = slice(head * WIDTH, (head + 1) * WIDTH)

        def step(i):
            pair = head * per_head + i
            at = columns(pair, PAIR)
            here = columns(i, PAIR)
            d = dot_nt(v_ref[:, cols], pair_rows(g_ref, pair))
            p = p_ref[head, :, here].astype(F32)
            delta = cross_ref[0:1, at] * fin_ref[0:1, at] + jnp.sum(p * d, axis=0, keepdims=True)
            delta_ref[0:1, at] = delta
            ds_ref[head, :, here] = (p * (d - delta)).astype(BF16)

        repeat(per_head, unroll, step)
        dk = (dot_nn(ds_ref[head], stacked_rows(q_ref, head, 2 * per_head)) * SCALE).astype(BF16)
        for shift in range(shifts):
            back_ref[shift, :, cols] = dk[shift * own_keys : (shift + 1) * own_keys]


def last_kernel(
    unroll, q_ref, g_ref, k_ref, p_ref, d_ref, fin_ref, delta_ref, fk_ref, fds_ref,
    dq_ref, dtk_ref, dtv_ref, dok_ref, dov_ref, low_ref, ds_ref,
):
    tail = dtk_ref.shape[0]
    heads = k_ref.shape[1] // WIDTH
    per_head = q_ref.shape[1] // PAIR // heads
    for head in range(heads):
        cols = slice(head * WIDTH, (head + 1) * WIDTH)

        def step(i):
            pair = head * per_head + i
            at = columns(pair, PAIR)
            here = columns(i, PAIR)
            p = p_ref[head, :, here] * fin_ref[0:1, at]
            ds = (p * (d_ref[head, :, here] - delta_ref[0:1, at])).astype(BF16)
            low_ref[:, here] = p.astype(BF16)
            ds_ref[:, here] = ds
            dq = dot_tn(k_ref[:, cols], ds) + dot_tn(fk_ref[:, cols], fds_ref[head, :, here])
            dq = dq * SCALE
            dq = jnp.concatenate([dq[:, :WIDTH].T, dq[:, WIDTH:].T], axis=1)
            dq_ref[:, at] = dq.astype(BF16)

        repeat(per_head, unroll, step)
        dk = dot_nn(ds_ref[...], stacked_rows(q_ref, head, 2 * per_head)) * SCALE
        dv = dot_nn(low_ref[...], stacked_rows(g_ref, head, 2 * per_head))
        dtk_ref[:, cols] = dk[:tail].astype(BF16)
        dtv_ref[:, cols] = dv[:tail].astype(BF16)
        dok_ref[:, cols] = dk[tail:]
        dov_ref[:, cols] = dv[tail:]


def call(kernel, spaces, outs, scratch, flops, mib, *args):
    vmem = pl.BlockSpec(memory_space=pltpu.VMEM)
    moved = sum(a.size * a.dtype.itemsize for a in args) + sum(
        math.prod(o.shape) * o.dtype.itemsize for o in outs
    )
    return pl.pallas_call(
        kernel,
        out_shape=outs,
        in_specs=[pl.BlockSpec(memory_space=space) for space in spaces],
        out_specs=[vmem] * len(outs),
        scratch_shapes=scratch,
        compiler_params=pltpu.CompilerParams(vmem_limit_bytes=mib * 2**20),
        cost_estimate=pl.CostEstimate(flops=flops, bytes_accessed=moved, transcendentals=0),
    )(*args)


def body(q, g, tk, tv, ck, cv, row_list, read_owner, read_tile, read_list, read_count):
    ctx = lax.axis_size("ctx")
    rows, q_width = q.shape
    kv_width = tk.shape[1]
    heads = kv_width // WIDTH
    group_rows = rows * (q_width // kv_width)
    own_keys = ck.shape[0]
    own = own_keys // TILE
    far_keys = (ctx - 1) * own_keys
    near_keys = rows + own_keys
    slots = -(-ctx * own // 8) * 8
    unroll = ctx <= 2
    row_list = row_list.reshape(1, rows)

    def shifted(x, shift):
        return lax.ppermute(x, "ctx", [(o, (o - shift) % ctx) for o in range(ctx)])

    far_k = [shifted(ck, s) for s in range(1, ctx)]
    shape = jax.ShapeDtypeStruct
    product = 2 * q_width * rows * WIDTH
    small = read_owner.shape
    here = [
        pltpu.with_memory_space_constraint(a, pltpu.HBM)
        for a in (q, g, tk, tv, ck, cv, row_list, read_owner, read_tile, read_list)
    ]
    q, g, near_k, tv, cv, near_p, stats, table = call(
        functools.partial(near_key_kernel, ctx),
        [pltpu.HBM] * len(here) + [pltpu.SMEM],
        [
            shape(q.shape, BF16),
            shape(g.shape, BF16),
            shape((near_keys, kv_width), BF16),
            shape(tv.shape, BF16),
            shape(cv.shape, BF16),
            shape((heads, near_keys, group_rows), F32),
            shape((8, heads * group_rows), F32),
            shape((slots, rows), F32),
        ],
        [
            pltpu.VMEM(row_list.shape, jnp.int32),
            pltpu.VMEM(small, jnp.int32),
            pltpu.VMEM(small, jnp.int32),
            pltpu.VMEM(small, jnp.int32),
            pltpu.SemaphoreType.DMA((10,)),
        ],
        product * near_keys // WIDTH,
        32,
        *here, read_count,
    )
    far_v = [shifted(cv, s) for s in range(1, ctx)]
    near_d, cross = call(
        near_value_kernel,
        [pltpu.VMEM] * 4,
        [shape((heads, near_keys, group_rows), F32), shape((8, heads * group_rows), F32)],
        [],
        product * near_keys // WIDTH,
        32,
        g, tv, cv, near_p,
    )
    mib = 32 if unroll else 60
    far_k = far_k[0] if ctx == 2 else jnp.concatenate(far_k, axis=0)
    back_v, far_p, fin = call(
        functools.partial(far_key_kernel, unroll),
        [pltpu.VMEM] * 5,
        [
            shape((ctx - 1, own_keys, kv_width), BF16),
            shape((heads, far_keys, group_rows), F32 if unroll else BF16),
            shape((8, heads * group_rows), F32),
        ],
        [pltpu.VMEM((far_keys, group_rows), BF16)],
        2 * product * far_keys // WIDTH,
        mib,
        q, g, far_k, stats, table,
    )
    returned_v = [shifted(back_v[s - 1], -s) for s in range(1, ctx)]
    far_v = far_v[0] if ctx == 2 else jnp.concatenate(far_v, axis=0)
    back_k, far_ds, delta = call(
        functools.partial(far_value_kernel, unroll),
        [pltpu.VMEM] * 6,
        [
            shape((ctx - 1, own_keys, kv_width), BF16),
            shape((heads, far_keys, group_rows), BF16),
            shape((8, heads * group_rows), F32),
        ],
        [],
        2 * product * far_keys // WIDTH,
        mib,
        q, g, far_v, far_p, fin, cross,
    )
    returned_k = [shifted(back_k[s - 1], -s) for s in range(1, ctx)]
    dq, dtk, dtv, dok, dov = call(
        functools.partial(last_kernel, unroll),
        [pltpu.VMEM] * 9,
        [
            shape(q.shape, BF16),
            shape(tk.shape, BF16),
            shape(tv.shape, BF16),
            shape(ck.shape, F32),
            shape(cv.shape, F32),
        ],
        [pltpu.VMEM((near_keys, group_rows), BF16), pltpu.VMEM((near_keys, group_rows), BF16)],
        product * (3 * near_keys + far_keys) // WIDTH,
        mib,
        q, g, near_k, near_p, near_d, fin, delta, far_k, far_ds,
    )
    for key_block, value_block in zip(returned_k, returned_v):
        dok = dok + key_block.astype(F32)
        dov = dov + value_block.astype(F32)
    return dq, dtk, dtv, dok, dov


def solution(mesh):
    wide = P(("dp", "ctx"), "tp")
    lone = P(("dp", "ctx"))
    flat = P(("dp", "ctx"), None)
    return jax.shard_map(
        body,
        mesh=mesh,
        in_specs=(wide,) * 6 + (lone, flat, flat, flat, lone),
        out_specs=(wide,) * 5,
        check_vma=False,
    )
```

```python
import functools
import math

import jax
import jax.numpy as jnp
from jax import lax
from jax.experimental import pallas as pl
from jax.experimental.pallas import tpu as pltpu
from jax.sharding import PartitionSpec as P

WIDTH = 128
TILE = 128
PAIR = 2 * WIDTH
NEG = -1e30
SCALE = 1.0 / math.sqrt(WIDTH)
SCALE2 = SCALE * math.log2(math.e)
F32 = jnp.float32
BF16 = jnp.bfloat16


def dot_nt(a, b):
    return lax.dot_general(a, b, (((1,), (1,)), ((), ())), preferred_element_type=F32)


def dot_nn(a, b):
    return lax.dot_general(a, b, (((1,), (0,)), ((), ())), preferred_element_type=F32)


def dot_tn(a, b):
    return lax.dot_general(a, b, (((0,), (0,)), ((), ())), preferred_element_type=F32)


def repeat(steps, unroll, step):
    if unroll:
        for i in range(steps):
            step(i)
    else:

        def one(i, carry):
            step(i)
            return carry

        lax.fori_loop(0, steps, one, 0)


def columns(i, width):
    if isinstance(i, int):
        return pl.ds(i * width, width)
    return pl.ds(pl.multiple_of(i * width, width), width)


def pair_rows(ref, i):
    block = ref[:, columns(i, PAIR)]
    return jnp.concatenate([block[:, :WIDTH], block[:, WIDTH:]], axis=0)


def stacked_rows(ref, head, group):
    first = head * group
    return jnp.concatenate(
        [ref[:, (first + g) * WIDTH : (first + g + 1) * WIDTH] for g in range(group)], axis=0
    )


def twice(row):
    return jnp.concatenate([row, row], axis=1)


def tile_bias(table, first, tiles):
    return [twice(table[first + t : first + t + 1, :]) for t in range(tiles)]


def add_tiles(scores, biases):
    parts = [
        scores[t * TILE : (t + 1) * TILE, :] * SCALE2 + bias for t, bias in enumerate(biases)
    ]
    return parts[0] if len(parts) == 1 else jnp.concatenate(parts, axis=0)


def tail_bias(row_list):
    rows = row_list.shape[1]
    cut = jnp.sum((row_list == 0).astype(jnp.int32), axis=1, keepdims=True)
    key_at = lax.broadcasted_iota(jnp.int32, (rows, rows), 0)
    row_at = lax.broadcasted_iota(jnp.int32, (rows, rows), 1)
    allowed = ((key_at < cut) == (row_at < cut)) & (key_at <= row_at)
    return twice(jnp.where(allowed, 0.0, NEG).astype(F32))


def load_kernel(
    q_in, g_in, tk_in, ok_in, tv_in, ov_in, rl_in, ro_in, rt_in, rs_in,
    q_ref, g_ref, k_ref, tv_ref, ov_ref, rl_ref, ro_ref, rt_ref, rs_ref, sems,
):
    tail = tk_in.shape[0]
    moves = [
        (ov_in, ov_ref), (tk_in, k_ref.at[:tail]), (ok_in, k_ref.at[tail:]), (q_in, q_ref),
        (tv_in, tv_ref), (g_in, g_ref),
        (rl_in, rl_ref), (ro_in, ro_ref), (rt_in, rt_ref), (rs_in, rs_ref),
    ]
    copies = [pltpu.make_async_copy(a, b, sems.at[i]) for i, (a, b) in enumerate(moves)]
    for copy in copies:
        copy.start()
    for copy in copies:
        copy.wait()


def near_key_kernel(
    ctx, own, q_ref, k_ref, rl_ref, ro_ref, rt_ref, rs_ref, rc_ref, p_ref, stats_ref, table_ref
):
    heads = k_ref.shape[1] // WIDTH
    per_head = q_ref.shape[1] // PAIR // heads
    reads = ro_ref.shape[1]
    slots = table_ref.shape[0]
    row_list = rl_ref[...]
    owner = ro_ref[...] - lax.axis_index("ctx")
    owner = jnp.where(owner < 0, owner + ctx, owner)
    wanted = owner * own + rt_ref[...]
    live = lax.broadcasted_iota(jnp.int32, (1, reads), 1) < rc_ref[0]
    wanted = jnp.where(live, wanted, -1)
    hit = lax.broadcasted_iota(jnp.int32, (slots, reads), 0) == wanted
    first = rs_ref[...] == 0
    count0 = jnp.sum(jnp.where(hit & first, 1.0, 0.0), axis=1, keepdims=True)
    count1 = jnp.sum(jnp.where(hit & jnp.logical_not(first), 1.0, 0.0), axis=1, keepdims=True)
    count = jnp.where(row_list == 0, count0, count1)
    table = jnp.where(count > 0.5, jnp.log2(jnp.maximum(count, 1.0)), NEG)
    table_ref[...] = table
    biases = [tail_bias(row_list)] + tile_bias(table, 0, own)
    for head in range(heads):
        cols = slice(head * WIDTH, (head + 1) * WIDTH)
        for i in range(per_head):
            pair = head * per_head + i
            at = columns(pair, PAIR)
            s = add_tiles(dot_nt(k_ref[:, cols], pair_rows(q_ref, pair)), biases)
            top = jnp.max(s, axis=0, keepdims=True)
            p = jnp.exp2(s - top)
            p_ref[head, :, columns(i, PAIR)] = p
            stats_ref[0:1, at] = top
            stats_ref[1:2, at] = jnp.sum(p, axis=0, keepdims=True)


def near_value_kernel(g_ref, tv_ref, ov_ref, p_ref, d_ref, cross_ref):
    heads = tv_ref.shape[1] // WIDTH
    per_head = g_ref.shape[1] // PAIR // heads
    for head in range(heads):
        cols = slice(head * WIDTH, (head + 1) * WIDTH)
        values = jnp.concatenate([tv_ref[:, cols], ov_ref[:, cols]], axis=0)
        for i in range(per_head):
            pair = head * per_head + i
            here = columns(i, PAIR)
            d = dot_nt(values, pair_rows(g_ref, pair))
            d_ref[head, :, here] = d
            cross = jnp.sum(p_ref[head, :, here] * d, axis=0, keepdims=True)
            cross_ref[0:1, columns(pair, PAIR)] = cross


def far_key_kernel(
    unroll, q_ref, g_ref, k_ref, stats_ref, table_ref, back_ref, p_ref, fin_ref, low_ref
):
    far_tiles = k_ref.shape[0] // TILE
    heads = k_ref.shape[1] // WIDTH
    per_head = q_ref.shape[1] // PAIR // heads
    shifts, own_keys, _ = back_ref.shape
    biases = tile_bias(table_ref[...], own_keys // TILE, far_tiles)
    for head in range(heads):
        cols = slice(head * WIDTH, (head + 1) * WIDTH)

        def step(i):
            pair = head * per_head + i
            at = columns(pair, PAIR)
            here = columns(i, PAIR)
            s = add_tiles(dot_nt(k_ref[:, cols], pair_rows(q_ref, pair)), biases)
            near_top = stats_ref[0:1, at]
            top = jnp.maximum(near_top, jnp.max(s, axis=0, keepdims=True))
            p = jnp.exp2(s - top)
            fade = jnp.exp2(near_top - top)
            inverse = 1.0 / (stats_ref[1:2, at] * fade + jnp.sum(p, axis=0, keepdims=True))
            fin_ref[0:1, at] = fade * inverse
            p = p * inverse
            p_ref[head, :, here] = p.astype(p_ref.dtype)
            low_ref[:, here] = p.astype(BF16)

        repeat(per_head, unroll, step)
        dv = dot_nn(low_ref[...], stacked_rows(g_ref, head, 2 * per_head)).astype(BF16)
        for shift in range(shifts):
            back_ref[shift, :, cols] = dv[shift * own_keys : (shift + 1) * own_keys]


def far_value_kernel(
    unroll, q_ref, g_ref, v_ref, p_ref, fin_ref, cross_ref, back_ref, ds_ref, delta_ref
):
    heads = v_ref.shape[1] // WIDTH
    per_head = q_ref.shape[1] // PAIR // heads
    shifts, own_keys, _ = back_ref.shape
    for head in range(heads):
        cols = slice(head * WIDTH, (head + 1) * WIDTH)

        def step(i):
            pair = head * per_head + i
            at = columns(pair, PAIR)
            here = columns(i, PAIR)
            d = dot_nt(v_ref[:, cols], pair_rows(g_ref, pair))
            p = p_ref[head, :, here].astype(F32)
            delta = cross_ref[0:1, at] * fin_ref[0:1, at] + jnp.sum(p * d, axis=0, keepdims=True)
            delta_ref[0:1, at] = delta
            ds_ref[head, :, here] = (p * (d - delta)).astype(BF16)

        repeat(per_head, unroll, step)
        dk = (dot_nn(ds_ref[head], stacked_rows(q_ref, head, 2 * per_head)) * SCALE).astype(BF16)
        for shift in range(shifts):
            back_ref[shift, :, cols] = dk[shift * own_keys : (shift + 1) * own_keys]


def last_kernel(
    unroll, q_ref, g_ref, k_ref, p_ref, d_ref, fin_ref, delta_ref, fk_ref, fds_ref,
    dq_ref, dtk_ref, dtv_ref, dok_ref, dov_ref, low_ref, ds_ref,
):
    tail = dtk_ref.shape[0]
    heads = k_ref.shape[1] // WIDTH
    per_head = q_ref.shape[1] // PAIR // heads
    for head in range(heads):
        cols = slice(head * WIDTH, (head + 1) * WIDTH)

        def step(i):
            pair = head * per_head + i
            at = columns(pair, PAIR)
            here = columns(i, PAIR)
            p = p_ref[head, :, here] * fin_ref[0:1, at]
            ds = (p * (d_ref[head, :, here] - delta_ref[0:1, at])).astype(BF16)
            low_ref[:, here] = p.astype(BF16)
            ds_ref[:, here] = ds
            dq = dot_tn(k_ref[:, cols], ds) + dot_tn(fk_ref[:, cols], fds_ref[head, :, here])
            dq = dq * SCALE
            dq = jnp.concatenate([dq[:, :WIDTH].T, dq[:, WIDTH:].T], axis=1)
            dq_ref[:, at] = dq.astype(BF16)

        repeat(per_head, unroll, step)
        dk = dot_nn(ds_ref[...], stacked_rows(q_ref, head, 2 * per_head)) * SCALE
        dv = dot_nn(low_ref[...], stacked_rows(g_ref, head, 2 * per_head))
        dtk_ref[:, cols] = dk[:tail].astype(BF16)
        dtv_ref[:, cols] = dv[:tail].astype(BF16)
        dok_ref[:, cols] = dk[tail:]
        dov_ref[:, cols] = dv[tail:]


def call(kernel, spaces, outs, scratch, flops, mib, *args):
    vmem = pl.BlockSpec(memory_space=pltpu.VMEM)
    moved = sum(a.size * a.dtype.itemsize for a in args) + sum(
        math.prod(o.shape) * o.dtype.itemsize for o in outs
    )
    return pl.pallas_call(
        kernel,
        out_shape=outs,
        in_specs=[pl.BlockSpec(memory_space=space) for space in spaces],
        out_specs=[vmem] * len(outs),
        scratch_shapes=scratch,
        compiler_params=pltpu.CompilerParams(vmem_limit_bytes=mib * 2**20),
        cost_estimate=pl.CostEstimate(flops=flops, bytes_accessed=moved, transcendentals=0),
    )(*args)


def body(q, g, tk, tv, ck, cv, row_list, read_owner, read_tile, read_list, read_count):
    ctx = lax.axis_size("ctx")
    rows, q_width = q.shape
    kv_width = tk.shape[1]
    heads = kv_width // WIDTH
    group_rows = rows * (q_width // kv_width)
    own_keys = ck.shape[0]
    own = own_keys // TILE
    far_keys = (ctx - 1) * own_keys
    near_keys = rows + own_keys
    slots = -(-ctx * own // 8) * 8
    unroll = ctx <= 2
    row_list = row_list.reshape(1, rows)

    def shifted(x, shift):
        return lax.ppermute(x, "ctx", [(o, (o - shift) % ctx) for o in range(ctx)])

    far_k = [shifted(ck, s) for s in range(1, ctx)]
    shape = jax.ShapeDtypeStruct
    product = 2 * q_width * rows * WIDTH
    small = read_owner.shape
    here = [
        pltpu.with_memory_space_constraint(a, pltpu.HBM)
        for a in (q, g, tk, ck, tv, cv, row_list, read_owner, read_tile, read_list)
    ]
    integer = jnp.int32
    q, g, near_k, tv, cv, row_list, read_owner, read_tile, read_list = call(
        load_kernel,
        [pltpu.HBM] * len(here),
        [
            shape(q.shape, BF16),
            shape(g.shape, BF16),
            shape((near_keys, kv_width), BF16),
            shape(tv.shape, BF16),
            shape(cv.shape, BF16),
            shape(row_list.shape, integer),
            shape(small, integer),
            shape(small, integer),
            shape(small, integer),
        ],
        [pltpu.SemaphoreType.DMA((10,))],
        0,
        32,
        *here,
    )
    near_p, stats, table = call(
        functools.partial(near_key_kernel, ctx, own),
        [pltpu.VMEM] * 6 + [pltpu.SMEM],
        [
            shape((heads, near_keys, group_rows), F32),
            shape((8, heads * group_rows), F32),
            shape((slots, rows), F32),
        ],
        [],
        product * near_keys // WIDTH,
        32,
        q, near_k, row_list, read_owner, read_tile, read_list, read_count,
    )
    far_v = [shifted(cv, s) for s in range(1, ctx)]
    near_d, cross = call(
        near_value_kernel,
        [pltpu.VMEM] * 4,
        [shape((heads, near_keys, group_rows), F32), shape((8, heads * group_rows), F32)],
        [],
        product * near_keys // WIDTH,
        32,
        g, tv, cv, near_p,
    )
    mib = 32 if unroll else 60
    far_k = far_k[0] if ctx == 2 else jnp.concatenate(far_k, axis=0)
    back_v, far_p, fin = call(
        functools.partial(far_key_kernel, unroll),
        [pltpu.VMEM] * 5,
        [
            shape((ctx - 1, own_keys, kv_width), BF16),
            shape((heads, far_keys, group_rows), F32 if unroll else BF16),
            shape((8, heads * group_rows), F32),
        ],
        [pltpu.VMEM((far_keys, group_rows), BF16)],
        2 * product * far_keys // WIDTH,
        mib,
        q, g, far_k, stats, table,
    )
    returned_v = [shifted(back_v[s - 1], -s) for s in range(1, ctx)]
    far_v = far_v[0] if ctx == 2 else jnp.concatenate(far_v, axis=0)
    back_k, far_ds, delta = call(
        functools.partial(far_value_kernel, unroll),
        [pltpu.VMEM] * 6,
        [
            shape((ctx - 1, own_keys, kv_width), BF16),
            shape((heads, far_keys, group_rows), BF16),
            shape((8, heads * group_rows), F32),
        ],
        [],
        2 * product * far_keys // WIDTH,
        mib,
        q, g, far_v, far_p, fin, cross,
    )
    returned_k = [shifted(back_k[s - 1], -s) for s in range(1, ctx)]
    dq, dtk, dtv, dok, dov = call(
        functools.partial(last_kernel, unroll),
        [pltpu.VMEM] * 9,
        [
            shape(q.shape, BF16),
            shape(tk.shape, BF16),
            shape(tv.shape, BF16),
            shape(ck.shape, F32),
            shape(cv.shape, F32),
        ],
        [pltpu.VMEM((near_keys, group_rows), BF16), pltpu.VMEM((near_keys, group_rows), BF16)],
        product * (3 * near_keys + far_keys) // WIDTH,
        mib,
        q, g, near_k, near_p, near_d, fin, delta, far_k, far_ds,
    )
    for key_block, value_block in zip(returned_k, returned_v):
        dok = dok + key_block.astype(F32)
        dov = dov + value_block.astype(F32)
    return dq, dtk, dtv, dok, dov


def solution(mesh):
    wide = P(("dp", "ctx"), "tp")
    lone = P(("dp", "ctx"))
    flat = P(("dp", "ctx"), None)
    return jax.shard_map(
        body,
        mesh=mesh,
        in_specs=(wide,) * 6 + (lone, flat, flat, flat, lone),
        out_specs=(wide,) * 5,
        check_vma=False,
    )
```

```python
import functools
import math

import jax
import jax.numpy as jnp
from jax import lax
from jax.experimental import pallas as pl
from jax.experimental.pallas import tpu as pltpu
from jax.sharding import PartitionSpec as P

WIDTH = 128
TILE = 128
PAIR = 2 * WIDTH
PARTS = 2
NEG = -1e30
SCALE = 1.0 / math.sqrt(WIDTH)
SCALE2 = SCALE * math.log2(math.e)
F32 = jnp.float32
BF16 = jnp.bfloat16


def dot_nt(a, b):
    return lax.dot_general(a, b, (((1,), (1,)), ((), ())), preferred_element_type=F32)


def dot_nn(a, b):
    return lax.dot_general(a, b, (((1,), (0,)), ((), ())), preferred_element_type=F32)


def dot_tn(a, b):
    return lax.dot_general(a, b, (((0,), (0,)), ((), ())), preferred_element_type=F32)


def repeat(steps, unroll, step):
    if unroll:
        for i in range(steps):
            step(i)
    else:

        def one(i, carry):
            step(i)
            return carry

        lax.fori_loop(0, steps, one, 0)


def columns(i, width):
    if isinstance(i, int):
        return pl.ds(i * width, width)
    return pl.ds(pl.multiple_of(i * width, width), width)


def pair_rows(ref, i):
    block = ref[:, columns(i, PAIR)]
    return jnp.concatenate([block[:, :WIDTH], block[:, WIDTH:]], axis=0)


def stacked_rows(ref, head, group):
    first = head * group
    return jnp.concatenate(
        [ref[:, (first + g) * WIDTH : (first + g + 1) * WIDTH] for g in range(group)], axis=0
    )


def twice(row):
    return jnp.concatenate([row, row], axis=1)


def tile_bias(table, first, tiles):
    return [twice(table[first + t : first + t + 1, :]) for t in range(tiles)]


def add_tiles(scores, biases):
    parts = [
        scores[t * TILE : (t + 1) * TILE, :] * SCALE2 + bias for t, bias in enumerate(biases)
    ]
    return parts[0] if len(parts) == 1 else jnp.concatenate(parts, axis=0)


def tail_bias(row_list):
    rows = row_list.shape[1]
    cut = jnp.sum((row_list == 0).astype(jnp.int32), axis=1, keepdims=True)
    key_at = lax.broadcasted_iota(jnp.int32, (rows, rows), 0)
    row_at = lax.broadcasted_iota(jnp.int32, (rows, rows), 1)
    allowed = ((key_at < cut) == (row_at < cut)) & (key_at <= row_at)
    return twice(jnp.where(allowed, 0.0, NEG).astype(F32))


def near_kernel(
    ctx, q_in, g_in, tk_in, tv_in, ok_in, ov_in, rl_in, ro_in, rt_in, rs_in, rc_ref,
    q_ref, g_ref, k_ref, p_ref, d_ref, stats_ref, table_ref,
    v_ref, rl_ref, ro_ref, rt_ref, rs_ref, sems,
):
    tail = tk_in.shape[0]
    own = ok_in.shape[0] // TILE
    heads = tk_in.shape[1] // WIDTH
    pairs = q_ref.shape[1] // PAIR
    reads = ro_ref.shape[1]
    slots = table_ref.shape[0]
    moves = [
        (rl_in, rl_ref), (ro_in, ro_ref), (rt_in, rt_ref), (rs_in, rs_ref),
        (tk_in, k_ref.at[:tail]), (ok_in, k_ref.at[tail:]), (q_in, q_ref),
        (tv_in, v_ref.at[:tail]), (ov_in, v_ref.at[tail:]), (g_in, g_ref),
    ]
    copies = [pltpu.make_async_copy(a, b, sems.at[i]) for i, (a, b) in enumerate(moves)]
    for copy in copies:
        copy.start()
    for copy in copies[:4]:
        copy.wait()
    row_list = rl_ref[...]
    owner = ro_ref[...] - lax.axis_index("ctx")
    owner = jnp.where(owner < 0, owner + ctx, owner)
    wanted = owner * own + rt_ref[...]
    live = lax.broadcasted_iota(jnp.int32, (1, reads), 1) < rc_ref[0]
    wanted = jnp.where(live, wanted, -1)
    hit = lax.broadcasted_iota(jnp.int32, (slots, reads), 0) == wanted
    first = rs_ref[...] == 0
    count0 = jnp.sum(jnp.where(hit & first, 1.0, 0.0), axis=1, keepdims=True)
    count1 = jnp.sum(jnp.where(hit & jnp.logical_not(first), 1.0, 0.0), axis=1, keepdims=True)
    count = jnp.where(row_list == 0, count0, count1)
    table = jnp.where(count > 0.5, jnp.log2(jnp.maximum(count, 1.0)), NEG)
    table_ref[...] = table
    biases = [tail_bias(row_list)] + tile_bias(table, 0, own)
    for copy in copies[4:]:
        copy.wait()
    for head in range(heads):
        cols = slice(head * WIDTH, (head + 1) * WIDTH)
        for pair in range(head * pairs // heads, (head + 1) * pairs // heads):
            s = add_tiles(dot_nt(k_ref[:, cols], pair_rows(q_ref, pair)), biases)
            top = jnp.max(s, axis=0, keepdims=True)
            p = jnp.exp2(s - top)
            d = dot_nt(v_ref[:, cols], pair_rows(g_ref, pair))
            at = slice(pair * PAIR, (pair + 1) * PAIR)
            here = columns(pair - head * pairs // heads, PAIR)
            p_ref[head, :, here] = p
            d_ref[head, :, here] = d
            stats_ref[0:1, at] = top
            stats_ref[1:2, at] = jnp.sum(p, axis=0, keepdims=True)
            stats_ref[2:3, at] = jnp.sum(p * d, axis=0, keepdims=True)


def far_key_kernel(
    unroll, q_ref, g_ref, k_ref, stats_ref, table_ref, back_ref, p_ref, fin_ref, low_ref
):
    far_tiles = k_ref.shape[0] // TILE
    heads = k_ref.shape[1] // WIDTH
    per_head = q_ref.shape[1] // PAIR // heads
    biases = tile_bias(table_ref[...], back_ref.shape[1] // TILE, far_tiles)
    for head in range(heads):
        cols = slice(head * WIDTH, (head + 1) * WIDTH)

        def step(i):
            pair = head * per_head + i
            at = columns(pair, PAIR)
            here = columns(i, PAIR)
            s = add_tiles(dot_nt(k_ref[:, cols], pair_rows(q_ref, pair)), biases)
            near_top = stats_ref[0:1, at]
            top = jnp.maximum(near_top, jnp.max(s, axis=0, keepdims=True))
            p = jnp.exp2(s - top)
            fade = jnp.exp2(near_top - top)
            inverse = 1.0 / (stats_ref[1:2, at] * fade + jnp.sum(p, axis=0, keepdims=True))
            fade = fade * inverse
            fin_ref[0:1, at] = fade
            fin_ref[1:2, at] = stats_ref[2:3, at] * fade
            p = p * inverse
            p_ref[head, :, here] = p.astype(p_ref.dtype)
            low_ref[:, here] = p.astype(BF16)

        repeat(per_head, unroll, step)
        dv = dot_nn(low_ref[...], stacked_rows(g_ref, head, 2 * per_head)).astype(BF16)
        store_parts([back_ref], cols, dv)


def far_value_kernel(unroll, q_ref, g_ref, v_ref, p_ref, fin_ref, *refs):
    back_refs, (ds_ref, delta_ref) = refs[:PARTS], refs[PARTS:]
    heads = v_ref.shape[1] // WIDTH
    per_head = q_ref.shape[1] // PAIR // heads
    for head in range(heads):
        cols = slice(head * WIDTH, (head + 1) * WIDTH)

        def step(i):
            pair = head * per_head + i
            at = columns(pair, PAIR)
            here = columns(i, PAIR)
            d = dot_nt(v_ref[:, cols], pair_rows(g_ref, pair))
            p = p_ref[head, :, here].astype(F32)
            delta = fin_ref[1:2, at] + jnp.sum(p * d, axis=0, keepdims=True)
            delta_ref[0:1, at] = delta
            ds_ref[head, :, here] = (p * (d - delta)).astype(BF16)

        repeat(per_head, unroll, step)
        dk = (dot_nn(ds_ref[head], stacked_rows(q_ref, head, 2 * per_head)) * SCALE).astype(BF16)
        store_parts(back_refs, cols, dk)


def store_parts(refs, cols, terms):
    shifts, keys, _ = refs[0].shape
    for shift in range(shifts):
        for part, ref in enumerate(refs):
            first = (shift * len(refs) + part) * keys
            ref[shift, :, cols] = terms[first : first + keys]


def sum_kernel(after_ref, own_ref, *refs):
    out_ref = refs[-1]
    keys = refs[0].shape[0]
    parts = out_ref.shape[0] // keys
    for part in range(parts):
        rows = slice(part * keys, (part + 1) * keys)
        total = own_ref[rows, :]
        for ref in refs[part:-1:parts]:
            total = total + ref[...].astype(F32)
        out_ref[rows, :] = total


def last_kernel(
    unroll, q_ref, g_ref, k_ref, p_ref, d_ref, fin_ref, delta_ref, fk_ref, fds_ref,
    dq_ref, dtk_ref, dtv_ref, dok_ref, dov_ref, low_ref, ds_ref,
):
    tail = dtk_ref.shape[0]
    heads = k_ref.shape[1] // WIDTH
    per_head = q_ref.shape[1] // PAIR // heads
    for head in range(heads):
        cols = slice(head * WIDTH, (head + 1) * WIDTH)

        def step(i):
            pair = head * per_head + i
            at = columns(pair, PAIR)
            here = columns(i, PAIR)
            p = p_ref[head, :, here] * fin_ref[0:1, at]
            ds = (p * (d_ref[head, :, here] - delta_ref[0:1, at])).astype(BF16)
            low_ref[:, here] = p.astype(BF16)
            ds_ref[:, here] = ds
            dq = dot_tn(k_ref[:, cols], ds) + dot_tn(fk_ref[:, cols], fds_ref[head, :, here])
            dq = dq * SCALE
            dq = jnp.concatenate([dq[:, :WIDTH].T, dq[:, WIDTH:].T], axis=1)
            dq_ref[:, at] = dq.astype(BF16)

        repeat(per_head, unroll, step)
        dk = dot_nn(ds_ref[...], stacked_rows(q_ref, head, 2 * per_head)) * SCALE
        dv = dot_nn(low_ref[...], stacked_rows(g_ref, head, 2 * per_head))
        dtk_ref[:, cols] = dk[:tail].astype(BF16)
        dtv_ref[:, cols] = dv[:tail].astype(BF16)
        dok_ref[:, cols] = dk[tail:]
        dov_ref[:, cols] = dv[tail:]


def call(kernel, spaces, outs, scratch, flops, mib, *args):
    vmem = pl.BlockSpec(memory_space=pltpu.VMEM)
    moved = sum(a.size * a.dtype.itemsize for a in args) + sum(
        math.prod(o.shape) * o.dtype.itemsize for o in outs
    )
    return pl.pallas_call(
        kernel,
        out_shape=outs,
        in_specs=[pl.BlockSpec(memory_space=space) for space in spaces],
        out_specs=[vmem] * len(outs),
        scratch_shapes=scratch,
        compiler_params=pltpu.CompilerParams(vmem_limit_bytes=mib * 2**20),
        cost_estimate=pl.CostEstimate(flops=flops, bytes_accessed=moved, transcendentals=0),
    )(*args)


def body(q, g, tk, tv, ck, cv, row_list, read_owner, read_tile, read_list, read_count):
    ctx = lax.axis_size("ctx")
    rows, q_width = q.shape
    kv_width = tk.shape[1]
    heads = kv_width // WIDTH
    group_rows = rows * (q_width // kv_width)
    own_keys = ck.shape[0]
    own = own_keys // TILE
    far_keys = (ctx - 1) * own_keys
    near_keys = rows + own_keys
    slots = -(-ctx * own // 8) * 8
    unroll = ctx <= 2
    row_list = row_list.reshape(1, rows)

    def shifted(x, shift):
        return lax.ppermute(x, "ctx", [(o, (o - shift) % ctx) for o in range(ctx)])

    far_k = [shifted(ck, s) for s in range(1, ctx)]
    far_v = [shifted(cv, s) for s in range(1, ctx)]
    shape = jax.ShapeDtypeStruct
    product = 2 * q_width * rows * WIDTH
    small = read_owner.shape
    here = [
        pltpu.with_memory_space_constraint(a, pltpu.HBM)
        for a in (q, g, tk, tv, ck, cv, row_list, read_owner, read_tile, read_list)
    ]
    q, g, near_k, near_p, near_d, stats, table = call(
        functools.partial(near_kernel, ctx),
        [pltpu.HBM] * len(here) + [pltpu.SMEM],
        [
            shape(q.shape, BF16),
            shape(g.shape, BF16),
            shape((near_keys, kv_width), BF16),
            shape((heads, near_keys, group_rows), F32),
            shape((heads, near_keys, group_rows), F32),
            shape((8, heads * group_rows), F32),
            shape((slots, rows), F32),
        ],
        [
            pltpu.VMEM((near_keys, kv_width), BF16),
            pltpu.VMEM(row_list.shape, jnp.int32),
            pltpu.VMEM(small, jnp.int32),
            pltpu.VMEM(small, jnp.int32),
            pltpu.VMEM(small, jnp.int32),
            pltpu.SemaphoreType.DMA((10,)),
        ],
        2 * product * near_keys // WIDTH,
        32,
        *here, read_count,
    )
    mib = 32 if unroll else 60
    far_k = far_k[0] if ctx == 2 else jnp.concatenate(far_k, axis=0)
    back_v, far_p, fin = call(
        functools.partial(far_key_kernel, unroll),
        [pltpu.VMEM] * 5,
        [
            shape((ctx - 1, own_keys, kv_width), BF16),
            shape((heads, far_keys, group_rows), F32 if unroll else BF16),
            shape((8, heads * group_rows), F32),
        ],
        [pltpu.VMEM((far_keys, group_rows), BF16)],
        2 * product * far_keys // WIDTH,
        mib,
        q, g, far_k, stats, table,
    )
    returned_v = [shifted(back_v[s - 1], -s) for s in range(1, ctx)]
    far_v = far_v[0] if ctx == 2 else jnp.concatenate(far_v, axis=0)
    *back_k, far_ds, delta = call(
        functools.partial(far_value_kernel, unroll),
        [pltpu.VMEM] * 5,
        [shape((ctx - 1, own_keys // PARTS, kv_width), BF16)] * PARTS
        + [
            shape((heads, far_keys, group_rows), BF16),
            shape((8, heads * group_rows), F32),
        ],
        [],
        2 * product * far_keys // WIDTH,
        mib,
        q, g, far_v, far_p, fin,
    )
    returned_k = [shifted(b[s - 1], -s) for s in range(1, ctx) for b in back_k]
    dq, dtk, dtv, dok, dov = call(
        functools.partial(last_kernel, unroll),
        [pltpu.VMEM] * 9,
        [
            shape(q.shape, BF16),
            shape(tk.shape, BF16),
            shape(tv.shape, BF16),
            shape(ck.shape, F32),
            shape(cv.shape, F32),
        ],
        [pltpu.VMEM((near_keys, group_rows), BF16), pltpu.VMEM((near_keys, group_rows), BF16)],
        product * (3 * near_keys + far_keys) // WIDTH,
        mib,
        q, g, near_k, near_p, near_d, fin, delta, far_k, far_ds,
    )

    def summed(after, own_sum, returned):
        return call(
            sum_kernel,
            [pltpu.HBM] + [pltpu.VMEM] * (1 + len(returned)),
            [shape(own_sum.shape, F32)],
            [],
            0,
            mib,
            pltpu.with_memory_space_constraint(after, pltpu.HBM), own_sum, *returned,
        )[0]

    dov = summed(dq, dov, returned_v)
    dok = summed(dov, dok, returned_k)
    return dq, dtk, dtv, dok, dov


def solution(mesh):
    wide = P(("dp", "ctx"), "tp")
    lone = P(("dp", "ctx"))
    flat = P(("dp", "ctx"), None)
    return jax.shard_map(
        body,
        mesh=mesh,
        in_specs=(wide,) * 6 + (lone, flat, flat, flat, lone),
        out_specs=(wide,) * 5,
        check_vma=False,
    )
```

```python
import functools
import math

import jax
import jax.numpy as jnp
from jax import lax
from jax.experimental import pallas as pl
from jax.experimental.pallas import tpu as pltpu
from jax.sharding import PartitionSpec as P

WIDTH = 128
TILE = 128
PAIR = 2 * WIDTH
NEG = -1e30
SCALE = 1.0 / math.sqrt(WIDTH)
SCALE2 = SCALE * math.log2(math.e)
F32 = jnp.float32
BF16 = jnp.bfloat16


def dot_nt(a, b):
    return lax.dot_general(a, b, (((1,), (1,)), ((), ())), preferred_element_type=F32)


def dot_nn(a, b):
    return lax.dot_general(a, b, (((1,), (0,)), ((), ())), preferred_element_type=F32)


def dot_tn(a, b):
    return lax.dot_general(a, b, (((0,), (0,)), ((), ())), preferred_element_type=F32)


def repeat(steps, unroll, step):
    if unroll:
        for i in range(steps):
            step(i)
    else:

        def one(i, carry):
            step(i)
            return carry

        lax.fori_loop(0, steps, one, 0)


def columns(i, width):
    if isinstance(i, int):
        return pl.ds(i * width, width)
    return pl.ds(pl.multiple_of(i * width, width), width)


def pair_rows(ref, i):
    block = ref[:, columns(i, PAIR)]
    return jnp.concatenate([block[:, :WIDTH], block[:, WIDTH:]], axis=0)


def stacked_rows(ref, head, group):
    first = head * group
    return jnp.concatenate(
        [ref[:, (first + g) * WIDTH : (first + g + 1) * WIDTH] for g in range(group)], axis=0
    )


def twice(row):
    return jnp.concatenate([row, row], axis=1)


def tile_bias(table, first, tiles):
    return [twice(table[first + t : first + t + 1, :]) for t in range(tiles)]


def add_tiles(scores, biases):
    parts = [
        scores[t * TILE : (t + 1) * TILE, :] * SCALE2 + bias for t, bias in enumerate(biases)
    ]
    return parts[0] if len(parts) == 1 else jnp.concatenate(parts, axis=0)


def tail_bias(row_list):
    rows = row_list.shape[1]
    cut = jnp.sum((row_list == 0).astype(jnp.int32), axis=1, keepdims=True)
    key_at = lax.broadcasted_iota(jnp.int32, (rows, rows), 0)
    row_at = lax.broadcasted_iota(jnp.int32, (rows, rows), 1)
    allowed = ((key_at < cut) == (row_at < cut)) & (key_at <= row_at)
    return twice(jnp.where(allowed, 0.0, NEG).astype(F32))


def near_kernel(
    ctx, q_in, g_in, tk_in, tv_in, ok_in, ov_in, rl_in, ro_in, rt_in, rs_in, rc_ref,
    q_ref, g_ref, k_ref, p_ref, d_ref, stats_ref, table_ref,
    v_ref, rl_ref, ro_ref, rt_ref, rs_ref, sems,
):
    tail = tk_in.shape[0]
    own = ok_in.shape[0] // TILE
    heads = tk_in.shape[1] // WIDTH
    pairs = q_ref.shape[1] // PAIR
    reads = ro_ref.shape[1]
    slots = table_ref.shape[0]
    moves = [
        (rl_in, rl_ref), (ro_in, ro_ref), (rt_in, rt_ref), (rs_in, rs_ref),
        (tk_in, k_ref.at[:tail]), (ok_in, k_ref.at[tail:]), (q_in, q_ref),
        (tv_in, v_ref.at[:tail]), (ov_in, v_ref.at[tail:]), (g_in, g_ref),
    ]
    copies = [pltpu.make_async_copy(a, b, sems.at[i]) for i, (a, b) in enumerate(moves)]
    for copy in copies:
        copy.start()
    for copy in copies[:4]:
        copy.wait()
    row_list = rl_ref[...]
    owner = ro_ref[...] - lax.axis_index("ctx")
    owner = jnp.where(owner < 0, owner + ctx, owner)
    wanted = owner * own + rt_ref[...]
    live = lax.broadcasted_iota(jnp.int32, (1, reads), 1) < rc_ref[0]
    wanted = jnp.where(live, wanted, -1)
    hit = lax.broadcasted_iota(jnp.int32, (slots, reads), 0) == wanted
    first = rs_ref[...] == 0
    count0 = jnp.sum(jnp.where(hit & first, 1.0, 0.0), axis=1, keepdims=True)
    count1 = jnp.sum(jnp.where(hit & jnp.logical_not(first), 1.0, 0.0), axis=1, keepdims=True)
    count = jnp.where(row_list == 0, count0, count1)
    table = jnp.where(count > 0.5, jnp.log2(jnp.maximum(count, 1.0)), NEG)
    table_ref[...] = table
    biases = [tail_bias(row_list)] + tile_bias(table, 0, own)
    for copy in copies[4:]:
        copy.wait()
    for head in range(heads):
        cols = slice(head * WIDTH, (head + 1) * WIDTH)
        for pair in range(head * pairs // heads, (head + 1) * pairs // heads):
            s = add_tiles(dot_nt(k_ref[:, cols], pair_rows(q_ref, pair)), biases)
            top = jnp.max(s, axis=0, keepdims=True)
            p = jnp.exp2(s - top)
            d = dot_nt(v_ref[:, cols], pair_rows(g_ref, pair))
            at = slice(pair * PAIR, (pair + 1) * PAIR)
            here = columns(pair - head * pairs // heads, PAIR)
            p_ref[head, :, here] = p
            d_ref[head, :, here] = d
            stats_ref[0:1, at] = top
            stats_ref[1:2, at] = jnp.sum(p, axis=0, keepdims=True)
            stats_ref[2:3, at] = jnp.sum(p * d, axis=0, keepdims=True)


def load_far(all_ref, far_ref, sems):
    keys = all_ref.shape[0] - far_ref.shape[0]
    shifts = far_ref.shape[0] // keys
    ctx = shifts + 1
    me = lax.axis_index("ctx")
    copies = []
    for shift in range(shifts):
        owner = lax.rem(me + shift + 1, ctx)
        copies.append(
            pltpu.make_async_copy(
                all_ref.at[pl.ds(pl.multiple_of(owner * keys, keys), keys)],
                far_ref.at[shift * keys : (shift + 1) * keys],
                sems.at[shift],
            )
        )
    for copy in copies:
        copy.start()
    for copy in copies:
        copy.wait()


def far_key_kernel(
    unroll, q_ref, g_ref, all_ref, stats_ref, table_ref, back_ref, p_ref, fin_ref, k_ref, low_ref, sems
):
    load_far(all_ref, k_ref, sems)
    far_tiles = k_ref.shape[0] // TILE
    heads = k_ref.shape[1] // WIDTH
    per_head = q_ref.shape[1] // PAIR // heads
    shifts, own_keys, _ = back_ref.shape
    biases = tile_bias(table_ref[...], own_keys // TILE, far_tiles)
    for head in range(heads):
        cols = slice(head * WIDTH, (head + 1) * WIDTH)

        def step(i):
            pair = head * per_head + i
            at = columns(pair, PAIR)
            here = columns(i, PAIR)
            s = add_tiles(dot_nt(k_ref[:, cols], pair_rows(q_ref, pair)), biases)
            near_top = stats_ref[0:1, at]
            top = jnp.maximum(near_top, jnp.max(s, axis=0, keepdims=True))
            p = jnp.exp2(s - top)
            fade = jnp.exp2(near_top - top)
            inverse = 1.0 / (stats_ref[1:2, at] * fade + jnp.sum(p, axis=0, keepdims=True))
            fade = fade * inverse
            fin_ref[0:1, at] = fade
            fin_ref[1:2, at] = stats_ref[2:3, at] * fade
            p = p * inverse
            p_ref[head, :, here] = p.astype(p_ref.dtype)
            low_ref[:, here] = p.astype(BF16)

        repeat(per_head, unroll, step)
        dv = dot_nn(low_ref[...], stacked_rows(g_ref, head, 2 * per_head)).astype(BF16)
        for shift in range(shifts):
            back_ref[shift, :, cols] = dv[shift * own_keys : (shift + 1) * own_keys]


def far_value_kernel(
    unroll, q_ref, g_ref, all_ref, p_ref, fin_ref, back_ref, ds_ref, delta_ref, v_ref, sems
):
    load_far(all_ref, v_ref, sems)
    heads = v_ref.shape[1] // WIDTH
    per_head = q_ref.shape[1] // PAIR // heads
    shifts, own_keys, _ = back_ref.shape
    for head in range(heads):
        cols = slice(head * WIDTH, (head + 1) * WIDTH)

        def step(i):
            pair = head * per_head + i
            at = columns(pair, PAIR)
            here = columns(i, PAIR)
            d = dot_nt(v_ref[:, cols], pair_rows(g_ref, pair))
            p = p_ref[head, :, here].astype(F32)
            delta = fin_ref[1:2, at] + jnp.sum(p * d, axis=0, keepdims=True)
            delta_ref[0:1, at] = delta
            ds_ref[head, :, here] = (p * (d - delta)).astype(BF16)

        repeat(per_head, unroll, step)
        dk = (dot_nn(ds_ref[head], stacked_rows(q_ref, head, 2 * per_head)) * SCALE).astype(BF16)
        for shift in range(shifts):
            back_ref[shift, :, cols] = dk[shift * own_keys : (shift + 1) * own_keys]


def last_kernel(
    unroll, q_ref, g_ref, k_ref, p_ref, d_ref, fin_ref, delta_ref, fk_ref, fds_ref,
    dq_ref, dtk_ref, dtv_ref, dok_ref, dov_ref, low_ref, ds_ref,
):
    tail = dtk_ref.shape[0]
    heads = k_ref.shape[1] // WIDTH
    per_head = q_ref.shape[1] // PAIR // heads
    for head in range(heads):
        cols = slice(head * WIDTH, (head + 1) * WIDTH)

        def step(i):
            pair = head * per_head + i
            at = columns(pair, PAIR)
            here = columns(i, PAIR)
            p = p_ref[head, :, here] * fin_ref[0:1, at]
            ds = (p * (d_ref[head, :, here] - delta_ref[0:1, at])).astype(BF16)
            low_ref[:, here] = p.astype(BF16)
            ds_ref[:, here] = ds
            dq = dot_tn(k_ref[:, cols], ds) + dot_tn(fk_ref[:, cols], fds_ref[head, :, here])
            dq = dq * SCALE
            dq = jnp.concatenate([dq[:, :WIDTH].T, dq[:, WIDTH:].T], axis=1)
            dq_ref[:, at] = dq.astype(BF16)

        repeat(per_head, unroll, step)
        dk = dot_nn(ds_ref[...], stacked_rows(q_ref, head, 2 * per_head)) * SCALE
        dv = dot_nn(low_ref[...], stacked_rows(g_ref, head, 2 * per_head))
        dtk_ref[:, cols] = dk[:tail].astype(BF16)
        dtv_ref[:, cols] = dv[:tail].astype(BF16)
        dok_ref[:, cols] = dk[tail:]
        dov_ref[:, cols] = dv[tail:]


def call(kernel, spaces, outs, scratch, flops, mib, *args):
    vmem = pl.BlockSpec(memory_space=pltpu.VMEM)
    moved = sum(a.size * a.dtype.itemsize for a in args) + sum(
        math.prod(o.shape) * o.dtype.itemsize for o in outs
    )
    return pl.pallas_call(
        kernel,
        out_shape=outs,
        in_specs=[pl.BlockSpec(memory_space=space) for space in spaces],
        out_specs=[vmem] * len(outs),
        scratch_shapes=scratch,
        compiler_params=pltpu.CompilerParams(vmem_limit_bytes=mib * 2**20),
        cost_estimate=pl.CostEstimate(flops=flops, bytes_accessed=moved, transcendentals=0),
    )(*args)


def body(q, g, tk, tv, ck, cv, row_list, read_owner, read_tile, read_list, read_count):
    ctx = lax.axis_size("ctx")
    rows, q_width = q.shape
    kv_width = tk.shape[1]
    heads = kv_width // WIDTH
    group_rows = rows * (q_width // kv_width)
    own_keys = ck.shape[0]
    own = own_keys // TILE
    far_keys = (ctx - 1) * own_keys
    near_keys = rows + own_keys
    slots = -(-ctx * own // 8) * 8
    unroll = ctx <= 2
    row_list = row_list.reshape(1, rows)

    def shifted(x, shift):
        return lax.ppermute(x, "ctx", [(o, (o - shift) % ctx) for o in range(ctx)])

    all_k = lax.all_gather(ck, "ctx", axis=0, tiled=True)
    all_v = lax.all_gather(cv, "ctx", axis=0, tiled=True)
    shape = jax.ShapeDtypeStruct
    product = 2 * q_width * rows * WIDTH
    small = read_owner.shape
    here = [
        pltpu.with_memory_space_constraint(a, pltpu.HBM)
        for a in (q, g, tk, tv, ck, cv, row_list, read_owner, read_tile, read_list)
    ]
    q, g, near_k, near_p, near_d, stats, table = call(
        functools.partial(near_kernel, ctx),
        [pltpu.HBM] * len(here) + [pltpu.SMEM],
        [
            shape(q.shape, BF16),
            shape(g.shape, BF16),
            shape((near_keys, kv_width), BF16),
            shape((heads, near_keys, group_rows), F32),
            shape((heads, near_keys, group_rows), F32),
            shape((8, heads * group_rows), F32),
            shape((slots, rows), F32),
        ],
        [
            pltpu.VMEM((near_keys, kv_width), BF16),
            pltpu.VMEM(row_list.shape, jnp.int32),
            pltpu.VMEM(small, jnp.int32),
            pltpu.VMEM(small, jnp.int32),
            pltpu.VMEM(small, jnp.int32),
            pltpu.SemaphoreType.DMA((10,)),
        ],
        2 * product * near_keys // WIDTH,
        32,
        *here, read_count,
    )
    mib = 32 if unroll else 60
    back_v, far_p, fin, far_k = call(
        functools.partial(far_key_kernel, unroll),
        [pltpu.VMEM, pltpu.VMEM, pltpu.HBM, pltpu.VMEM, pltpu.VMEM],
        [
            shape((ctx - 1, own_keys, kv_width), BF16),
            shape((heads, far_keys, group_rows), F32 if unroll else BF16),
            shape((8, heads * group_rows), F32),
            shape((far_keys, kv_width), BF16),
        ],
        [pltpu.VMEM((far_keys, group_rows), BF16), pltpu.SemaphoreType.DMA((ctx - 1,))],
        2 * product * far_keys // WIDTH,
        mib,
        q, g, pltpu.with_memory_space_constraint(all_k, pltpu.HBM), stats, table,
    )
    returned_v = [shifted(back_v[s - 1], -s) for s in range(1, ctx)]
    back_k, far_ds, delta = call(
        functools.partial(far_value_kernel, unroll),
        [pltpu.VMEM, pltpu.VMEM, pltpu.HBM, pltpu.VMEM, pltpu.VMEM],
        [
            shape((ctx - 1, own_keys, kv_width), BF16),
            shape((heads, far_keys, group_rows), BF16),
            shape((8, heads * group_rows), F32),
        ],
        [pltpu.VMEM((far_keys, kv_width), BF16), pltpu.SemaphoreType.DMA((ctx - 1,))],
        2 * product * far_keys // WIDTH,
        mib,
        q, g, pltpu.with_memory_space_constraint(all_v, pltpu.HBM), far_p, fin,
    )
    returned_k = [shifted(back_k[s - 1], -s) for s in range(1, ctx)]
    dq, dtk, dtv, dok, dov = call(
        functools.partial(last_kernel, unroll),
        [pltpu.VMEM] * 9,
        [
            shape(q.shape, BF16),
            shape(tk.shape, BF16),
            shape(tv.shape, BF16),
            shape(ck.shape, F32),
            shape(cv.shape, F32),
        ],
        [pltpu.VMEM((near_keys, group_rows), BF16), pltpu.VMEM((near_keys, group_rows), BF16)],
        product * (3 * near_keys + far_keys) // WIDTH,
        mib,
        q, g, near_k, near_p, near_d, fin, delta, far_k, far_ds,
    )
    for key_block, value_block in zip(returned_k, returned_v):
        dok = dok + key_block.astype(F32)
        dov = dov + value_block.astype(F32)
    return dq, dtk, dtv, dok, dov


def solution(mesh):
    wide = P(("dp", "ctx"), "tp")
    lone = P(("dp", "ctx"))
    flat = P(("dp", "ctx"), None)
    return jax.shard_map(
        body,
        mesh=mesh,
        in_specs=(wide,) * 6 + (lone, flat, flat, flat, lone),
        out_specs=(wide,) * 5,
        check_vma=False,
    )
```

```python
import functools
import math

import jax
import jax.numpy as jnp
from jax import lax
from jax.experimental import pallas as pl
from jax.experimental.pallas import tpu as pltpu
from jax.sharding import PartitionSpec as P

WIDTH = 128
TILE = 128
PAIR = 2 * WIDTH
NEG = -1e30
SCALE = 1.0 / math.sqrt(WIDTH)
SCALE2 = SCALE * math.log2(math.e)
F32 = jnp.float32
BF16 = jnp.bfloat16


def dot_nt(a, b):
    return lax.dot_general(a, b, (((1,), (1,)), ((), ())), preferred_element_type=F32)


def dot_nn(a, b):
    return lax.dot_general(a, b, (((1,), (0,)), ((), ())), preferred_element_type=F32)


def dot_tn(a, b):
    return lax.dot_general(a, b, (((0,), (0,)), ((), ())), preferred_element_type=F32)


def repeat(steps, unroll, step):
    if unroll:
        for i in range(steps):
            step(i)
    else:

        def one(i, carry):
            step(i)
            return carry

        lax.fori_loop(0, steps, one, 0)


def added(steps, unroll, step, total_ref):
    if unroll:
        return functools.reduce(jnp.add, [step(i) for i in range(steps)])
    (total_ref,) = total_ref
    total_ref[...] = jnp.zeros_like(total_ref)

    def one(i):
        total_ref[...] += step(i)

    repeat(steps, unroll, one)
    return total_ref[...]


def columns(i, width):
    if isinstance(i, int):
        return pl.ds(i * width, width)
    return pl.ds(pl.multiple_of(i * width, width), width)


def pair_rows(ref, i):
    block = ref[:, columns(i, PAIR)]
    return jnp.concatenate([block[:, :WIDTH], block[:, WIDTH:]], axis=0)


def stacked_rows(ref, head, group):
    first = head * group
    return jnp.concatenate(
        [ref[:, (first + g) * WIDTH : (first + g + 1) * WIDTH] for g in range(group)], axis=0
    )


def twice(row):
    return jnp.concatenate([row, row], axis=1)


def tile_bias(table, first, tiles):
    return [twice(table[first + t : first + t + 1, :]) for t in range(tiles)]


def add_tiles(scores, biases):
    parts = [
        scores[t * TILE : (t + 1) * TILE, :] * SCALE2 + bias for t, bias in enumerate(biases)
    ]
    return parts[0] if len(parts) == 1 else jnp.concatenate(parts, axis=0)


def tail_bias(row_list):
    rows = row_list.shape[1]
    cut = jnp.sum((row_list == 0).astype(jnp.int32), axis=1, keepdims=True)
    key_at = lax.broadcasted_iota(jnp.int32, (rows, rows), 0)
    row_at = lax.broadcasted_iota(jnp.int32, (rows, rows), 1)
    allowed = ((key_at < cut) == (row_at < cut)) & (key_at <= row_at)
    return twice(jnp.where(allowed, 0.0, NEG).astype(F32))


def near_kernel(
    ctx, q_in, g_in, tk_in, tv_in, ok_in, ov_in, rl_in, ro_in, rt_in, rs_in, rc_ref,
    q_ref, g_ref, k_ref, p_ref, d_ref, stats_ref, table_ref,
    v_ref, rl_ref, ro_ref, rt_ref, rs_ref, sems,
):
    tail = tk_in.shape[0]
    own = ok_in.shape[0] // TILE
    heads = tk_in.shape[1] // WIDTH
    pairs = q_ref.shape[1] // PAIR
    reads = ro_ref.shape[1]
    slots = table_ref.shape[0]
    moves = [
        (rl_in, rl_ref), (ro_in, ro_ref), (rt_in, rt_ref), (rs_in, rs_ref),
        (tk_in, k_ref.at[:tail]), (ok_in, k_ref.at[tail:]), (q_in, q_ref),
        (tv_in, v_ref.at[:tail]), (ov_in, v_ref.at[tail:]), (g_in, g_ref),
    ]
    copies = [pltpu.make_async_copy(a, b, sems.at[i]) for i, (a, b) in enumerate(moves)]
    for copy in copies:
        copy.start()
    for copy in copies[:4]:
        copy.wait()
    row_list = rl_ref[...]
    owner = ro_ref[...] - lax.axis_index("ctx")
    owner = jnp.where(owner < 0, owner + ctx, owner)
    wanted = owner * own + rt_ref[...]
    live = lax.broadcasted_iota(jnp.int32, (1, reads), 1) < rc_ref[0]
    wanted = jnp.where(live, wanted, -1)
    hit = lax.broadcasted_iota(jnp.int32, (slots, reads), 0) == wanted
    first = rs_ref[...] == 0
    count0 = jnp.sum(jnp.where(hit & first, 1.0, 0.0), axis=1, keepdims=True)
    count1 = jnp.sum(jnp.where(hit & jnp.logical_not(first), 1.0, 0.0), axis=1, keepdims=True)
    count = jnp.where(row_list == 0, count0, count1)
    table = jnp.where(count > 0.5, jnp.log2(jnp.maximum(count, 1.0)), NEG)
    table_ref[...] = table
    biases = [tail_bias(row_list)] + tile_bias(table, 0, own)
    for copy in copies[4:]:
        copy.wait()
    for head in range(heads):
        cols = slice(head * WIDTH, (head + 1) * WIDTH)
        for pair in range(head * pairs // heads, (head + 1) * pairs // heads):
            s = add_tiles(dot_nt(k_ref[:, cols], pair_rows(q_ref, pair)), biases)
            top = jnp.max(s, axis=0, keepdims=True)
            p = jnp.exp2(s - top)
            d = dot_nt(v_ref[:, cols], pair_rows(g_ref, pair))
            at = slice(pair * PAIR, (pair + 1) * PAIR)
            here = columns(pair - head * pairs // heads, PAIR)
            p_ref[head, :, here] = p
            d_ref[head, :, here] = d
            stats_ref[0:1, at] = top
            stats_ref[1:2, at] = jnp.sum(p, axis=0, keepdims=True)
            stats_ref[2:3, at] = jnp.sum(p * d, axis=0, keepdims=True)


def far_key_kernel(
    unroll, q_ref, g_ref, k_ref, stats_ref, table_ref, back_ref, p_ref, fin_ref, *total_ref
):
    far_tiles = k_ref.shape[0] // TILE
    heads = k_ref.shape[1] // WIDTH
    per_head = q_ref.shape[1] // PAIR // heads
    shifts, own_keys, _ = back_ref.shape
    biases = tile_bias(table_ref[...], own_keys // TILE, far_tiles)
    for head in range(heads):
        cols = slice(head * WIDTH, (head + 1) * WIDTH)

        def step(i):
            pair = head * per_head + i
            at = columns(pair, PAIR)
            here = columns(i, PAIR)
            s = add_tiles(dot_nt(k_ref[:, cols], pair_rows(q_ref, pair)), biases)
            near_top = stats_ref[0:1, at]
            top = jnp.maximum(near_top, jnp.max(s, axis=0, keepdims=True))
            p = jnp.exp2(s - top)
            fade = jnp.exp2(near_top - top)
            inverse = 1.0 / (stats_ref[1:2, at] * fade + jnp.sum(p, axis=0, keepdims=True))
            fade = fade * inverse
            fin_ref[0:1, at] = fade
            fin_ref[1:2, at] = stats_ref[2:3, at] * fade
            p = (p * inverse).astype(BF16)
            p_ref[head, :, here] = p
            return dot_nn(p, pair_rows(g_ref, pair))

        dv = added(per_head, unroll, step, total_ref).astype(BF16)
        for shift in range(shifts):
            back_ref[shift, :, cols] = dv[shift * own_keys : (shift + 1) * own_keys]


def far_value_kernel(
    unroll, q_ref, g_ref, v_ref, p_ref, fin_ref, back_ref, ds_ref, delta_ref, *total_ref
):
    heads = v_ref.shape[1] // WIDTH
    per_head = q_ref.shape[1] // PAIR // heads
    shifts, own_keys, _ = back_ref.shape
    for head in range(heads):
        cols = slice(head * WIDTH, (head + 1) * WIDTH)

        def step(i):
            pair = head * per_head + i
            at = columns(pair, PAIR)
            here = columns(i, PAIR)
            d = dot_nt(v_ref[:, cols], pair_rows(g_ref, pair))
            p = p_ref[head, :, here].astype(F32)
            delta = fin_ref[1:2, at] + jnp.sum(p * d, axis=0, keepdims=True)
            delta_ref[0:1, at] = delta
            ds = (p * (d - delta)).astype(BF16)
            ds_ref[head, :, here] = ds
            return dot_nn(ds, pair_rows(q_ref, pair))

        dk = (added(per_head, unroll, step, total_ref) * SCALE).astype(BF16)
        for shift in range(shifts):
            back_ref[shift, :, cols] = dk[shift * own_keys : (shift + 1) * own_keys]


def last_kernel(
    unroll, q_ref, g_ref, k_ref, p_ref, d_ref, fin_ref, delta_ref, fk_ref, fds_ref,
    dq_ref, dtk_ref, dtv_ref, dok_ref, dov_ref, low_ref, ds_ref,
):
    tail = dtk_ref.shape[0]
    heads = k_ref.shape[1] // WIDTH
    per_head = q_ref.shape[1] // PAIR // heads
    for head in range(heads):
        cols = slice(head * WIDTH, (head + 1) * WIDTH)

        def step(i):
            pair = head * per_head + i
            at = columns(pair, PAIR)
            here = columns(i, PAIR)
            p = p_ref[head, :, here] * fin_ref[0:1, at]
            ds = (p * (d_ref[head, :, here] - delta_ref[0:1, at])).astype(BF16)
            low_ref[head, :, here] = p.astype(BF16)
            ds_ref[head, :, here] = ds
            dq = dot_tn(k_ref[:, cols], ds) + dot_tn(fk_ref[:, cols], fds_ref[head, :, here])
            dq = dq * SCALE
            dq = jnp.concatenate([dq[:, :WIDTH].T, dq[:, WIDTH:].T], axis=1)
            dq_ref[:, at] = dq.astype(BF16)

        repeat(per_head, unroll, step)
        dk = dot_nn(ds_ref[head], stacked_rows(q_ref, head, 2 * per_head)) * SCALE
        dv = dot_nn(low_ref[head], stacked_rows(g_ref, head, 2 * per_head))
        dtk_ref[:, cols] = dk[:tail].astype(BF16)
        dtv_ref[:, cols] = dv[:tail].astype(BF16)
        dok_ref[:, cols] = dk[tail:]
        dov_ref[:, cols] = dv[tail:]


def call(kernel, spaces, outs, scratch, flops, mib, *args):
    vmem = pl.BlockSpec(memory_space=pltpu.VMEM)
    moved = sum(a.size * a.dtype.itemsize for a in args) + sum(
        math.prod(o.shape) * o.dtype.itemsize for o in outs
    )
    return pl.pallas_call(
        kernel,
        out_shape=outs,
        in_specs=[pl.BlockSpec(memory_space=space) for space in spaces],
        out_specs=[vmem] * len(outs),
        scratch_shapes=scratch,
        compiler_params=pltpu.CompilerParams(vmem_limit_bytes=mib * 2**20),
        cost_estimate=pl.CostEstimate(flops=flops, bytes_accessed=moved, transcendentals=0),
    )(*args)


def body(q, g, tk, tv, ck, cv, row_list, read_owner, read_tile, read_list, read_count):
    ctx = lax.axis_size("ctx")
    rows, q_width = q.shape
    kv_width = tk.shape[1]
    heads = kv_width // WIDTH
    group_rows = rows * (q_width // kv_width)
    own_keys = ck.shape[0]
    own = own_keys // TILE
    far_keys = (ctx - 1) * own_keys
    near_keys = rows + own_keys
    slots = -(-ctx * own // 8) * 8
    unroll = ctx <= 2
    row_list = row_list.reshape(1, rows)

    def shifted(x, shift):
        return lax.ppermute(x, "ctx", [(o, (o - shift) % ctx) for o in range(ctx)])

    far_k = [shifted(ck, s) for s in range(1, ctx)]
    far_v = [shifted(cv, s) for s in range(1, ctx)]
    shape = jax.ShapeDtypeStruct
    product = 2 * q_width * rows * WIDTH
    small = read_owner.shape
    here = [
        pltpu.with_memory_space_constraint(a, pltpu.HBM)
        for a in (q, g, tk, tv, ck, cv, row_list, read_owner, read_tile, read_list)
    ]
    q, g, near_k, near_p, near_d, stats, table = call(
        functools.partial(near_kernel, ctx),
        [pltpu.HBM] * len(here) + [pltpu.SMEM],
        [
            shape(q.shape, BF16),
            shape(g.shape, BF16),
            shape((near_keys, kv_width), BF16),
            shape((heads, near_keys, group_rows), F32),
            shape((heads, near_keys, group_rows), F32),
            shape((8, heads * group_rows), F32),
            shape((slots, rows), F32),
        ],
        [
            pltpu.VMEM((near_keys, kv_width), BF16),
            pltpu.VMEM(row_list.shape, jnp.int32),
            pltpu.VMEM(small, jnp.int32),
            pltpu.VMEM(small, jnp.int32),
            pltpu.VMEM(small, jnp.int32),
            pltpu.SemaphoreType.DMA((10,)),
        ],
        2 * product * near_keys // WIDTH,
        32,
        *here, read_count,
    )
    mib = 32 if unroll else 60
    total = [] if unroll else [pltpu.VMEM((far_keys, WIDTH), F32)]
    far_k = far_k[0] if ctx == 2 else jnp.concatenate(far_k, axis=0)
    back_v, far_p, fin = call(
        functools.partial(far_key_kernel, unroll),
        [pltpu.VMEM] * 5,
        [
            shape((ctx - 1, own_keys, kv_width), BF16),
            shape((heads, far_keys, group_rows), BF16),
            shape((8, heads * group_rows), F32),
        ],
        total,
        2 * product * far_keys // WIDTH,
        mib,
        q, g, far_k, stats, table,
    )
    returned_v = [shifted(back_v[s - 1], -s) for s in range(1, ctx)]
    far_v = far_v[0] if ctx == 2 else jnp.concatenate(far_v, axis=0)
    back_k, far_ds, delta = call(
        functools.partial(far_value_kernel, unroll),
        [pltpu.VMEM] * 5,
        [
            shape((ctx - 1, own_keys, kv_width), BF16),
            shape((heads, far_keys, group_rows), BF16),
            shape((8, heads * group_rows), F32),
        ],
        total,
        2 * product * far_keys // WIDTH,
        mib,
        q, g, far_v, far_p, fin,
    )
    returned_k = [shifted(back_k[s - 1], -s) for s in range(1, ctx)]
    dq, dtk, dtv, dok, dov = call(
        functools.partial(last_kernel, unroll),
        [pltpu.VMEM] * 9,
        [
            shape(q.shape, BF16),
            shape(tk.shape, BF16),
            shape(tv.shape, BF16),
            shape(ck.shape, F32),
            shape(cv.shape, F32),
        ],
        [pltpu.VMEM((heads, near_keys, group_rows), BF16)] * 2,
        product * (3 * near_keys + far_keys) // WIDTH,
        mib,
        q, g, near_k, near_p, near_d, fin, delta, far_k, far_ds,
    )
    for key_block, value_block in zip(returned_k, returned_v):
        dok = dok + key_block.astype(F32)
        dov = dov + value_block.astype(F32)
    return dq, dtk, dtv, dok, dov


def solution(mesh):
    wide = P(("dp", "ctx"), "tp")
    lone = P(("dp", "ctx"))
    flat = P(("dp", "ctx"), None)
    return jax.shard_map(
        body,
        mesh=mesh,
        in_specs=(wide,) * 6 + (lone, flat, flat, flat, lone),
        out_specs=(wide,) * 5,
        check_vma=False,
    )
```

```python
import functools
import math

import jax
import jax.numpy as jnp
from jax import lax
from jax.experimental import pallas as pl
from jax.experimental.pallas import tpu as pltpu
from jax.sharding import PartitionSpec as P

WIDTH = 128
TILE = 128
PAIR = 2 * WIDTH
NEG = -1e30
SCALE = 1.0 / math.sqrt(WIDTH)
SCALE2 = SCALE * math.log2(math.e)
F32 = jnp.float32
BF16 = jnp.bfloat16


def dot_nt(a, b):
    return lax.dot_general(a, b, (((1,), (1,)), ((), ())), preferred_element_type=F32)


def dot_nn(a, b):
    return lax.dot_general(a, b, (((1,), (0,)), ((), ())), preferred_element_type=F32)


def dot_tn(a, b):
    return lax.dot_general(a, b, (((0,), (0,)), ((), ())), preferred_element_type=F32)


def repeat(steps, unroll, step):
    if unroll:
        for i in range(steps):
            step(i)
    else:

        def one(i, carry):
            step(i)
            return carry

        lax.fori_loop(0, steps, one, 0)


def added(steps, unroll, step, total_ref):
    if unroll:
        return functools.reduce(jnp.add, [step(i) for i in range(steps)])
    (total_ref,) = total_ref
    total_ref[...] = jnp.zeros_like(total_ref)

    def one(i):
        total_ref[...] += step(i)

    repeat(steps, unroll, one)
    return total_ref[...]


def columns(i, width):
    if isinstance(i, int):
        return pl.ds(i * width, width)
    return pl.ds(pl.multiple_of(i * width, width), width)


def pair_rows(ref, i):
    block = ref[:, columns(i, PAIR)]
    return jnp.concatenate([block[:, :WIDTH], block[:, WIDTH:]], axis=0)


def stacked_rows(ref, head, group):
    first = head * group
    return jnp.concatenate(
        [ref[:, (first + g) * WIDTH : (first + g + 1) * WIDTH] for g in range(group)], axis=0
    )


def twice(row):
    return jnp.concatenate([row, row], axis=1)


def tile_bias(table, first, tiles):
    return [twice(table[first + t : first + t + 1, :]) for t in range(tiles)]


def add_tiles(scores, biases):
    parts = [
        scores[t * TILE : (t + 1) * TILE, :] * SCALE2 + bias for t, bias in enumerate(biases)
    ]
    return parts[0] if len(parts) == 1 else jnp.concatenate(parts, axis=0)


def tail_bias(row_list):
    rows = row_list.shape[1]
    cut = jnp.sum((row_list == 0).astype(jnp.int32), axis=1, keepdims=True)
    key_at = lax.broadcasted_iota(jnp.int32, (rows, rows), 0)
    row_at = lax.broadcasted_iota(jnp.int32, (rows, rows), 1)
    allowed = ((key_at < cut) == (row_at < cut)) & (key_at <= row_at)
    return twice(jnp.where(allowed, 0.0, NEG).astype(F32))


def near_kernel(
    ctx, q_in, g_in, tk_in, tv_in, ok_in, ov_in, rl_in, ro_in, rt_in, rs_in, rc_ref,
    q_ref, g_ref, k_ref, p_ref, d_ref, stats_ref, table_ref,
    v_ref, rl_ref, ro_ref, rt_ref, rs_ref, sems,
):
    tail = tk_in.shape[0]
    own = ok_in.shape[0] // TILE
    heads = tk_in.shape[1] // WIDTH
    pairs = q_ref.shape[1] // PAIR
    reads = ro_ref.shape[1]
    slots = table_ref.shape[0]
    moves = [
        (rl_in, rl_ref), (ro_in, ro_ref), (rt_in, rt_ref), (rs_in, rs_ref),
        (tk_in, k_ref.at[:tail]), (ok_in, k_ref.at[tail:]), (q_in, q_ref),
        (tv_in, v_ref.at[:tail]), (ov_in, v_ref.at[tail:]), (g_in, g_ref),
    ]
    copies = [pltpu.make_async_copy(a, b, sems.at[i]) for i, (a, b) in enumerate(moves)]
    for copy in copies:
        copy.start()
    for copy in copies[:4]:
        copy.wait()
    row_list = rl_ref[...]
    owner = ro_ref[...] - lax.axis_index("ctx")
    owner = jnp.where(owner < 0, owner + ctx, owner)
    wanted = owner * own + rt_ref[...]
    live = lax.broadcasted_iota(jnp.int32, (1, reads), 1) < rc_ref[0]
    wanted = jnp.where(live, wanted, -1)
    hit = lax.broadcasted_iota(jnp.int32, (slots, reads), 0) == wanted
    first = rs_ref[...] == 0
    count0 = jnp.sum(jnp.where(hit & first, 1.0, 0.0), axis=1, keepdims=True)
    count1 = jnp.sum(jnp.where(hit & jnp.logical_not(first), 1.0, 0.0), axis=1, keepdims=True)
    count = jnp.where(row_list == 0, count0, count1)
    table = jnp.where(count > 0.5, jnp.log2(jnp.maximum(count, 1.0)), NEG)
    table_ref[...] = table
    biases = [tail_bias(row_list)] + tile_bias(table, 0, own)
    for copy in copies[4:]:
        copy.wait()
    for head in range(heads):
        cols = slice(head * WIDTH, (head + 1) * WIDTH)
        for pair in range(head * pairs // heads, (head + 1) * pairs // heads):
            s = add_tiles(dot_nt(k_ref[:, cols], pair_rows(q_ref, pair)), biases)
            top = jnp.max(s, axis=0, keepdims=True)
            p = jnp.exp2(s - top)
            d = dot_nt(v_ref[:, cols], pair_rows(g_ref, pair))
            at = slice(pair * PAIR, (pair + 1) * PAIR)
            here = columns(pair - head * pairs // heads, PAIR)
            p_ref[head, :, here] = p
            d_ref[head, :, here] = d
            stats_ref[0:1, at] = top
            stats_ref[1:2, at] = jnp.sum(p, axis=0, keepdims=True)
            stats_ref[2:3, at] = jnp.sum(p * d, axis=0, keepdims=True)


def far_key_kernel(
    unroll, q_ref, g_ref, k_ref, stats_ref, table_ref, back_ref, p_ref, fin_ref, *total_ref
):
    far_tiles = k_ref.shape[0] // TILE
    heads = k_ref.shape[1] // WIDTH
    per_head = q_ref.shape[1] // PAIR // heads
    shifts, own_keys, _ = back_ref.shape
    biases = tile_bias(table_ref[...], own_keys // TILE, far_tiles)
    for head in range(heads):
        cols = slice(head * WIDTH, (head + 1) * WIDTH)

        def step(i):
            pair = head * per_head + i
            at = columns(pair, PAIR)
            here = columns(i, PAIR)
            s = add_tiles(dot_nt(k_ref[:, cols], pair_rows(q_ref, pair)), biases)
            near_top = stats_ref[0:1, at]
            top = jnp.maximum(near_top, jnp.max(s, axis=0, keepdims=True))
            p = jnp.exp2(s - top)
            fade = jnp.exp2(near_top - top)
            inverse = 1.0 / (stats_ref[1:2, at] * fade + jnp.sum(p, axis=0, keepdims=True))
            fade = fade * inverse
            fin_ref[0:1, at] = fade
            fin_ref[1:2, at] = stats_ref[2:3, at] * fade
            p = (p * inverse).astype(BF16)
            p_ref[head, :, here] = p
            return dot_nn(p, pair_rows(g_ref, pair))

        dv = added(per_head, unroll, step, total_ref).astype(BF16)
        for shift in range(shifts):
            back_ref[shift, :, cols] = dv[shift * own_keys : (shift + 1) * own_keys]


def far_value_kernel(
    unroll, q_ref, g_ref, v_ref, p_ref, fin_ref, back_ref, ds_ref, delta_ref, *total_ref
):
    heads = v_ref.shape[1] // WIDTH
    per_head = q_ref.shape[1] // PAIR // heads
    shifts, own_keys, _ = back_ref.shape
    for head in range(heads):
        cols = slice(head * WIDTH, (head + 1) * WIDTH)

        def step(i):
            pair = head * per_head + i
            at = columns(pair, PAIR)
            here = columns(i, PAIR)
            d = dot_nt(v_ref[:, cols], pair_rows(g_ref, pair))
            p = p_ref[head, :, here].astype(F32)
            delta = fin_ref[1:2, at] + jnp.sum(p * d, axis=0, keepdims=True)
            delta_ref[0:1, at] = delta
            ds = (p * (d - delta)).astype(BF16)
            ds_ref[head, :, here] = ds
            return dot_nn(ds, pair_rows(q_ref, pair))

        dk = (added(per_head, unroll, step, total_ref) * SCALE).astype(BF16)
        for shift in range(shifts):
            back_ref[shift, :, cols] = dk[shift * own_keys : (shift + 1) * own_keys]


def sum_kernel(after_ref, own_ref, *refs):
    total = own_ref[...]
    for ref in refs[:-1]:
        total = total + ref[...].astype(F32)
    refs[-1][...] = total


def last_kernel(
    unroll, q_ref, g_ref, k_ref, p_ref, d_ref, fin_ref, delta_ref, fk_ref, fds_ref,
    dq_ref, dtk_ref, dtv_ref, dok_ref, dov_ref, low_ref, ds_ref,
):
    tail = dtk_ref.shape[0]
    heads = k_ref.shape[1] // WIDTH
    per_head = q_ref.shape[1] // PAIR // heads
    for head in range(heads):
        cols = slice(head * WIDTH, (head + 1) * WIDTH)

        def step(i):
            pair = head * per_head + i
            at = columns(pair, PAIR)
            here = columns(i, PAIR)
            p = p_ref[head, :, here] * fin_ref[0:1, at]
            ds = (p * (d_ref[head, :, here] - delta_ref[0:1, at])).astype(BF16)
            low_ref[head, :, here] = p.astype(BF16)
            ds_ref[head, :, here] = ds
            dq = dot_tn(k_ref[:, cols], ds) + dot_tn(fk_ref[:, cols], fds_ref[head, :, here])
            dq = dq * SCALE
            dq = jnp.concatenate([dq[:, :WIDTH].T, dq[:, WIDTH:].T], axis=1)
            dq_ref[:, at] = dq.astype(BF16)

        repeat(per_head, unroll, step)
        dk = dot_nn(ds_ref[head], stacked_rows(q_ref, head, 2 * per_head)) * SCALE
        dv = dot_nn(low_ref[head], stacked_rows(g_ref, head, 2 * per_head))
        dtk_ref[:, cols] = dk[:tail].astype(BF16)
        dtv_ref[:, cols] = dv[:tail].astype(BF16)
        dok_ref[:, cols] = dk[tail:]
        dov_ref[:, cols] = dv[tail:]


def call(kernel, spaces, outs, scratch, flops, mib, *args):
    vmem = pl.BlockSpec(memory_space=pltpu.VMEM)
    moved = sum(a.size * a.dtype.itemsize for a in args) + sum(
        math.prod(o.shape) * o.dtype.itemsize for o in outs
    )
    return pl.pallas_call(
        kernel,
        out_shape=outs,
        in_specs=[pl.BlockSpec(memory_space=space) for space in spaces],
        out_specs=[vmem] * len(outs),
        scratch_shapes=scratch,
        compiler_params=pltpu.CompilerParams(vmem_limit_bytes=mib * 2**20),
        cost_estimate=pl.CostEstimate(flops=flops, bytes_accessed=moved, transcendentals=0),
    )(*args)


def body(q, g, tk, tv, ck, cv, row_list, read_owner, read_tile, read_list, read_count):
    ctx = lax.axis_size("ctx")
    rows, q_width = q.shape
    kv_width = tk.shape[1]
    heads = kv_width // WIDTH
    group_rows = rows * (q_width // kv_width)
    own_keys = ck.shape[0]
    own = own_keys // TILE
    far_keys = (ctx - 1) * own_keys
    near_keys = rows + own_keys
    slots = -(-ctx * own // 8) * 8
    unroll = ctx <= 2
    row_list = row_list.reshape(1, rows)

    def shifted(x, shift):
        return lax.ppermute(x, "ctx", [(o, (o - shift) % ctx) for o in range(ctx)])

    far_k = [shifted(ck, s) for s in range(1, ctx)]
    far_v = [shifted(cv, s) for s in range(1, ctx)]
    shape = jax.ShapeDtypeStruct
    product = 2 * q_width * rows * WIDTH
    small = read_owner.shape
    here = [
        pltpu.with_memory_space_constraint(a, pltpu.HBM)
        for a in (q, g, tk, tv, ck, cv, row_list, read_owner, read_tile, read_list)
    ]
    q, g, near_k, near_p, near_d, stats, table = call(
        functools.partial(near_kernel, ctx),
        [pltpu.HBM] * len(here) + [pltpu.SMEM],
        [
            shape(q.shape, BF16),
            shape(g.shape, BF16),
            shape((near_keys, kv_width), BF16),
            shape((heads, near_keys, group_rows), F32),
            shape((heads, near_keys, group_rows), F32),
            shape((8, heads * group_rows), F32),
            shape((slots, rows), F32),
        ],
        [
            pltpu.VMEM((near_keys, kv_width), BF16),
            pltpu.VMEM(row_list.shape, jnp.int32),
            pltpu.VMEM(small, jnp.int32),
            pltpu.VMEM(small, jnp.int32),
            pltpu.VMEM(small, jnp.int32),
            pltpu.SemaphoreType.DMA((10,)),
        ],
        2 * product * near_keys // WIDTH,
        32,
        *here, read_count,
    )
    mib = 32 if unroll else 60
    total = [] if unroll else [pltpu.VMEM((far_keys, WIDTH), F32)]
    far_k = far_k[0] if ctx == 2 else jnp.concatenate(far_k, axis=0)
    back_v, far_p, fin = call(
        functools.partial(far_key_kernel, unroll),
        [pltpu.VMEM] * 5,
        [
            shape((ctx - 1, own_keys, kv_width), BF16),
            shape((heads, far_keys, group_rows), BF16),
            shape((8, heads * group_rows), F32),
        ],
        total,
        2 * product * far_keys // WIDTH,
        mib,
        q, g, far_k, stats, table,
    )
    returned_v = [shifted(back_v[s - 1], -s) for s in range(1, ctx)]
    far_v = far_v[0] if ctx == 2 else jnp.concatenate(far_v, axis=0)
    back_k, far_ds, delta = call(
        functools.partial(far_value_kernel, unroll),
        [pltpu.VMEM] * 5,
        [
            shape((ctx - 1, own_keys, kv_width), BF16),
            shape((heads, far_keys, group_rows), BF16),
            shape((8, heads * group_rows), F32),
        ],
        total,
        2 * product * far_keys // WIDTH,
        mib,
        q, g, far_v, far_p, fin,
    )
    returned_k = [shifted(back_k[s - 1], -s) for s in range(1, ctx)]
    dq, dtk, dtv, dok, dov = call(
        functools.partial(last_kernel, unroll),
        [pltpu.VMEM] * 9,
        [
            shape(q.shape, BF16),
            shape(tk.shape, BF16),
            shape(tv.shape, BF16),
            shape(ck.shape, F32),
            shape(cv.shape, F32),
        ],
        [pltpu.VMEM((heads, near_keys, group_rows), BF16)] * 2,
        product * (3 * near_keys + far_keys) // WIDTH,
        mib,
        q, g, near_k, near_p, near_d, fin, delta, far_k, far_ds,
    )

    def summed(after, own_sum, returned):
        return call(
            sum_kernel,
            [pltpu.HBM] + [pltpu.VMEM] * (1 + len(returned)),
            [shape(own_sum.shape, F32)],
            [],
            0,
            mib,
            pltpu.with_memory_space_constraint(after, pltpu.HBM), own_sum, *returned,
        )[0]

    dov = summed(dq, dov, returned_v)
    dok = summed(dov, dok, returned_k)
    return dq, dtk, dtv, dok, dov


def solution(mesh):
    wide = P(("dp", "ctx"), "tp")
    lone = P(("dp", "ctx"))
    flat = P(("dp", "ctx"), None)
    return jax.shard_map(
        body,
        mesh=mesh,
        in_specs=(wide,) * 6 + (lone, flat, flat, flat, lone),
        out_specs=(wide,) * 5,
        check_vma=False,
    )
```

```python
import functools
import math

import jax
import jax.numpy as jnp
from jax import lax
from jax.experimental import pallas as pl
from jax.experimental.pallas import tpu as pltpu
from jax.sharding import PartitionSpec as P

WIDTH = 128
TILE = 128
PAIR = 2 * WIDTH
NEAR_OUTS = 7
NEG = -1e30
SCALE = 1.0 / math.sqrt(WIDTH)
SCALE2 = SCALE * math.log2(math.e)
F32 = jnp.float32
BF16 = jnp.bfloat16


def dot_nt(a, b):
    return lax.dot_general(a, b, (((1,), (1,)), ((), ())), preferred_element_type=F32)


def dot_nn(a, b):
    return lax.dot_general(a, b, (((1,), (0,)), ((), ())), preferred_element_type=F32)


def dot_tn(a, b):
    return lax.dot_general(a, b, (((0,), (0,)), ((), ())), preferred_element_type=F32)


def repeat(steps, unroll, step):
    if unroll:
        for i in range(steps):
            step(i)
    else:

        def one(i, carry):
            step(i)
            return carry

        lax.fori_loop(0, steps, one, 0)


def added(steps, unroll, step, total_ref):
    if unroll:
        return functools.reduce(jnp.add, [step(i) for i in range(steps)])
    (total_ref,) = total_ref
    total_ref[...] = jnp.zeros_like(total_ref)

    def one(i):
        total_ref[...] += step(i)

    repeat(steps, unroll, one)
    return total_ref[...]


def columns(i, width):
    if isinstance(i, int):
        return pl.ds(i * width, width)
    return pl.ds(pl.multiple_of(i * width, width), width)


def pair_rows(ref, i):
    block = ref[:, columns(i, PAIR)]
    return jnp.concatenate([block[:, :WIDTH], block[:, WIDTH:]], axis=0)


def stacked_rows(ref, head, group):
    first = head * group
    return jnp.concatenate(
        [ref[:, (first + g) * WIDTH : (first + g + 1) * WIDTH] for g in range(group)], axis=0
    )


def twice(row):
    return jnp.concatenate([row, row], axis=1)


def tile_bias(table, first, tiles):
    return [twice(table[first + t : first + t + 1, :]) for t in range(tiles)]


def add_tiles(scores, biases):
    parts = [
        scores[t * TILE : (t + 1) * TILE, :] * SCALE2 + bias for t, bias in enumerate(biases)
    ]
    return parts[0] if len(parts) == 1 else jnp.concatenate(parts, axis=0)


def tail_bias(row_list):
    rows = row_list.shape[1]
    cut = jnp.sum((row_list == 0).astype(jnp.int32), axis=1, keepdims=True)
    key_at = lax.broadcasted_iota(jnp.int32, (rows, rows), 0)
    row_at = lax.broadcasted_iota(jnp.int32, (rows, rows), 1)
    allowed = ((key_at < cut) == (row_at < cut)) & (key_at <= row_at)
    return twice(jnp.where(allowed, 0.0, NEG).astype(F32))


def near_kernel(ctx, odd, *refs):
    ins, rest = refs[:11], refs[11 if odd else 11 + NEAR_OUTS :]

    @pl.when(lax.rem(lax.axis_index("dp"), 2) == int(odd))
    def work():
        near_work(ctx, *ins, *rest)


def near_work(
    ctx, q_in, g_in, tk_in, tv_in, ok_in, ov_in, rl_in, ro_in, rt_in, rs_in, rc_ref,
    q_ref, g_ref, k_ref, p_ref, d_ref, stats_ref, table_ref,
    v_ref, rl_ref, ro_ref, rt_ref, rs_ref, sems,
):
    tail = tk_in.shape[0]
    own = ok_in.shape[0] // TILE
    heads = tk_in.shape[1] // WIDTH
    pairs = q_ref.shape[1] // PAIR
    reads = ro_ref.shape[1]
    slots = table_ref.shape[0]
    moves = [
        (rl_in, rl_ref), (ro_in, ro_ref), (rt_in, rt_ref), (rs_in, rs_ref),
        (tk_in, k_ref.at[:tail]), (ok_in, k_ref.at[tail:]), (q_in, q_ref),
        (tv_in, v_ref.at[:tail]), (ov_in, v_ref.at[tail:]), (g_in, g_ref),
    ]
    copies = [pltpu.make_async_copy(a, b, sems.at[i]) for i, (a, b) in enumerate(moves)]
    for copy in copies:
        copy.start()
    for copy in copies[:4]:
        copy.wait()
    row_list = rl_ref[...]
    owner = ro_ref[...] - lax.axis_index("ctx")
    owner = jnp.where(owner < 0, owner + ctx, owner)
    wanted = owner * own + rt_ref[...]
    live = lax.broadcasted_iota(jnp.int32, (1, reads), 1) < rc_ref[0]
    wanted = jnp.where(live, wanted, -1)
    hit = lax.broadcasted_iota(jnp.int32, (slots, reads), 0) == wanted
    first = rs_ref[...] == 0
    count0 = jnp.sum(jnp.where(hit & first, 1.0, 0.0), axis=1, keepdims=True)
    count1 = jnp.sum(jnp.where(hit & jnp.logical_not(first), 1.0, 0.0), axis=1, keepdims=True)
    count = jnp.where(row_list == 0, count0, count1)
    table = jnp.where(count > 0.5, jnp.log2(jnp.maximum(count, 1.0)), NEG)
    table_ref[...] = table
    biases = [tail_bias(row_list)] + tile_bias(table, 0, own)
    for copy in copies[4:]:
        copy.wait()
    for head in range(heads):
        cols = slice(head * WIDTH, (head + 1) * WIDTH)
        for pair in range(head * pairs // heads, (head + 1) * pairs // heads):
            s = add_tiles(dot_nt(k_ref[:, cols], pair_rows(q_ref, pair)), biases)
            top = jnp.max(s, axis=0, keepdims=True)
            p = jnp.exp2(s - top)
            d = dot_nt(v_ref[:, cols], pair_rows(g_ref, pair))
            at = slice(pair * PAIR, (pair + 1) * PAIR)
            here = columns(pair - head * pairs // heads, PAIR)
            p_ref[head, :, here] = p
            d_ref[head, :, here] = d
            stats_ref[0:1, at] = top
            stats_ref[1:2, at] = jnp.sum(p, axis=0, keepdims=True)
            stats_ref[2:3, at] = jnp.sum(p * d, axis=0, keepdims=True)


def far_key_kernel(
    unroll, q_ref, g_ref, k_ref, stats_ref, table_ref, back_ref, p_ref, fin_ref, *total_ref
):
    far_tiles = k_ref.shape[0] // TILE
    heads = k_ref.shape[1] // WIDTH
    per_head = q_ref.shape[1] // PAIR // heads
    shifts, own_keys, _ = back_ref.shape
    biases = tile_bias(table_ref[...], own_keys // TILE, far_tiles)
    for head in range(heads):
        cols = slice(head * WIDTH, (head + 1) * WIDTH)

        def step(i):
            pair = head * per_head + i
            at = columns(pair, PAIR)
            here = columns(i, PAIR)
            s = add_tiles(dot_nt(k_ref[:, cols], pair_rows(q_ref, pair)), biases)
            near_top = stats_ref[0:1, at]
            top = jnp.maximum(near_top, jnp.max(s, axis=0, keepdims=True))
            p = jnp.exp2(s - top)
            fade = jnp.exp2(near_top - top)
            inverse = 1.0 / (stats_ref[1:2, at] * fade + jnp.sum(p, axis=0, keepdims=True))
            fade = fade * inverse
            fin_ref[0:1, at] = fade
            fin_ref[1:2, at] = stats_ref[2:3, at] * fade
            p = (p * inverse).astype(BF16)
            p_ref[head, :, here] = p
            return dot_nn(p, pair_rows(g_ref, pair))

        dv = added(per_head, unroll, step, total_ref).astype(BF16)
        for shift in range(shifts):
            back_ref[shift, :, cols] = dv[shift * own_keys : (shift + 1) * own_keys]


def far_value_kernel(
    unroll, q_ref, g_ref, v_ref, p_ref, fin_ref, back_ref, ds_ref, delta_ref, *total_ref
):
    heads = v_ref.shape[1] // WIDTH
    per_head = q_ref.shape[1] // PAIR // heads
    shifts, own_keys, _ = back_ref.shape
    for head in range(heads):
        cols = slice(head * WIDTH, (head + 1) * WIDTH)

        def step(i):
            pair = head * per_head + i
            at = columns(pair, PAIR)
            here = columns(i, PAIR)
            d = dot_nt(v_ref[:, cols], pair_rows(g_ref, pair))
            p = p_ref[head, :, here].astype(F32)
            delta = fin_ref[1:2, at] + jnp.sum(p * d, axis=0, keepdims=True)
            delta_ref[0:1, at] = delta
            ds = (p * (d - delta)).astype(BF16)
            ds_ref[head, :, here] = ds
            return dot_nn(ds, pair_rows(q_ref, pair))

        dk = (added(per_head, unroll, step, total_ref) * SCALE).astype(BF16)
        for shift in range(shifts):
            back_ref[shift, :, cols] = dk[shift * own_keys : (shift + 1) * own_keys]


def sum_kernel(after_ref, own_ref, *refs):
    total = own_ref[...]
    for ref in refs[:-1]:
        total = total + ref[...].astype(F32)
    refs[-1][...] = total


def last_kernel(
    unroll, q_ref, g_ref, k_ref, p_ref, d_ref, fin_ref, delta_ref, fk_ref, fds_ref,
    dq_ref, dtk_ref, dtv_ref, dok_ref, dov_ref, low_ref, ds_ref,
):
    tail = dtk_ref.shape[0]
    heads = k_ref.shape[1] // WIDTH
    per_head = q_ref.shape[1] // PAIR // heads
    for head in range(heads):
        cols = slice(head * WIDTH, (head + 1) * WIDTH)

        def step(i):
            pair = head * per_head + i
            at = columns(pair, PAIR)
            here = columns(i, PAIR)
            p = p_ref[head, :, here] * fin_ref[0:1, at]
            ds = (p * (d_ref[head, :, here] - delta_ref[0:1, at])).astype(BF16)
            low_ref[head, :, here] = p.astype(BF16)
            ds_ref[head, :, here] = ds
            dq = dot_tn(k_ref[:, cols], ds) + dot_tn(fk_ref[:, cols], fds_ref[head, :, here])
            dq = dq * SCALE
            dq = jnp.concatenate([dq[:, :WIDTH].T, dq[:, WIDTH:].T], axis=1)
            dq_ref[:, at] = dq.astype(BF16)

        repeat(per_head, unroll, step)
        dk = dot_nn(ds_ref[head], stacked_rows(q_ref, head, 2 * per_head)) * SCALE
        dv = dot_nn(low_ref[head], stacked_rows(g_ref, head, 2 * per_head))
        dtk_ref[:, cols] = dk[:tail].astype(BF16)
        dtv_ref[:, cols] = dv[:tail].astype(BF16)
        dok_ref[:, cols] = dk[tail:]
        dov_ref[:, cols] = dv[tail:]


def call(kernel, spaces, outs, scratch, flops, mib, *args, aliases={}):
    vmem = pl.BlockSpec(memory_space=pltpu.VMEM)
    moved = sum(a.size * a.dtype.itemsize for a in args) + sum(
        math.prod(o.shape) * o.dtype.itemsize for o in outs
    )
    return pl.pallas_call(
        kernel,
        out_shape=outs,
        in_specs=[pl.BlockSpec(memory_space=space) for space in spaces],
        out_specs=[vmem] * len(outs),
        scratch_shapes=scratch,
        input_output_aliases=aliases,
        compiler_params=pltpu.CompilerParams(vmem_limit_bytes=mib * 2**20),
        cost_estimate=pl.CostEstimate(flops=flops, bytes_accessed=moved, transcendentals=0),
    )(*args)


def body(q, g, tk, tv, ck, cv, row_list, read_owner, read_tile, read_list, read_count):
    ctx = lax.axis_size("ctx")
    rows, q_width = q.shape
    kv_width = tk.shape[1]
    heads = kv_width // WIDTH
    group_rows = rows * (q_width // kv_width)
    own_keys = ck.shape[0]
    own = own_keys // TILE
    far_keys = (ctx - 1) * own_keys
    near_keys = rows + own_keys
    slots = -(-ctx * own // 8) * 8
    unroll = ctx <= 2
    row_list = row_list.reshape(1, rows)

    def shifted(x, shift):
        return lax.ppermute(x, "ctx", [(o, (o - shift) % ctx) for o in range(ctx)])

    far_k = [shifted(ck, s) for s in range(1, ctx)]
    shape = jax.ShapeDtypeStruct
    product = 2 * q_width * rows * WIDTH
    small = read_owner.shape
    here = [
        pltpu.with_memory_space_constraint(a, pltpu.HBM)
        for a in (q, g, tk, tv, ck, cv, row_list, read_owner, read_tile, read_list)
    ]
    near_outs = [
        shape(q.shape, BF16),
        shape(g.shape, BF16),
        shape((near_keys, kv_width), BF16),
        shape((heads, near_keys, group_rows), F32),
        shape((heads, near_keys, group_rows), F32),
        shape((8, heads * group_rows), F32),
        shape((slots, rows), F32),
    ]
    near = [
        [pltpu.HBM] * len(here) + [pltpu.SMEM],
        near_outs,
        [
            pltpu.VMEM((near_keys, kv_width), BF16),
            pltpu.VMEM(row_list.shape, jnp.int32),
            pltpu.VMEM(small, jnp.int32),
            pltpu.VMEM(small, jnp.int32),
            pltpu.VMEM(small, jnp.int32),
            pltpu.SemaphoreType.DMA((10,)),
        ],
        2 * product * near_keys // WIDTH,
        32,
        *here, read_count,
    ]
    early = list(call(functools.partial(near_kernel, ctx, True), *near))
    own_v, early[-1] = lax.optimization_barrier((cv, early[-1]))
    far_v = [shifted(own_v, s) for s in range(1, ctx)]
    near[0] = near[0] + [pltpu.VMEM] * NEAR_OUTS
    first = len(here) + 1
    q, g, near_k, near_p, near_d, stats, table = call(
        functools.partial(near_kernel, ctx, False), *near, *early,
        aliases={first + i: i for i in range(NEAR_OUTS)},
    )
    mib = 32 if unroll else 60
    total = [] if unroll else [pltpu.VMEM((far_keys, WIDTH), F32)]
    far_k = far_k[0] if ctx == 2 else jnp.concatenate(far_k, axis=0)
    back_v, far_p, fin = call(
        functools.partial(far_key_kernel, unroll),
        [pltpu.VMEM] * 5,
        [
            shape((ctx - 1, own_keys, kv_width), BF16),
            shape((heads, far_keys, group_rows), BF16),
            shape((8, heads * group_rows), F32),
        ],
        total,
        2 * product * far_keys // WIDTH,
        mib,
        q, g, far_k, stats, table,
    )
    returned_v = [shifted(back_v[s - 1], -s) for s in range(1, ctx)]
    far_v = far_v[0] if ctx == 2 else jnp.concatenate(far_v, axis=0)
    back_k, far_ds, delta = call(
        functools.partial(far_value_kernel, unroll),
        [pltpu.VMEM] * 5,
        [
            shape((ctx - 1, own_keys, kv_width), BF16),
            shape((heads, far_keys, group_rows), BF16),
            shape((8, heads * group_rows), F32),
        ],
        total,
        2 * product * far_keys // WIDTH,
        mib,
        q, g, far_v, far_p, fin,
    )
    returned_k = [shifted(back_k[s - 1], -s) for s in range(1, ctx)]
    dq, dtk, dtv, dok, dov = call(
        functools.partial(last_kernel, unroll),
        [pltpu.VMEM] * 9,
        [
            shape(q.shape, BF16),
            shape(tk.shape, BF16),
            shape(tv.shape, BF16),
            shape(ck.shape, F32),
            shape(cv.shape, F32),
        ],
        [pltpu.VMEM((heads, near_keys, group_rows), BF16)] * 2,
        product * (3 * near_keys + far_keys) // WIDTH,
        mib,
        q, g, near_k, near_p, near_d, fin, delta, far_k, far_ds,
    )

    def summed(after, own_sum, returned):
        return call(
            sum_kernel,
            [pltpu.HBM] + [pltpu.VMEM] * (1 + len(returned)),
            [shape(own_sum.shape, F32)],
            [],
            0,
            mib,
            pltpu.with_memory_space_constraint(after, pltpu.HBM), own_sum, *returned,
        )[0]

    dov = summed(dq, dov, returned_v)
    dok = summed(dov, dok, returned_k)
    return dq, dtk, dtv, dok, dov


def solution(mesh):
    wide = P(("dp", "ctx"), "tp")
    lone = P(("dp", "ctx"))
    flat = P(("dp", "ctx"), None)
    return jax.shard_map(
        body,
        mesh=mesh,
        in_specs=(wide,) * 6 + (lone, flat, flat, flat, lone),
        out_specs=(wide,) * 5,
        check_vma=False,
    )
```

```python
import functools
import math

import jax
import jax.numpy as jnp
from jax import lax
from jax.experimental import pallas as pl
from jax.experimental.pallas import tpu as pltpu
from jax.sharding import PartitionSpec as P

WIDTH = 128
TILE = 128
PAIR = 2 * WIDTH
NEAR_OUTS = 8
NEG = -1e30
SCALE = 1.0 / math.sqrt(WIDTH)
SCALE2 = SCALE * math.log2(math.e)
F32 = jnp.float32
BF16 = jnp.bfloat16


def dot_nt(a, b):
    return lax.dot_general(a, b, (((1,), (1,)), ((), ())), preferred_element_type=F32)


def dot_nn(a, b):
    return lax.dot_general(a, b, (((1,), (0,)), ((), ())), preferred_element_type=F32)


def dot_tn(a, b):
    return lax.dot_general(a, b, (((0,), (0,)), ((), ())), preferred_element_type=F32)


def repeat(steps, unroll, step):
    if unroll:
        for i in range(steps):
            step(i)
    else:

        def one(i, carry):
            step(i)
            return carry

        lax.fori_loop(0, steps, one, 0)


def added(steps, unroll, step, total_ref):
    if unroll:
        return functools.reduce(jnp.add, [step(i) for i in range(steps)])
    (total_ref,) = total_ref
    total_ref[...] = jnp.zeros_like(total_ref)

    def one(i):
        total_ref[...] += step(i)

    repeat(steps, unroll, one)
    return total_ref[...]


def columns(i, width):
    if isinstance(i, int):
        return pl.ds(i * width, width)
    return pl.ds(pl.multiple_of(i * width, width), width)


def pair_rows(ref, i):
    block = ref[:, columns(i, PAIR)]
    return jnp.concatenate([block[:, :WIDTH], block[:, WIDTH:]], axis=0)


def stacked_rows(ref, head, group):
    first = head * group
    return jnp.concatenate(
        [ref[:, (first + g) * WIDTH : (first + g + 1) * WIDTH] for g in range(group)], axis=0
    )


def twice(row):
    return jnp.concatenate([row, row], axis=1)


def tile_bias(table, first, tiles):
    return [twice(table[first + t : first + t + 1, :]) for t in range(tiles)]


def add_tiles(scores, biases):
    parts = [
        scores[t * TILE : (t + 1) * TILE, :] * SCALE2 + bias for t, bias in enumerate(biases)
    ]
    return parts[0] if len(parts) == 1 else jnp.concatenate(parts, axis=0)


def tail_bias(row_list):
    rows = row_list.shape[1]
    cut = jnp.sum((row_list == 0).astype(jnp.int32), axis=1, keepdims=True)
    key_at = lax.broadcasted_iota(jnp.int32, (rows, rows), 0)
    row_at = lax.broadcasted_iota(jnp.int32, (rows, rows), 1)
    allowed = ((key_at < cut) == (row_at < cut)) & (key_at <= row_at)
    return twice(jnp.where(allowed, 0.0, NEG).astype(F32))


def is_odd():
    return lax.rem(lax.axis_index("dp"), 2) == 1


def load_copies(ins, q_ref, g_ref, k_ref, v_ref, small_refs, sems):
    q_in, g_in, tk_in, tv_in, ok_in, ov_in, *small_ins = ins
    tail = tk_in.shape[0]
    moves = list(zip(small_ins, small_refs)) + [
        (tk_in, k_ref.at[:tail]), (ok_in, k_ref.at[tail:]), (q_in, q_ref),
        (tv_in, v_ref.at[:tail]), (ov_in, v_ref.at[tail:]), (g_in, g_ref),
    ]
    copies = [pltpu.make_async_copy(a, b, sems.at[i]) for i, (a, b) in enumerate(moves)]
    for copy in copies:
        copy.start()
    return copies


def near_key_work(
    ctx, own, copies, q_ref, k_ref, p_ref, stats_ref, table_ref, rl_ref, ro_ref, rt_ref, rs_ref, rc_ref
):
    heads = k_ref.shape[1] // WIDTH
    per_head = q_ref.shape[1] // PAIR // heads
    reads = ro_ref.shape[1]
    slots = table_ref.shape[0]
    for copy in copies[:4]:
        copy.wait()
    row_list = rl_ref[...]
    owner = ro_ref[...] - lax.axis_index("ctx")
    owner = jnp.where(owner < 0, owner + ctx, owner)
    wanted = owner * own + rt_ref[...]
    live = lax.broadcasted_iota(jnp.int32, (1, reads), 1) < rc_ref[0]
    wanted = jnp.where(live, wanted, -1)
    hit = lax.broadcasted_iota(jnp.int32, (slots, reads), 0) == wanted
    first = rs_ref[...] == 0
    count0 = jnp.sum(jnp.where(hit & first, 1.0, 0.0), axis=1, keepdims=True)
    count1 = jnp.sum(jnp.where(hit & jnp.logical_not(first), 1.0, 0.0), axis=1, keepdims=True)
    count = jnp.where(row_list == 0, count0, count1)
    table = jnp.where(count > 0.5, jnp.log2(jnp.maximum(count, 1.0)), NEG)
    table_ref[...] = table
    biases = [tail_bias(row_list)] + tile_bias(table, 0, own)
    for copy in copies[4:7]:
        copy.wait()
    for head in range(heads):
        cols = slice(head * WIDTH, (head + 1) * WIDTH)
        for i in range(per_head):
            pair = head * per_head + i
            at = columns(pair, PAIR)
            s = add_tiles(dot_nt(k_ref[:, cols], pair_rows(q_ref, pair)), biases)
            top = jnp.max(s, axis=0, keepdims=True)
            p = jnp.exp2(s - top)
            p_ref[head, :, columns(i, PAIR)] = p
            stats_ref[0:1, at] = top
            stats_ref[1:2, at] = jnp.sum(p, axis=0, keepdims=True)


def near_value_work(g_ref, v_ref, p_ref, d_ref, stats_ref):
    heads = v_ref.shape[1] // WIDTH
    per_head = g_ref.shape[1] // PAIR // heads
    for head in range(heads):
        cols = slice(head * WIDTH, (head + 1) * WIDTH)
        for i in range(per_head):
            pair = head * per_head + i
            here = columns(i, PAIR)
            d = dot_nt(v_ref[:, cols], pair_rows(g_ref, pair))
            d_ref[head, :, here] = d
            cross = jnp.sum(p_ref[head, :, here] * d, axis=0, keepdims=True)
            stats_ref[2:3, columns(pair, PAIR)] = cross


def near_kernel(ctx, early, *refs):
    ins, rc_ref, rest = refs[:10], refs[10], refs[11 if early else 11 + NEAR_OUTS :]
    q_ref, g_ref, k_ref, v_ref, p_ref, d_ref, stats_ref, table_ref = rest[:NEAR_OUTS]
    small_refs, sems = rest[NEAR_OUTS:-1], rest[-1]
    own = ins[4].shape[0] // TILE

    def key_part():
        copies = load_copies(ins, q_ref, g_ref, k_ref, v_ref, small_refs, sems)
        near_key_work(
            ctx, own, copies, q_ref, k_ref, p_ref, stats_ref, table_ref, *small_refs, rc_ref
        )
        for copy in copies[7:]:
            copy.wait()

    if early:
        pl.when(is_odd())(key_part)
    else:
        pl.when(jnp.logical_not(is_odd()))(key_part)
        near_value_work(g_ref, v_ref, p_ref, d_ref, stats_ref)


def far_key_kernel(
    unroll, q_ref, g_ref, k_ref, stats_ref, table_ref, back_ref, p_ref, fin_ref, *total_ref
):
    far_tiles = k_ref.shape[0] // TILE
    heads = k_ref.shape[1] // WIDTH
    per_head = q_ref.shape[1] // PAIR // heads
    shifts, own_keys, _ = back_ref.shape
    biases = tile_bias(table_ref[...], own_keys // TILE, far_tiles)
    for head in range(heads):
        cols = slice(head * WIDTH, (head + 1) * WIDTH)

        def step(i):
            pair = head * per_head + i
            at = columns(pair, PAIR)
            here = columns(i, PAIR)
            s = add_tiles(dot_nt(k_ref[:, cols], pair_rows(q_ref, pair)), biases)
            near_top = stats_ref[0:1, at]
            top = jnp.maximum(near_top, jnp.max(s, axis=0, keepdims=True))
            p = jnp.exp2(s - top)
            fade = jnp.exp2(near_top - top)
            inverse = 1.0 / (stats_ref[1:2, at] * fade + jnp.sum(p, axis=0, keepdims=True))
            fade = fade * inverse
            fin_ref[0:1, at] = fade
            fin_ref[1:2, at] = stats_ref[2:3, at] * fade
            p = (p * inverse).astype(BF16)
            p_ref[head, :, here] = p
            return dot_nn(p, pair_rows(g_ref, pair))

        dv = added(per_head, unroll, step, total_ref).astype(BF16)
        for shift in range(shifts):
            back_ref[shift, :, cols] = dv[shift * own_keys : (shift + 1) * own_keys]


def far_value_kernel(
    unroll, q_ref, g_ref, v_ref, p_ref, fin_ref, near_p_ref,
    back_ref, ds_ref, delta_ref, terms_ref, low_ref, *total_ref
):
    heads = v_ref.shape[1] // WIDTH
    per_head = q_ref.shape[1] // PAIR // heads
    shifts, own_keys, _ = back_ref.shape
    for head in range(heads):
        cols = slice(head * WIDTH, (head + 1) * WIDTH)

        def step(i):
            pair = head * per_head + i
            at = columns(pair, PAIR)
            here = columns(i, PAIR)
            d = dot_nt(v_ref[:, cols], pair_rows(g_ref, pair))
            p = p_ref[head, :, here].astype(F32)
            delta = fin_ref[1:2, at] + jnp.sum(p * d, axis=0, keepdims=True)
            delta_ref[0:1, at] = delta
            ds = (p * (d - delta)).astype(BF16)
            ds_ref[head, :, here] = ds
            return dot_nn(ds, pair_rows(q_ref, pair))

        dk = (added(per_head, unroll, step, total_ref) * SCALE).astype(BF16)
        for shift in range(shifts):
            back_ref[shift, :, cols] = dk[shift * own_keys : (shift + 1) * own_keys]

    @pl.when(is_odd())
    def near_terms():
        for head in range(heads):

            def fill(i):
                here = columns(i, PAIR)
                p = near_p_ref[head, :, here] * fin_ref[0:1, columns(head * per_head + i, PAIR)]
                low_ref[head, :, here] = p.astype(BF16)

            repeat(per_head, unroll, fill)
            rows = stacked_rows(g_ref, head, 2 * per_head)
            terms_ref[:, head * WIDTH : (head + 1) * WIDTH] = dot_nn(low_ref[head], rows)


def sum_kernel(after_ref, own_ref, *refs):
    total = own_ref[...]
    for ref in refs[:-1]:
        total = total + ref[...].astype(F32)
    refs[-1][...] = total


def last_kernel(
    unroll, q_ref, g_ref, k_ref, p_ref, d_ref, fin_ref, delta_ref, fk_ref, fds_ref, terms_ref,
    dq_ref, dtk_ref, dtv_ref, dok_ref, dov_ref, low_ref, ds_ref,
):
    tail = dtk_ref.shape[0]
    heads = k_ref.shape[1] // WIDTH
    per_head = q_ref.shape[1] // PAIR // heads
    for head in range(heads):
        cols = slice(head * WIDTH, (head + 1) * WIDTH)

        def step(i):
            pair = head * per_head + i
            at = columns(pair, PAIR)
            here = columns(i, PAIR)
            p = p_ref[head, :, here] * fin_ref[0:1, at]
            ds = (p * (d_ref[head, :, here] - delta_ref[0:1, at])).astype(BF16)
            low_ref[head, :, here] = p.astype(BF16)
            ds_ref[head, :, here] = ds
            dq = dot_tn(k_ref[:, cols], ds) + dot_tn(fk_ref[:, cols], fds_ref[head, :, here])
            dq = dq * SCALE
            dq = jnp.concatenate([dq[:, :WIDTH].T, dq[:, WIDTH:].T], axis=1)
            dq_ref[:, at] = dq.astype(BF16)

        repeat(per_head, unroll, step)
        dk = dot_nn(ds_ref[head], stacked_rows(q_ref, head, 2 * per_head)) * SCALE
        dtk_ref[:, cols] = dk[:tail].astype(BF16)
        dok_ref[:, cols] = dk[tail:]

        @pl.when(jnp.logical_not(is_odd()))
        def near_terms():
            dv = dot_nn(low_ref[head], stacked_rows(g_ref, head, 2 * per_head))
            dtv_ref[:, cols] = dv[:tail].astype(BF16)
            dov_ref[:, cols] = dv[tail:]

        @pl.when(is_odd())
        def near_terms_made():
            dtv_ref[:, cols] = terms_ref[:tail, cols].astype(BF16)
            dov_ref[:, cols] = terms_ref[tail:, cols]


def call(kernel, spaces, outs, scratch, flops, mib, *args, aliases={}):
    vmem = pl.BlockSpec(memory_space=pltpu.VMEM)
    moved = sum(a.size * a.dtype.itemsize for a in args) + sum(
        math.prod(o.shape) * jnp.dtype(o.dtype).itemsize for o in outs
    )
    return pl.pallas_call(
        kernel,
        out_shape=outs,
        in_specs=[pl.BlockSpec(memory_space=space) for space in spaces],
        out_specs=[vmem] * len(outs),
        scratch_shapes=scratch,
        input_output_aliases=aliases,
        compiler_params=pltpu.CompilerParams(vmem_limit_bytes=mib * 2**20),
        cost_estimate=pl.CostEstimate(flops=flops, bytes_accessed=moved, transcendentals=0),
    )(*args)


def body(q, g, tk, tv, ck, cv, row_list, read_owner, read_tile, read_list, read_count):
    ctx = lax.axis_size("ctx")
    rows, q_width = q.shape
    kv_width = tk.shape[1]
    heads = kv_width // WIDTH
    group_rows = rows * (q_width // kv_width)
    own_keys = ck.shape[0]
    own = own_keys // TILE
    far_keys = (ctx - 1) * own_keys
    near_keys = rows + own_keys
    slots = -(-ctx * own // 8) * 8
    unroll = ctx <= 2
    row_list = row_list.reshape(1, rows)

    def shifted(x, shift):
        return lax.ppermute(x, "ctx", [(o, (o - shift) % ctx) for o in range(ctx)])

    far_k = [shifted(ck, s) for s in range(1, ctx)]
    shape = jax.ShapeDtypeStruct
    product = 2 * q_width * rows * WIDTH
    small = read_owner.shape
    here = [
        pltpu.with_memory_space_constraint(a, pltpu.HBM)
        for a in (q, g, tk, tv, ck, cv, row_list, read_owner, read_tile, read_list)
    ]
    near_outs = [
        pltpu.VMEM(q.shape, BF16),
        pltpu.VMEM(g.shape, BF16),
        pltpu.VMEM((near_keys, kv_width), BF16),
        pltpu.VMEM((near_keys, kv_width), BF16),
        pltpu.VMEM((heads, near_keys, group_rows), F32),
        pltpu.VMEM((heads, near_keys, group_rows), F32),
        pltpu.VMEM((8, heads * group_rows), F32),
        pltpu.VMEM((slots, rows), F32),
    ]
    near = [
        [pltpu.HBM] * len(here) + [pltpu.SMEM],
        near_outs,
        [
            pltpu.VMEM(row_list.shape, jnp.int32),
            pltpu.VMEM(small, jnp.int32),
            pltpu.VMEM(small, jnp.int32),
            pltpu.VMEM(small, jnp.int32),
            pltpu.SemaphoreType.DMA((10,)),
        ],
        2 * product * near_keys // WIDTH,
        32,
        *here, read_count,
    ]
    early = list(call(functools.partial(near_kernel, ctx, True), *near))
    own_v, early[-1] = lax.optimization_barrier((cv, early[-1]))
    far_v = [shifted(own_v, s) for s in range(1, ctx)]
    near[0] = near[0] + [pltpu.VMEM] * NEAR_OUTS
    first = len(here) + 1
    early = [pltpu.with_memory_space_constraint(a, pltpu.VMEM) for a in early]
    q, g, near_k, near_v, near_p, near_d, stats, table = call(
        functools.partial(near_kernel, ctx, False), *near, *early,
        aliases={first + i: i for i in range(NEAR_OUTS)},
    )
    mib = 32 if unroll else 60
    total = [] if unroll else [pltpu.VMEM((far_keys, WIDTH), F32)]
    far_k = far_k[0] if ctx == 2 else jnp.concatenate(far_k, axis=0)
    back_v, far_p, fin = call(
        functools.partial(far_key_kernel, unroll),
        [pltpu.VMEM] * 5,
        [
            shape((ctx - 1, own_keys, kv_width), BF16),
            shape((heads, far_keys, group_rows), BF16),
            shape((8, heads * group_rows), F32),
        ],
        total,
        2 * product * far_keys // WIDTH,
        mib,
        q, g, far_k, stats, table,
    )
    returned_v = [shifted(back_v[s - 1], -s) for s in range(1, ctx)]
    far_v = far_v[0] if ctx == 2 else jnp.concatenate(far_v, axis=0)
    back_k, far_ds, delta, terms = call(
        functools.partial(far_value_kernel, unroll),
        [pltpu.VMEM] * 6,
        [
            shape((ctx - 1, own_keys, kv_width), BF16),
            shape((heads, far_keys, group_rows), BF16),
            shape((8, heads * group_rows), F32),
            shape((near_keys, kv_width), F32),
        ],
        [pltpu.VMEM((heads, near_keys, group_rows), BF16)] + total,
        2 * product * far_keys // WIDTH,
        mib,
        q, g, far_v, far_p, fin, near_p,
    )
    returned_k = [shifted(back_k[s - 1], -s) for s in range(1, ctx)]
    dq, dtk, dtv, dok, dov = call(
        functools.partial(last_kernel, unroll),
        [pltpu.VMEM] * 10,
        [
            shape(q.shape, BF16),
            shape(tk.shape, BF16),
            shape(tv.shape, BF16),
            shape(ck.shape, F32),
            shape(cv.shape, F32),
        ],
        [pltpu.VMEM((heads, near_keys, group_rows), BF16)] * 2,
        product * (3 * near_keys + far_keys) // WIDTH,
        mib,
        q, g, near_k, near_p, near_d, fin, delta, far_k, far_ds, terms,
    )

    def summed(after, own_sum, returned):
        return call(
            sum_kernel,
            [pltpu.HBM] + [pltpu.VMEM] * (1 + len(returned)),
            [shape(own_sum.shape, F32)],
            [],
            0,
            mib,
            pltpu.with_memory_space_constraint(after, pltpu.HBM), own_sum, *returned,
        )[0]

    dov = summed(dq, dov, returned_v)
    dok = summed(dov, dok, returned_k)
    return dq, dtk, dtv, dok, dov


def solution(mesh):
    wide = P(("dp", "ctx"), "tp")
    lone = P(("dp", "ctx"))
    flat = P(("dp", "ctx"), None)
    return jax.shard_map(
        body,
        mesh=mesh,
        in_specs=(wide,) * 6 + (lone, flat, flat, flat, lone),
        out_specs=(wide,) * 5,
        check_vma=False,
    )
```

```python
import functools
import math

import jax
import jax.numpy as jnp
from jax import lax
from jax.experimental import pallas as pl
from jax.experimental.pallas import tpu as pltpu
from jax.sharding import PartitionSpec as P

WIDTH = 128
TILE = 128
PAIR = 2 * WIDTH
NEAR_OUTS = 8
NEG = -1e30
SCALE = 1.0 / math.sqrt(WIDTH)
SCALE2 = SCALE * math.log2(math.e)
F32 = jnp.float32
BF16 = jnp.bfloat16


def dot_nt(a, b):
    return lax.dot_general(a, b, (((1,), (1,)), ((), ())), preferred_element_type=F32)


def dot_nn(a, b):
    return lax.dot_general(a, b, (((1,), (0,)), ((), ())), preferred_element_type=F32)


def dot_tn(a, b):
    return lax.dot_general(a, b, (((0,), (0,)), ((), ())), preferred_element_type=F32)


def repeat(steps, unroll, step):
    if unroll:
        for i in range(steps):
            step(i)
    else:

        def one(i, carry):
            step(i)
            return carry

        lax.fori_loop(0, steps, one, 0)


def added(steps, unroll, step, total_ref):
    if unroll:
        return functools.reduce(jnp.add, [step(i) for i in range(steps)])
    (total_ref,) = total_ref
    total_ref[...] = jnp.zeros_like(total_ref)

    def one(i):
        total_ref[...] += step(i)

    repeat(steps, unroll, one)
    return total_ref[...]


def columns(i, width):
    if isinstance(i, int):
        return pl.ds(i * width, width)
    return pl.ds(pl.multiple_of(i * width, width), width)


def pair_rows(ref, i):
    block = ref[:, columns(i, PAIR)]
    return jnp.concatenate([block[:, :WIDTH], block[:, WIDTH:]], axis=0)


def stacked_rows(ref, head, group):
    first = head * group
    return jnp.concatenate(
        [ref[:, (first + g) * WIDTH : (first + g + 1) * WIDTH] for g in range(group)], axis=0
    )


def twice(row):
    return jnp.concatenate([row, row], axis=1)


def tile_bias(table, first, tiles):
    return [twice(table[first + t : first + t + 1, :]) for t in range(tiles)]


def add_tiles(scores, biases):
    parts = [
        scores[t * TILE : (t + 1) * TILE, :] * SCALE2 + bias for t, bias in enumerate(biases)
    ]
    return parts[0] if len(parts) == 1 else jnp.concatenate(parts, axis=0)


def tail_bias(row_list):
    rows = row_list.shape[1]
    cut = jnp.sum((row_list == 0).astype(jnp.int32), axis=1, keepdims=True)
    key_at = lax.broadcasted_iota(jnp.int32, (rows, rows), 0)
    row_at = lax.broadcasted_iota(jnp.int32, (rows, rows), 1)
    allowed = ((key_at < cut) == (row_at < cut)) & (key_at <= row_at)
    return twice(jnp.where(allowed, 0.0, NEG).astype(F32))


def is_odd():
    return lax.rem(lax.axis_index("dp"), 2) == 1


def value_part_late():
    return jnp.logical_and(jnp.logical_not(is_odd()), lax.axis_index("ctx") > 0)


def load_copies(ins, q_ref, g_ref, k_ref, v_ref, small_refs, sems):
    q_in, g_in, tk_in, tv_in, ok_in, ov_in, *small_ins = ins
    tail = tk_in.shape[0]
    moves = list(zip(small_ins, small_refs)) + [
        (tk_in, k_ref.at[:tail]), (ok_in, k_ref.at[tail:]), (q_in, q_ref),
        (tv_in, v_ref.at[:tail]), (ov_in, v_ref.at[tail:]), (g_in, g_ref),
    ]
    copies = [pltpu.make_async_copy(a, b, sems.at[i]) for i, (a, b) in enumerate(moves)]
    for copy in copies:
        copy.start()
    return copies


def near_key_work(
    ctx, own, copies, q_ref, k_ref, p_ref, stats_ref, table_ref, rl_ref, ro_ref, rt_ref, rs_ref, rc_ref
):
    heads = k_ref.shape[1] // WIDTH
    per_head = q_ref.shape[1] // PAIR // heads
    reads = ro_ref.shape[1]
    slots = table_ref.shape[0]
    for copy in copies[:4]:
        copy.wait()
    row_list = rl_ref[...]
    owner = ro_ref[...] - lax.axis_index("ctx")
    owner = jnp.where(owner < 0, owner + ctx, owner)
    wanted = owner * own + rt_ref[...]
    live = lax.broadcasted_iota(jnp.int32, (1, reads), 1) < rc_ref[0]
    wanted = jnp.where(live, wanted, -1)
    hit = lax.broadcasted_iota(jnp.int32, (slots, reads), 0) == wanted
    first = rs_ref[...] == 0
    count0 = jnp.sum(jnp.where(hit & first, 1.0, 0.0), axis=1, keepdims=True)
    count1 = jnp.sum(jnp.where(hit & jnp.logical_not(first), 1.0, 0.0), axis=1, keepdims=True)
    count = jnp.where(row_list == 0, count0, count1)
    table = jnp.where(count > 0.5, jnp.log2(jnp.maximum(count, 1.0)), NEG)
    table_ref[...] = table
    biases = [tail_bias(row_list)] + tile_bias(table, 0, own)
    for copy in copies[4:7]:
        copy.wait()
    for head in range(heads):
        cols = slice(head * WIDTH, (head + 1) * WIDTH)
        for i in range(per_head):
            pair = head * per_head + i
            at = columns(pair, PAIR)
            s = add_tiles(dot_nt(k_ref[:, cols], pair_rows(q_ref, pair)), biases)
            top = jnp.max(s, axis=0, keepdims=True)
            p = jnp.exp2(s - top)
            p_ref[head, :, columns(i, PAIR)] = p
            stats_ref[0:1, at] = top
            stats_ref[1:2, at] = jnp.sum(p, axis=0, keepdims=True)


def near_value_work(g_ref, v_ref, p_ref, d_ref, stats_ref):
    heads = v_ref.shape[1] // WIDTH
    per_head = g_ref.shape[1] // PAIR // heads
    for head in range(heads):
        cols = slice(head * WIDTH, (head + 1) * WIDTH)
        for i in range(per_head):
            pair = head * per_head + i
            here = columns(i, PAIR)
            d = dot_nt(v_ref[:, cols], pair_rows(g_ref, pair))
            d_ref[head, :, here] = d
            cross = jnp.sum(p_ref[head, :, here] * d, axis=0, keepdims=True)
            stats_ref[2:3, columns(pair, PAIR)] = cross


def near_kernel(ctx, early, *refs):
    ins, rc_ref, rest = refs[:10], refs[10], refs[11 if early else 11 + NEAR_OUTS :]
    q_ref, g_ref, k_ref, v_ref, p_ref, d_ref, stats_ref, table_ref = rest[:NEAR_OUTS]
    small_refs, sems = rest[NEAR_OUTS:-1], rest[-1]
    own = ins[4].shape[0] // TILE

    def key_part():
        copies = load_copies(ins, q_ref, g_ref, k_ref, v_ref, small_refs, sems)
        near_key_work(
            ctx, own, copies, q_ref, k_ref, p_ref, stats_ref, table_ref, *small_refs, rc_ref
        )
        for copy in copies[7:]:
            copy.wait()

    if early:
        pl.when(is_odd())(key_part)
    else:
        pl.when(jnp.logical_not(is_odd()))(key_part)

        @pl.when(jnp.logical_not(value_part_late()))
        def value_part():
            near_value_work(g_ref, v_ref, p_ref, d_ref, stats_ref)


def far_key_kernel(
    unroll, q_ref, g_ref, k_ref, stats_ref, table_ref, back_ref, p_ref, fin_ref, *total_ref
):
    far_tiles = k_ref.shape[0] // TILE
    heads = k_ref.shape[1] // WIDTH
    per_head = q_ref.shape[1] // PAIR // heads
    shifts, own_keys, _ = back_ref.shape
    biases = tile_bias(table_ref[...], own_keys // TILE, far_tiles)
    for head in range(heads):
        cols = slice(head * WIDTH, (head + 1) * WIDTH)

        def step(i):
            pair = head * per_head + i
            at = columns(pair, PAIR)
            here = columns(i, PAIR)
            s = add_tiles(dot_nt(k_ref[:, cols], pair_rows(q_ref, pair)), biases)
            near_top = stats_ref[0:1, at]
            top = jnp.maximum(near_top, jnp.max(s, axis=0, keepdims=True))
            p = jnp.exp2(s - top)
            fade = jnp.exp2(near_top - top)
            inverse = 1.0 / (stats_ref[1:2, at] * fade + jnp.sum(p, axis=0, keepdims=True))
            fin_ref[0:1, at] = fade * inverse
            p = (p * inverse).astype(BF16)
            p_ref[head, :, here] = p
            return dot_nn(p, pair_rows(g_ref, pair))

        dv = added(per_head, unroll, step, total_ref).astype(BF16)
        for shift in range(shifts):
            back_ref[shift, :, cols] = dv[shift * own_keys : (shift + 1) * own_keys]


def far_value_kernel(
    unroll, q_ref, g_ref, v_ref, p_ref, fin_ref, near_v_ref, near_p_ref, *refs
):
    d_ref, stats_ref, back_ref, ds_ref, delta_ref, *total_ref = refs[2:]
    heads = v_ref.shape[1] // WIDTH
    per_head = q_ref.shape[1] // PAIR // heads
    shifts, own_keys, _ = back_ref.shape

    @pl.when(value_part_late())
    def value_part():
        near_value_work(g_ref, near_v_ref, near_p_ref, d_ref, stats_ref)

    for head in range(heads):
        cols = slice(head * WIDTH, (head + 1) * WIDTH)

        def step(i):
            pair = head * per_head + i
            at = columns(pair, PAIR)
            here = columns(i, PAIR)
            d = dot_nt(v_ref[:, cols], pair_rows(g_ref, pair))
            p = p_ref[head, :, here].astype(F32)
            delta = stats_ref[2:3, at] * fin_ref[0:1, at] + jnp.sum(p * d, axis=0, keepdims=True)
            delta_ref[0:1, at] = delta
            ds = (p * (d - delta)).astype(BF16)
            ds_ref[head, :, here] = ds
            return dot_nn(ds, pair_rows(q_ref, pair))

        dk = (added(per_head, unroll, step, total_ref) * SCALE).astype(BF16)
        for shift in range(shifts):
            back_ref[shift, :, cols] = dk[shift * own_keys : (shift + 1) * own_keys]


def sum_kernel(after_ref, own_ref, *refs):
    total = own_ref[...]
    for ref in refs[:-1]:
        total = total + ref[...].astype(F32)
    refs[-1][...] = total


def last_kernel(
    unroll, q_ref, g_ref, k_ref, p_ref, d_ref, fin_ref, delta_ref, fk_ref, fds_ref,
    dq_ref, dtk_ref, dtv_ref, dok_ref, dov_ref, low_ref, ds_ref,
):
    tail = dtk_ref.shape[0]
    heads = k_ref.shape[1] // WIDTH
    per_head = q_ref.shape[1] // PAIR // heads
    for head in range(heads):
        cols = slice(head * WIDTH, (head + 1) * WIDTH)

        def step(i):
            pair = head * per_head + i
            at = columns(pair, PAIR)
            here = columns(i, PAIR)
            p = p_ref[head, :, here] * fin_ref[0:1, at]
            ds = (p * (d_ref[head, :, here] - delta_ref[0:1, at])).astype(BF16)
            low_ref[head, :, here] = p.astype(BF16)
            ds_ref[head, :, here] = ds
            dq = dot_tn(k_ref[:, cols], ds) + dot_tn(fk_ref[:, cols], fds_ref[head, :, here])
            dq = dq * SCALE
            dq = jnp.concatenate([dq[:, :WIDTH].T, dq[:, WIDTH:].T], axis=1)
            dq_ref[:, at] = dq.astype(BF16)

        repeat(per_head, unroll, step)
        dk = dot_nn(ds_ref[head], stacked_rows(q_ref, head, 2 * per_head)) * SCALE
        dv = dot_nn(low_ref[head], stacked_rows(g_ref, head, 2 * per_head))
        dtk_ref[:, cols] = dk[:tail].astype(BF16)
        dtv_ref[:, cols] = dv[:tail].astype(BF16)
        dok_ref[:, cols] = dk[tail:]
        dov_ref[:, cols] = dv[tail:]


def call(kernel, spaces, outs, scratch, flops, mib, *args, aliases={}):
    vmem = pl.BlockSpec(memory_space=pltpu.VMEM)
    moved = sum(a.size * a.dtype.itemsize for a in args) + sum(
        math.prod(o.shape) * jnp.dtype(o.dtype).itemsize for o in outs
    )
    return pl.pallas_call(
        kernel,
        out_shape=outs,
        in_specs=[pl.BlockSpec(memory_space=space) for space in spaces],
        out_specs=[vmem] * len(outs),
        scratch_shapes=scratch,
        input_output_aliases=aliases,
        compiler_params=pltpu.CompilerParams(vmem_limit_bytes=mib * 2**20),
        cost_estimate=pl.CostEstimate(flops=flops, bytes_accessed=moved, transcendentals=0),
    )(*args)


def body(q, g, tk, tv, ck, cv, row_list, read_owner, read_tile, read_list, read_count):
    ctx = lax.axis_size("ctx")
    rows, q_width = q.shape
    kv_width = tk.shape[1]
    heads = kv_width // WIDTH
    group_rows = rows * (q_width // kv_width)
    own_keys = ck.shape[0]
    own = own_keys // TILE
    far_keys = (ctx - 1) * own_keys
    near_keys = rows + own_keys
    slots = -(-ctx * own // 8) * 8
    unroll = ctx <= 2
    row_list = row_list.reshape(1, rows)

    def shifted(x, shift):
        return lax.ppermute(x, "ctx", [(o, (o - shift) % ctx) for o in range(ctx)])

    far_k = [shifted(ck, s) for s in range(1, ctx)]
    shape = jax.ShapeDtypeStruct
    product = 2 * q_width * rows * WIDTH
    small = read_owner.shape
    here = [
        pltpu.with_memory_space_constraint(a, pltpu.HBM)
        for a in (q, g, tk, tv, ck, cv, row_list, read_owner, read_tile, read_list)
    ]
    near_outs = [
        pltpu.VMEM(q.shape, BF16),
        pltpu.VMEM(g.shape, BF16),
        pltpu.VMEM((near_keys, kv_width), BF16),
        pltpu.VMEM((near_keys, kv_width), BF16),
        pltpu.VMEM((heads, near_keys, group_rows), F32),
        pltpu.VMEM((heads, near_keys, group_rows), F32),
        pltpu.VMEM((8, heads * group_rows), F32),
        pltpu.VMEM((slots, rows), F32),
    ]
    near = [
        [pltpu.HBM] * len(here) + [pltpu.SMEM],
        near_outs,
        [
            pltpu.VMEM(row_list.shape, jnp.int32),
            pltpu.VMEM(small, jnp.int32),
            pltpu.VMEM(small, jnp.int32),
            pltpu.VMEM(small, jnp.int32),
            pltpu.SemaphoreType.DMA((10,)),
        ],
        2 * product * near_keys // WIDTH,
        32,
        *here, read_count,
    ]
    early = list(call(functools.partial(near_kernel, ctx, True), *near))
    own_v, early[-1] = lax.optimization_barrier((cv, early[-1]))
    far_v = [shifted(own_v, s) for s in range(1, ctx)]
    near[0] = near[0] + [pltpu.VMEM] * NEAR_OUTS
    first = len(here) + 1
    early = [pltpu.with_memory_space_constraint(a, pltpu.VMEM) for a in early]
    q, g, near_k, near_v, near_p, near_d, stats, table = call(
        functools.partial(near_kernel, ctx, False), *near, *early,
        aliases={first + i: i for i in range(NEAR_OUTS)},
    )
    mib = 32 if unroll else 60
    total = [] if unroll else [pltpu.VMEM((far_keys, WIDTH), F32)]
    far_k = far_k[0] if ctx == 2 else jnp.concatenate(far_k, axis=0)
    back_v, far_p, fin = call(
        functools.partial(far_key_kernel, unroll),
        [pltpu.VMEM] * 5,
        [
            shape((ctx - 1, own_keys, kv_width), BF16),
            shape((heads, far_keys, group_rows), BF16),
            shape((8, heads * group_rows), F32),
        ],
        total,
        2 * product * far_keys // WIDTH,
        mib,
        q, g, far_k, stats, table,
    )
    returned_v = [shifted(back_v[s - 1], -s) for s in range(1, ctx)]
    far_v = far_v[0] if ctx == 2 else jnp.concatenate(far_v, axis=0)
    near_d, stats = (pltpu.with_memory_space_constraint(a, pltpu.VMEM) for a in (near_d, stats))
    near_d, stats, back_k, far_ds, delta = call(
        functools.partial(far_value_kernel, unroll),
        [pltpu.VMEM] * 9,
        [
            pltpu.VMEM(near_d.shape, F32),
            pltpu.VMEM(stats.shape, F32),
            shape((ctx - 1, own_keys, kv_width), BF16),
            shape((heads, far_keys, group_rows), BF16),
            shape((8, heads * group_rows), F32),
        ],
        total,
        2 * product * far_keys // WIDTH,
        mib,
        q, g, far_v, far_p, fin, near_v, near_p, near_d, stats,
        aliases={7: 0, 8: 1},
    )
    returned_k = [shifted(back_k[s - 1], -s) for s in range(1, ctx)]
    dq, dtk, dtv, dok, dov = call(
        functools.partial(last_kernel, unroll),
        [pltpu.VMEM] * 9,
        [
            shape(q.shape, BF16),
            shape(tk.shape, BF16),
            shape(tv.shape, BF16),
            shape(ck.shape, F32),
            shape(cv.shape, F32),
        ],
        [pltpu.VMEM((heads, near_keys, group_rows), BF16)] * 2,
        product * (3 * near_keys + far_keys) // WIDTH,
        mib,
        q, g, near_k, near_p, near_d, fin, delta, far_k, far_ds,
    )

    def summed(after, own_sum, returned):
        return call(
            sum_kernel,
            [pltpu.HBM] + [pltpu.VMEM] * (1 + len(returned)),
            [shape(own_sum.shape, F32)],
            [],
            0,
            mib,
            pltpu.with_memory_space_constraint(after, pltpu.HBM), own_sum, *returned,
        )[0]

    dov = summed(dq, dov, returned_v)
    dok = summed(dov, dok, returned_k)
    return dq, dtk, dtv, dok, dov


def solution(mesh):
    wide = P(("dp", "ctx"), "tp")
    lone = P(("dp", "ctx"))
    flat = P(("dp", "ctx"), None)
    return jax.shard_map(
        body,
        mesh=mesh,
        in_specs=(wide,) * 6 + (lone, flat, flat, flat, lone),
        out_specs=(wide,) * 5,
        check_vma=False,
    )
```

```python
import functools
import math

import jax
import jax.numpy as jnp
from jax import lax
from jax.experimental import pallas as pl
from jax.experimental.pallas import tpu as pltpu
from jax.sharding import PartitionSpec as P

WIDTH = 128
TILE = 128
PAIR = 2 * WIDTH
NEAR_OUTS = 12
NEG = -1e30
SCALE = 1.0 / math.sqrt(WIDTH)
SCALE2 = SCALE * math.log2(math.e)
F32 = jnp.float32
BF16 = jnp.bfloat16


def dot_nt(a, b):
    return lax.dot_general(a, b, (((1,), (1,)), ((), ())), preferred_element_type=F32)


def dot_nn(a, b):
    return lax.dot_general(a, b, (((1,), (0,)), ((), ())), preferred_element_type=F32)


def dot_tn(a, b):
    return lax.dot_general(a, b, (((0,), (0,)), ((), ())), preferred_element_type=F32)


def repeat(steps, unroll, step):
    if unroll:
        for i in range(steps):
            step(i)
    else:

        def one(i, carry):
            step(i)
            return carry

        lax.fori_loop(0, steps, one, 0)


def added(steps, unroll, step, total_ref):
    if unroll:
        return functools.reduce(jnp.add, [step(i) for i in range(steps)])
    (total_ref,) = total_ref
    total_ref[...] = jnp.zeros_like(total_ref)

    def one(i):
        total_ref[...] += step(i)

    repeat(steps, unroll, one)
    return total_ref[...]


def columns(i, width):
    if isinstance(i, int):
        return pl.ds(i * width, width)
    return pl.ds(pl.multiple_of(i * width, width), width)


def pair_rows(ref, i):
    block = ref[:, columns(i, PAIR)]
    return jnp.concatenate([block[:, :WIDTH], block[:, WIDTH:]], axis=0)


def stacked_rows(ref, head, group):
    first = head * group
    return jnp.concatenate(
        [ref[:, (first + g) * WIDTH : (first + g + 1) * WIDTH] for g in range(group)], axis=0
    )


def twice(row):
    return jnp.concatenate([row, row], axis=1)


def tile_bias(table, first, tiles):
    return [twice(table[first + t : first + t + 1, :]) for t in range(tiles)]


def add_tiles(scores, biases):
    parts = [
        scores[t * TILE : (t + 1) * TILE, :] * SCALE2 + bias for t, bias in enumerate(biases)
    ]
    return parts[0] if len(parts) == 1 else jnp.concatenate(parts, axis=0)


def tail_bias(row_list):
    rows = row_list.shape[1]
    cut = jnp.sum((row_list == 0).astype(jnp.int32), axis=1, keepdims=True)
    key_at = lax.broadcasted_iota(jnp.int32, (rows, rows), 0)
    row_at = lax.broadcasted_iota(jnp.int32, (rows, rows), 1)
    allowed = ((key_at < cut) == (row_at < cut)) & (key_at <= row_at)
    return twice(jnp.where(allowed, 0.0, NEG).astype(F32))


def is_odd():
    return lax.rem(lax.axis_index("dp"), 2) == 1


def value_part_late():
    return jnp.logical_and(jnp.logical_not(is_odd()), lax.axis_index("ctx") > 0)


def load_copies(ins, q_ref, g_ref, k_ref, v_ref, small_refs, sems):
    q_in, g_in, tk_in, tv_in, ok_in, ov_in, *small_ins = ins
    tail = tk_in.shape[0]
    moves = list(zip(small_ins, small_refs)) + [
        (tk_in, k_ref.at[:tail]), (ok_in, k_ref.at[tail:]), (q_in, q_ref),
        (tv_in, v_ref.at[:tail]), (ov_in, v_ref.at[tail:]), (g_in, g_ref),
    ]
    copies = [pltpu.make_async_copy(a, b, sems.at[i]) for i, (a, b) in enumerate(moves)]
    for copy in copies:
        copy.start()
    return copies


def near_key_work(
    ctx, own, q_ref, k_ref, p_ref, stats_ref, table_ref, rl_ref, ro_ref, rt_ref, rs_ref, rc_ref
):
    heads = k_ref.shape[1] // WIDTH
    per_head = q_ref.shape[1] // PAIR // heads
    reads = ro_ref.shape[1]
    slots = table_ref.shape[0]
    row_list = rl_ref[...]
    owner = ro_ref[...] - lax.axis_index("ctx")
    owner = jnp.where(owner < 0, owner + ctx, owner)
    wanted = owner * own + rt_ref[...]
    live = lax.broadcasted_iota(jnp.int32, (1, reads), 1) < rc_ref[0]
    wanted = jnp.where(live, wanted, -1)
    hit = lax.broadcasted_iota(jnp.int32, (slots, reads), 0) == wanted
    first = rs_ref[...] == 0
    count0 = jnp.sum(jnp.where(hit & first, 1.0, 0.0), axis=1, keepdims=True)
    count1 = jnp.sum(jnp.where(hit & jnp.logical_not(first), 1.0, 0.0), axis=1, keepdims=True)
    count = jnp.where(row_list == 0, count0, count1)
    table = jnp.where(count > 0.5, jnp.log2(jnp.maximum(count, 1.0)), NEG)
    table_ref[...] = table
    biases = [tail_bias(row_list)] + tile_bias(table, 0, own)
    for head in range(heads):
        cols = slice(head * WIDTH, (head + 1) * WIDTH)
        for i in range(per_head):
            pair = head * per_head + i
            at = columns(pair, PAIR)
            s = add_tiles(dot_nt(k_ref[:, cols], pair_rows(q_ref, pair)), biases)
            top = jnp.max(s, axis=0, keepdims=True)
            p = jnp.exp2(s - top)
            p_ref[head, :, columns(i, PAIR)] = p
            stats_ref[0:1, at] = top
            stats_ref[1:2, at] = jnp.sum(p, axis=0, keepdims=True)


def near_value_work(g_ref, v_ref, p_ref, d_ref, stats_ref):
    heads = v_ref.shape[1] // WIDTH
    per_head = g_ref.shape[1] // PAIR // heads
    for head in range(heads):
        cols = slice(head * WIDTH, (head + 1) * WIDTH)
        for i in range(per_head):
            pair = head * per_head + i
            here = columns(i, PAIR)
            d = dot_nt(v_ref[:, cols], pair_rows(g_ref, pair))
            d_ref[head, :, here] = d
            cross = jnp.sum(p_ref[head, :, here] * d, axis=0, keepdims=True)
            stats_ref[2:3, columns(pair, PAIR)] = cross


def near_kernel(ctx, early, *refs):
    ins, rc_ref, rest = refs[:10], refs[10], refs[11 if early else 11 + NEAR_OUTS :]
    q_ref, g_ref, k_ref, v_ref, *small_refs = rest[:8]
    p_ref, d_ref, stats_ref, table_ref, sems = rest[8:]

    @pl.when(is_odd() == early)
    def load():
        copies = load_copies(ins, q_ref, g_ref, k_ref, v_ref, small_refs, sems)
        for copy in copies:
            copy.wait()

    if not early:
        own = ins[4].shape[0] // TILE
        near_key_work(ctx, own, q_ref, k_ref, p_ref, stats_ref, table_ref, *small_refs, rc_ref)

        @pl.when(jnp.logical_not(value_part_late()))
        def value_part():
            near_value_work(g_ref, v_ref, p_ref, d_ref, stats_ref)


def far_key_kernel(
    unroll, q_ref, g_ref, k_ref, stats_ref, table_ref, back_ref, p_ref, fin_ref, *total_ref
):
    far_tiles = k_ref.shape[0] // TILE
    heads = k_ref.shape[1] // WIDTH
    per_head = q_ref.shape[1] // PAIR // heads
    shifts, own_keys, _ = back_ref.shape
    biases = tile_bias(table_ref[...], own_keys // TILE, far_tiles)
    for head in range(heads):
        cols = slice(head * WIDTH, (head + 1) * WIDTH)

        def step(i):
            pair = head * per_head + i
            at = columns(pair, PAIR)
            here = columns(i, PAIR)
            s = add_tiles(dot_nt(k_ref[:, cols], pair_rows(q_ref, pair)), biases)
            near_top = stats_ref[0:1, at]
            top = jnp.maximum(near_top, jnp.max(s, axis=0, keepdims=True))
            p = jnp.exp2(s - top)
            fade = jnp.exp2(near_top - top)
            inverse = 1.0 / (stats_ref[1:2, at] * fade + jnp.sum(p, axis=0, keepdims=True))
            fin_ref[0:1, at] = fade * inverse
            p = (p * inverse).astype(BF16)
            p_ref[head, :, here] = p
            return dot_nn(p, pair_rows(g_ref, pair))

        dv = added(per_head, unroll, step, total_ref).astype(BF16)
        for shift in range(shifts):
            back_ref[shift, :, cols] = dv[shift * own_keys : (shift + 1) * own_keys]


def far_value_kernel(
    unroll, q_ref, g_ref, v_ref, p_ref, fin_ref, near_v_ref, near_p_ref, *refs
):
    d_ref, stats_ref, back_ref, ds_ref, delta_ref, *total_ref = refs[2:]
    heads = v_ref.shape[1] // WIDTH
    per_head = q_ref.shape[1] // PAIR // heads
    shifts, own_keys, _ = back_ref.shape

    @pl.when(value_part_late())
    def value_part():
        near_value_work(g_ref, near_v_ref, near_p_ref, d_ref, stats_ref)

    for head in range(heads):
        cols = slice(head * WIDTH, (head + 1) * WIDTH)

        def step(i):
            pair = head * per_head + i
            at = columns(pair, PAIR)
            here = columns(i, PAIR)
            d = dot_nt(v_ref[:, cols], pair_rows(g_ref, pair))
            p = p_ref[head, :, here].astype(F32)
            delta = stats_ref[2:3, at] * fin_ref[0:1, at] + jnp.sum(p * d, axis=0, keepdims=True)
            delta_ref[0:1, at] = delta
            ds = (p * (d - delta)).astype(BF16)
            ds_ref[head, :, here] = ds
            return dot_nn(ds, pair_rows(q_ref, pair))

        dk = (added(per_head, unroll, step, total_ref) * SCALE).astype(BF16)
        for shift in range(shifts):
            back_ref[shift, :, cols] = dk[shift * own_keys : (shift + 1) * own_keys]


def sum_kernel(after_ref, own_ref, *refs):
    total = own_ref[...]
    for ref in refs[:-1]:
        total = total + ref[...].astype(F32)
    refs[-1][...] = total


def last_kernel(
    unroll, q_ref, g_ref, k_ref, p_ref, d_ref, fin_ref, delta_ref, fk_ref, fds_ref,
    dq_ref, dtk_ref, dtv_ref, dok_ref, dov_ref, low_ref, ds_ref,
):
    tail = dtk_ref.shape[0]
    heads = k_ref.shape[1] // WIDTH
    per_head = q_ref.shape[1] // PAIR // heads
    for head in range(heads):
        cols = slice(head * WIDTH, (head + 1) * WIDTH)

        def step(i):
            pair = head * per_head + i
            at = columns(pair, PAIR)
            here = columns(i, PAIR)
            p = p_ref[head, :, here] * fin_ref[0:1, at]
            ds = (p * (d_ref[head, :, here] - delta_ref[0:1, at])).astype(BF16)
            low_ref[head, :, here] = p.astype(BF16)
            ds_ref[head, :, here] = ds
            dq = dot_tn(k_ref[:, cols], ds) + dot_tn(fk_ref[:, cols], fds_ref[head, :, here])
            dq = dq * SCALE
            dq = jnp.concatenate([dq[:, :WIDTH].T, dq[:, WIDTH:].T], axis=1)
            dq_ref[:, at] = dq.astype(BF16)

        repeat(per_head, unroll, step)
        dk = dot_nn(ds_ref[head], stacked_rows(q_ref, head, 2 * per_head)) * SCALE
        dv = dot_nn(low_ref[head], stacked_rows(g_ref, head, 2 * per_head))
        dtk_ref[:, cols] = dk[:tail].astype(BF16)
        dtv_ref[:, cols] = dv[:tail].astype(BF16)
        dok_ref[:, cols] = dk[tail:]
        dov_ref[:, cols] = dv[tail:]


def call(kernel, spaces, outs, scratch, flops, mib, *args, aliases={}):
    vmem = pl.BlockSpec(memory_space=pltpu.VMEM)
    moved = sum(a.size * a.dtype.itemsize for a in args) + sum(
        math.prod(o.shape) * jnp.dtype(o.dtype).itemsize for o in outs
    )
    return pl.pallas_call(
        kernel,
        out_shape=outs,
        in_specs=[pl.BlockSpec(memory_space=space) for space in spaces],
        out_specs=[vmem] * len(outs),
        scratch_shapes=scratch,
        input_output_aliases=aliases,
        compiler_params=pltpu.CompilerParams(vmem_limit_bytes=mib * 2**20),
        cost_estimate=pl.CostEstimate(flops=flops, bytes_accessed=moved, transcendentals=0),
    )(*args)


def body(q, g, tk, tv, ck, cv, row_list, read_owner, read_tile, read_list, read_count):
    ctx = lax.axis_size("ctx")
    rows, q_width = q.shape
    kv_width = tk.shape[1]
    heads = kv_width // WIDTH
    group_rows = rows * (q_width // kv_width)
    own_keys = ck.shape[0]
    own = own_keys // TILE
    far_keys = (ctx - 1) * own_keys
    near_keys = rows + own_keys
    slots = -(-ctx * own // 8) * 8
    unroll = ctx <= 2
    row_list = row_list.reshape(1, rows)

    def shifted(x, shift):
        return lax.ppermute(x, "ctx", [(o, (o - shift) % ctx) for o in range(ctx)])

    far_k = [shifted(ck, s) for s in range(1, ctx)]
    shape = jax.ShapeDtypeStruct
    product = 2 * q_width * rows * WIDTH
    small = read_owner.shape
    here = [
        pltpu.with_memory_space_constraint(a, pltpu.HBM)
        for a in (q, g, tk, tv, ck, cv, row_list, read_owner, read_tile, read_list)
    ]
    near_outs = [
        pltpu.VMEM(q.shape, BF16),
        pltpu.VMEM(g.shape, BF16),
        pltpu.VMEM((near_keys, kv_width), BF16),
        pltpu.VMEM((near_keys, kv_width), BF16),
        pltpu.VMEM(row_list.shape, jnp.int32),
        pltpu.VMEM(small, jnp.int32),
        pltpu.VMEM(small, jnp.int32),
        pltpu.VMEM(small, jnp.int32),
        pltpu.VMEM((heads, near_keys, group_rows), F32),
        pltpu.VMEM((heads, near_keys, group_rows), F32),
        pltpu.VMEM((8, heads * group_rows), F32),
        pltpu.VMEM((slots, rows), F32),
    ]
    near = [
        [pltpu.HBM] * len(here) + [pltpu.SMEM],
        near_outs,
        [pltpu.SemaphoreType.DMA((10,))],
        2 * product * near_keys // WIDTH,
        32,
        *here, read_count,
    ]
    early = list(call(functools.partial(near_kernel, ctx, True), *near))
    own_v, early[-1] = lax.optimization_barrier((cv, early[-1]))
    far_v = [shifted(own_v, s) for s in range(1, ctx)]
    near[0] = near[0] + [pltpu.VMEM] * NEAR_OUTS
    first = len(here) + 1
    early = [pltpu.with_memory_space_constraint(a, pltpu.VMEM) for a in early]
    q, g, near_k, near_v, _, _, _, _, near_p, near_d, stats, table = call(
        functools.partial(near_kernel, ctx, False), *near, *early,
        aliases={first + i: i for i in range(NEAR_OUTS)},
    )
    mib = 32 if unroll else 60
    total = [] if unroll else [pltpu.VMEM((far_keys, WIDTH), F32)]
    far_k = far_k[0] if ctx == 2 else jnp.concatenate(far_k, axis=0)
    back_v, far_p, fin = call(
        functools.partial(far_key_kernel, unroll),
        [pltpu.VMEM] * 5,
        [
            shape((ctx - 1, own_keys, kv_width), BF16),
            shape((heads, far_keys, group_rows), BF16),
            shape((8, heads * group_rows), F32),
        ],
        total,
        2 * product * far_keys // WIDTH,
        mib,
        q, g, far_k, stats, table,
    )
    returned_v = [shifted(back_v[s - 1], -s) for s in range(1, ctx)]
    far_v = far_v[0] if ctx == 2 else jnp.concatenate(far_v, axis=0)
    near_d, stats = (pltpu.with_memory_space_constraint(a, pltpu.VMEM) for a in (near_d, stats))
    near_d, stats, back_k, far_ds, delta = call(
        functools.partial(far_value_kernel, unroll),
        [pltpu.VMEM] * 9,
        [
            pltpu.VMEM(near_d.shape, F32),
            pltpu.VMEM(stats.shape, F32),
            shape((ctx - 1, own_keys, kv_width), BF16),
            shape((heads, far_keys, group_rows), BF16),
            shape((8, heads * group_rows), F32),
        ],
        total,
        2 * product * far_keys // WIDTH,
        mib,
        q, g, far_v, far_p, fin, near_v, near_p, near_d, stats,
        aliases={7: 0, 8: 1},
    )
    returned_k = [shifted(back_k[s - 1], -s) for s in range(1, ctx)]
    dq, dtk, dtv, dok, dov = call(
        functools.partial(last_kernel, unroll),
        [pltpu.VMEM] * 9,
        [
            shape(q.shape, BF16),
            shape(tk.shape, BF16),
            shape(tv.shape, BF16),
            shape(ck.shape, F32),
            shape(cv.shape, F32),
        ],
        [pltpu.VMEM((heads, near_keys, group_rows), BF16)] * 2,
        product * (3 * near_keys + far_keys) // WIDTH,
        mib,
        q, g, near_k, near_p, near_d, fin, delta, far_k, far_ds,
    )

    def summed(after, own_sum, returned):
        return call(
            sum_kernel,
            [pltpu.HBM] + [pltpu.VMEM] * (1 + len(returned)),
            [shape(own_sum.shape, F32)],
            [],
            0,
            mib,
            pltpu.with_memory_space_constraint(after, pltpu.HBM), own_sum, *returned,
        )[0]

    dov = summed(dq, dov, returned_v)
    dok = summed(dov, dok, returned_k)
    return dq, dtk, dtv, dok, dov


def solution(mesh):
    wide = P(("dp", "ctx"), "tp")
    lone = P(("dp", "ctx"))
    flat = P(("dp", "ctx"), None)
    return jax.shard_map(
        body,
        mesh=mesh,
        in_specs=(wide,) * 6 + (lone, flat, flat, flat, lone),
        out_specs=(wide,) * 5,
        check_vma=False,
    )
```

```python
import functools
import math

import jax
import jax.numpy as jnp
from jax import lax
from jax.experimental import pallas as pl
from jax.experimental.pallas import tpu as pltpu
from jax.sharding import PartitionSpec as P

WIDTH = 128
TILE = 128
PAIR = 2 * WIDTH
NEAR_OUTS = 8
NEG = -1e30
SCALE = 1.0 / math.sqrt(WIDTH)
SCALE2 = SCALE * math.log2(math.e)
F32 = jnp.float32
BF16 = jnp.bfloat16


def dot_nt(a, b):
    return lax.dot_general(a, b, (((1,), (1,)), ((), ())), preferred_element_type=F32)


def dot_nn(a, b):
    return lax.dot_general(a, b, (((1,), (0,)), ((), ())), preferred_element_type=F32)


def dot_tn(a, b):
    return lax.dot_general(a, b, (((0,), (0,)), ((), ())), preferred_element_type=F32)


def repeat(steps, unroll, step):
    if unroll:
        for i in range(steps):
            step(i)
    else:

        def one(i, carry):
            step(i)
            return carry

        lax.fori_loop(0, steps, one, 0)


def added(steps, unroll, step, total_ref):
    if unroll:
        return functools.reduce(jnp.add, [step(i) for i in range(steps)])
    (total_ref,) = total_ref
    total_ref[...] = jnp.zeros_like(total_ref)

    def one(i):
        total_ref[...] += step(i)

    repeat(steps, unroll, one)
    return total_ref[...]


def columns(i, width):
    if isinstance(i, int):
        return pl.ds(i * width, width)
    return pl.ds(pl.multiple_of(i * width, width), width)


def pair_rows(ref, i):
    block = ref[:, columns(i, PAIR)]
    return jnp.concatenate([block[:, :WIDTH], block[:, WIDTH:]], axis=0)


def stacked_rows(ref, head, group):
    first = head * group
    return jnp.concatenate(
        [ref[:, (first + g) * WIDTH : (first + g + 1) * WIDTH] for g in range(group)], axis=0
    )


def twice(row):
    return jnp.concatenate([row, row], axis=1)


def tile_bias(table, first, tiles):
    return [twice(table[first + t : first + t + 1, :]) for t in range(tiles)]


def tile_weights(raw, biases, floor=None):
    parts = [raw[t * TILE : (t + 1) * TILE, :] for t in range(len(biases))]
    tops = [] if floor is None else [floor]
    for t, bias in enumerate(biases):
        if bias.shape[0] == 1:
            tops.append(jnp.max(parts[t], axis=0, keepdims=True) * SCALE2 + bias)
        else:
            parts[t] = parts[t] * SCALE2 + bias
            tops.append(jnp.max(parts[t], axis=0, keepdims=True))
    top = functools.reduce(jnp.maximum, tops)
    weights = [
        jnp.exp2(part * SCALE2 + (bias - top) if bias.shape[0] == 1 else part - top)
        for part, bias in zip(parts, biases)
    ]
    return (weights[0] if len(weights) == 1 else jnp.concatenate(weights, axis=0)), top


def tail_bias(row_list):
    rows = row_list.shape[1]
    cut = jnp.sum((row_list == 0).astype(jnp.int32), axis=1, keepdims=True)
    key_at = lax.broadcasted_iota(jnp.int32, (rows, rows), 0)
    row_at = lax.broadcasted_iota(jnp.int32, (rows, rows), 1)
    allowed = ((key_at < cut) == (row_at < cut)) & (key_at <= row_at)
    return twice(jnp.where(allowed, 0.0, NEG).astype(F32))


def is_odd():
    return lax.rem(lax.axis_index("dp"), 2) == 1


def value_part_late():
    return jnp.logical_and(jnp.logical_not(is_odd()), lax.axis_index("ctx") > 0)


def load_copies(ins, q_ref, g_ref, k_ref, v_ref, small_refs, sems):
    q_in, g_in, tk_in, tv_in, ok_in, ov_in, *small_ins = ins
    tail = tk_in.shape[0]
    moves = list(zip(small_ins, small_refs)) + [
        (tk_in, k_ref.at[:tail]), (ok_in, k_ref.at[tail:]), (q_in, q_ref),
        (tv_in, v_ref.at[:tail]), (ov_in, v_ref.at[tail:]), (g_in, g_ref),
    ]
    copies = [pltpu.make_async_copy(a, b, sems.at[i]) for i, (a, b) in enumerate(moves)]
    for copy in copies:
        copy.start()
    return copies


def near_key_work(
    ctx, own, copies, q_ref, k_ref, p_ref, stats_ref, table_ref, rl_ref, ro_ref, rt_ref, rs_ref, rc_ref
):
    heads = k_ref.shape[1] // WIDTH
    per_head = q_ref.shape[1] // PAIR // heads
    reads = ro_ref.shape[1]
    slots = table_ref.shape[0]
    for copy in copies[:4]:
        copy.wait()
    row_list = rl_ref[...]
    owner = ro_ref[...] - lax.axis_index("ctx")
    owner = jnp.where(owner < 0, owner + ctx, owner)
    wanted = owner * own + rt_ref[...]
    live = lax.broadcasted_iota(jnp.int32, (1, reads), 1) < rc_ref[0]
    wanted = jnp.where(live, wanted, -1)
    hit = lax.broadcasted_iota(jnp.int32, (slots, reads), 0) == wanted
    first = rs_ref[...] == 0
    count0 = jnp.sum(jnp.where(hit & first, 1.0, 0.0), axis=1, keepdims=True)
    count1 = jnp.sum(jnp.where(hit & jnp.logical_not(first), 1.0, 0.0), axis=1, keepdims=True)
    count = jnp.where(row_list == 0, count0, count1)
    table = jnp.where(count > 0.5, jnp.log2(jnp.maximum(count, 1.0)), NEG)
    table_ref[...] = table
    biases = [tail_bias(row_list)] + tile_bias(table, 0, own)
    for copy in copies[4:7]:
        copy.wait()
    for head in range(heads):
        cols = slice(head * WIDTH, (head + 1) * WIDTH)
        for i in range(per_head):
            pair = head * per_head + i
            at = columns(pair, PAIR)
            p, top = tile_weights(dot_nt(k_ref[:, cols], pair_rows(q_ref, pair)), biases)
            p_ref[head, :, columns(i, PAIR)] = p
            stats_ref[0:1, at] = top
            stats_ref[1:2, at] = jnp.sum(p, axis=0, keepdims=True)


def near_value_work(g_ref, v_ref, p_ref, d_ref, stats_ref):
    heads = v_ref.shape[1] // WIDTH
    per_head = g_ref.shape[1] // PAIR // heads
    for head in range(heads):
        cols = slice(head * WIDTH, (head + 1) * WIDTH)
        for i in range(per_head):
            pair = head * per_head + i
            here = columns(i, PAIR)
            d = dot_nt(v_ref[:, cols], pair_rows(g_ref, pair))
            d_ref[head, :, here] = d
            cross = jnp.sum(p_ref[head, :, here] * d, axis=0, keepdims=True)
            stats_ref[2:3, columns(pair, PAIR)] = cross


def near_kernel(ctx, early, *refs):
    ins, rc_ref, rest = refs[:10], refs[10], refs[11 if early else 11 + NEAR_OUTS :]
    q_ref, g_ref, k_ref, v_ref, p_ref, d_ref, stats_ref, table_ref = rest[:NEAR_OUTS]
    small_refs, sems = rest[NEAR_OUTS:-1], rest[-1]
    own = ins[4].shape[0] // TILE

    def key_part():
        copies = load_copies(ins, q_ref, g_ref, k_ref, v_ref, small_refs, sems)
        near_key_work(
            ctx, own, copies, q_ref, k_ref, p_ref, stats_ref, table_ref, *small_refs, rc_ref
        )
        for copy in copies[7:]:
            copy.wait()

    if early:
        pl.when(is_odd())(key_part)
    else:
        pl.when(jnp.logical_not(is_odd()))(key_part)

        @pl.when(jnp.logical_not(value_part_late()))
        def value_part():
            near_value_work(g_ref, v_ref, p_ref, d_ref, stats_ref)


def far_key_kernel(
    unroll, q_ref, g_ref, k_ref, stats_ref, table_ref, back_ref, p_ref, fin_ref, *total_ref
):
    far_tiles = k_ref.shape[0] // TILE
    heads = k_ref.shape[1] // WIDTH
    per_head = q_ref.shape[1] // PAIR // heads
    shifts, own_keys, _ = back_ref.shape
    biases = tile_bias(table_ref[...], own_keys // TILE, far_tiles)
    for head in range(heads):
        cols = slice(head * WIDTH, (head + 1) * WIDTH)

        def step(i):
            pair = head * per_head + i
            at = columns(pair, PAIR)
            here = columns(i, PAIR)
            near_top = stats_ref[0:1, at]
            raw = dot_nt(k_ref[:, cols], pair_rows(q_ref, pair))
            p, top = tile_weights(raw, biases, near_top)
            fade = jnp.exp2(near_top - top)
            inverse = 1.0 / (stats_ref[1:2, at] * fade + jnp.sum(p, axis=0, keepdims=True))
            fin_ref[0:1, at] = fade * inverse
            p = p * inverse
            p_ref[head, :, here] = p.astype(p_ref.dtype)
            return dot_nn(p.astype(BF16), pair_rows(g_ref, pair))

        dv = added(per_head, unroll, step, total_ref).astype(BF16)
        for shift in range(shifts):
            back_ref[shift, :, cols] = dv[shift * own_keys : (shift + 1) * own_keys]


def far_value_kernel(
    unroll, q_ref, g_ref, v_ref, p_ref, fin_ref, near_v_ref, near_p_ref, *refs
):
    d_ref, stats_ref, back_ref, ds_ref, delta_ref, *total_ref = refs[2:]
    heads = v_ref.shape[1] // WIDTH
    per_head = q_ref.shape[1] // PAIR // heads
    shifts, own_keys, _ = back_ref.shape

    @pl.when(value_part_late())
    def value_part():
        near_value_work(g_ref, near_v_ref, near_p_ref, d_ref, stats_ref)

    for head in range(heads):
        cols = slice(head * WIDTH, (head + 1) * WIDTH)

        def step(i):
            pair = head * per_head + i
            at = columns(pair, PAIR)
            here = columns(i, PAIR)
            d = dot_nt(v_ref[:, cols], pair_rows(g_ref, pair))
            p = p_ref[head, :, here].astype(F32)
            delta = stats_ref[2:3, at] * fin_ref[0:1, at] + jnp.sum(p * d, axis=0, keepdims=True)
            delta_ref[0:1, at] = delta
            ds = (p * (d - delta)).astype(BF16)
            ds_ref[head, :, here] = ds
            return dot_nn(ds, pair_rows(q_ref, pair))

        dk = (added(per_head, unroll, step, total_ref) * SCALE).astype(BF16)
        for shift in range(shifts):
            back_ref[shift, :, cols] = dk[shift * own_keys : (shift + 1) * own_keys]


def sum_kernel(after_ref, own_ref, *refs):
    total = own_ref[...]
    for ref in refs[:-1]:
        total = total + ref[...].astype(F32)
    refs[-1][...] = total


def last_kernel(
    unroll, q_ref, g_ref, k_ref, p_ref, d_ref, fin_ref, delta_ref, fk_ref, fds_ref,
    dq_ref, dtk_ref, dtv_ref, dok_ref, dov_ref, low_ref, ds_ref,
):
    tail = dtk_ref.shape[0]
    heads = k_ref.shape[1] // WIDTH
    per_head = q_ref.shape[1] // PAIR // heads
    for head in range(heads):
        cols = slice(head * WIDTH, (head + 1) * WIDTH)

        def step(i):
            pair = head * per_head + i
            at = columns(pair, PAIR)
            here = columns(i, PAIR)
            p = p_ref[head, :, here] * fin_ref[0:1, at]
            ds = (p * (d_ref[head, :, here] - delta_ref[0:1, at])).astype(BF16)
            low_ref[head, :, here] = p.astype(BF16)
            ds_ref[head, :, here] = ds
            dq = dot_tn(k_ref[:, cols], ds) + dot_tn(fk_ref[:, cols], fds_ref[head, :, here])
            dq = dq * SCALE
            dq = jnp.concatenate([dq[:, :WIDTH].T, dq[:, WIDTH:].T], axis=1)
            dq_ref[:, at] = dq.astype(BF16)

        repeat(per_head, unroll, step)
        dk = dot_nn(ds_ref[head], stacked_rows(q_ref, head, 2 * per_head)) * SCALE
        dv = dot_nn(low_ref[head], stacked_rows(g_ref, head, 2 * per_head))
        dtk_ref[:, cols] = dk[:tail].astype(BF16)
        dtv_ref[:, cols] = dv[:tail].astype(BF16)
        dok_ref[:, cols] = dk[tail:]
        dov_ref[:, cols] = dv[tail:]


def call(kernel, spaces, outs, scratch, flops, mib, *args, aliases={}):
    vmem = pl.BlockSpec(memory_space=pltpu.VMEM)
    moved = sum(a.size * a.dtype.itemsize for a in args) + sum(
        math.prod(o.shape) * jnp.dtype(o.dtype).itemsize for o in outs
    )
    return pl.pallas_call(
        kernel,
        out_shape=outs,
        in_specs=[pl.BlockSpec(memory_space=space) for space in spaces],
        out_specs=[vmem] * len(outs),
        scratch_shapes=scratch,
        input_output_aliases=aliases,
        compiler_params=pltpu.CompilerParams(vmem_limit_bytes=mib * 2**20),
        cost_estimate=pl.CostEstimate(flops=flops, bytes_accessed=moved, transcendentals=0),
    )(*args)


def body(q, g, tk, tv, ck, cv, row_list, read_owner, read_tile, read_list, read_count):
    ctx = lax.axis_size("ctx")
    rows, q_width = q.shape
    kv_width = tk.shape[1]
    heads = kv_width // WIDTH
    group_rows = rows * (q_width // kv_width)
    own_keys = ck.shape[0]
    own = own_keys // TILE
    far_keys = (ctx - 1) * own_keys
    near_keys = rows + own_keys
    slots = -(-ctx * own // 8) * 8
    unroll = ctx <= 2
    row_list = row_list.reshape(1, rows)

    def shifted(x, shift):
        return lax.ppermute(x, "ctx", [(o, (o - shift) % ctx) for o in range(ctx)])

    far_k = [shifted(ck, s) for s in range(1, ctx)]
    shape = jax.ShapeDtypeStruct
    product = 2 * q_width * rows * WIDTH
    small = read_owner.shape
    here = [
        pltpu.with_memory_space_constraint(a, pltpu.HBM)
        for a in (q, g, tk, tv, ck, cv, row_list, read_owner, read_tile, read_list)
    ]
    near_outs = [
        pltpu.VMEM(q.shape, BF16),
        pltpu.VMEM(g.shape, BF16),
        pltpu.VMEM((near_keys, kv_width), BF16),
        pltpu.VMEM((near_keys, kv_width), BF16),
        pltpu.VMEM((heads, near_keys, group_rows), F32),
        pltpu.VMEM((heads, near_keys, group_rows), F32),
        pltpu.VMEM((8, heads * group_rows), F32),
        pltpu.VMEM((slots, rows), F32),
    ]
    near = [
        [pltpu.HBM] * len(here) + [pltpu.SMEM],
        near_outs,
        [
            pltpu.VMEM(row_list.shape, jnp.int32),
            pltpu.VMEM(small, jnp.int32),
            pltpu.VMEM(small, jnp.int32),
            pltpu.VMEM(small, jnp.int32),
            pltpu.SemaphoreType.DMA((10,)),
        ],
        2 * product * near_keys // WIDTH,
        32,
        *here, read_count,
    ]
    early = list(call(functools.partial(near_kernel, ctx, True), *near))
    own_v, early[-1] = lax.optimization_barrier((cv, early[-1]))
    far_v = [shifted(own_v, s) for s in range(1, ctx)]
    near[0] = near[0] + [pltpu.VMEM] * NEAR_OUTS
    first = len(here) + 1
    early = [pltpu.with_memory_space_constraint(a, pltpu.VMEM) for a in early]
    q, g, near_k, near_v, near_p, near_d, stats, table = call(
        functools.partial(near_kernel, ctx, False), *near, *early,
        aliases={first + i: i for i in range(NEAR_OUTS)},
    )
    mib = 32 if unroll else 60
    total = [] if unroll else [pltpu.VMEM((far_keys, WIDTH), F32)]
    far_k = far_k[0] if ctx == 2 else jnp.concatenate(far_k, axis=0)
    back_v, far_p, fin = call(
        functools.partial(far_key_kernel, unroll),
        [pltpu.VMEM] * 5,
        [
            shape((ctx - 1, own_keys, kv_width), BF16),
            shape((heads, far_keys, group_rows), F32 if unroll else BF16),
            shape((8, heads * group_rows), F32),
        ],
        total,
        2 * product * far_keys // WIDTH,
        mib,
        q, g, far_k, stats, table,
    )
    returned_v = [shifted(back_v[s - 1], -s) for s in range(1, ctx)]
    far_v = far_v[0] if ctx == 2 else jnp.concatenate(far_v, axis=0)
    near_d, stats = (pltpu.with_memory_space_constraint(a, pltpu.VMEM) for a in (near_d, stats))
    near_d, stats, back_k, far_ds, delta = call(
        functools.partial(far_value_kernel, unroll),
        [pltpu.VMEM] * 9,
        [
            pltpu.VMEM(near_d.shape, F32),
            pltpu.VMEM(stats.shape, F32),
            shape((ctx - 1, own_keys, kv_width), BF16),
            shape((heads, far_keys, group_rows), BF16),
            shape((8, heads * group_rows), F32),
        ],
        total,
        2 * product * far_keys // WIDTH,
        mib,
        q, g, far_v, far_p, fin, near_v, near_p, near_d, stats,
        aliases={7: 0, 8: 1},
    )
    returned_k = [shifted(back_k[s - 1], -s) for s in range(1, ctx)]
    dq, dtk, dtv, dok, dov = call(
        functools.partial(last_kernel, unroll),
        [pltpu.VMEM] * 9,
        [
            shape(q.shape, BF16),
            shape(tk.shape, BF16),
            shape(tv.shape, BF16),
            shape(ck.shape, F32),
            shape(cv.shape, F32),
        ],
        [pltpu.VMEM((heads, near_keys, group_rows), BF16)] * 2,
        product * (3 * near_keys + far_keys) // WIDTH,
        mib,
        q, g, near_k, near_p, near_d, fin, delta, far_k, far_ds,
    )

    def summed(after, own_sum, returned):
        return call(
            sum_kernel,
            [pltpu.HBM] + [pltpu.VMEM] * (1 + len(returned)),
            [shape(own_sum.shape, F32)],
            [],
            0,
            mib,
            pltpu.with_memory_space_constraint(after, pltpu.HBM), own_sum, *returned,
        )[0]

    dov = summed(dq, dov, returned_v)
    dok = summed(dov, dok, returned_k)
    return dq, dtk, dtv, dok, dov


def solution(mesh):
    wide = P(("dp", "ctx"), "tp")
    lone = P(("dp", "ctx"))
    flat = P(("dp", "ctx"), None)
    return jax.shard_map(
        body,
        mesh=mesh,
        in_specs=(wide,) * 6 + (lone, flat, flat, flat, lone),
        out_specs=(wide,) * 5,
        check_vma=False,
    )
```

```python
import functools
import math

import jax
import jax.numpy as jnp
from jax import lax
from jax.experimental import pallas as pl
from jax.experimental.pallas import tpu as pltpu
from jax.sharding import PartitionSpec as P

WIDTH = 128
TILE = 128
PAIR = 2 * WIDTH
NEAR_OUTS = 8
NEG = -1e30
SCALE = 1.0 / math.sqrt(WIDTH)
SCALE2 = SCALE * math.log2(math.e)
F32 = jnp.float32
BF16 = jnp.bfloat16


def dot_nt(a, b):
    return lax.dot_general(a, b, (((1,), (1,)), ((), ())), preferred_element_type=F32)


def dot_nn(a, b):
    return lax.dot_general(a, b, (((1,), (0,)), ((), ())), preferred_element_type=F32)


def dot_tn(a, b):
    return lax.dot_general(a, b, (((0,), (0,)), ((), ())), preferred_element_type=F32)


def repeat(steps, unroll, step):
    if unroll:
        for i in range(steps):
            step(i)
    else:

        def one(i, carry):
            step(i)
            return carry

        lax.fori_loop(0, steps, one, 0)


def added(steps, unroll, step, total_ref):
    if unroll:
        return functools.reduce(jnp.add, [step(i) for i in range(steps)])
    (total_ref,) = total_ref
    total_ref[...] = jnp.zeros_like(total_ref)

    def one(i):
        total_ref[...] += step(i)

    repeat(steps, unroll, one)
    return total_ref[...]


def columns(i, width):
    if isinstance(i, int):
        return pl.ds(i * width, width)
    return pl.ds(pl.multiple_of(i * width, width), width)


def pair_rows(ref, i):
    block = ref[:, columns(i, PAIR)]
    return jnp.concatenate([block[:, :WIDTH], block[:, WIDTH:]], axis=0)


def stacked_rows(ref, head, group):
    first = head * group
    return jnp.concatenate(
        [ref[:, (first + g) * WIDTH : (first + g + 1) * WIDTH] for g in range(group)], axis=0
    )


def twice(row):
    return jnp.concatenate([row, row], axis=1)


def tile_bias(table, first, tiles):
    return [twice(table[first + t : first + t + 1, :]) for t in range(tiles)]


def add_tiles(scores, biases):
    parts = [
        scores[t * TILE : (t + 1) * TILE, :] * SCALE2 + bias for t, bias in enumerate(biases)
    ]
    return parts[0] if len(parts) == 1 else jnp.concatenate(parts, axis=0)


def tail_bias(row_list):
    rows = row_list.shape[1]
    cut = jnp.sum((row_list == 0).astype(jnp.int32), axis=1, keepdims=True)
    key_at = lax.broadcasted_iota(jnp.int32, (rows, rows), 0)
    row_at = lax.broadcasted_iota(jnp.int32, (rows, rows), 1)
    allowed = ((key_at < cut) == (row_at < cut)) & (key_at <= row_at)
    return twice(jnp.where(allowed, 0.0, NEG).astype(F32))


def is_odd():
    return lax.rem(lax.axis_index("dp"), 2) == 1


def value_part_late():
    return jnp.logical_and(jnp.logical_not(is_odd()), lax.axis_index("ctx") > 0)


def load_copies(ins, q_ref, g_ref, k_ref, v_ref, small_refs, sems):
    q_in, g_in, tk_in, tv_in, ok_in, ov_in, *small_ins = ins
    tail = tk_in.shape[0]
    moves = list(zip(small_ins, small_refs)) + [
        (tk_in, k_ref.at[:tail]), (ok_in, k_ref.at[tail:]), (q_in, q_ref),
        (tv_in, v_ref.at[:tail]), (ov_in, v_ref.at[tail:]), (g_in, g_ref),
    ]
    copies = [pltpu.make_async_copy(a, b, sems.at[i]) for i, (a, b) in enumerate(moves)]
    for copy in copies:
        copy.start()
    return copies


def near_key_work(
    ctx, own, copies, q_ref, k_ref, p_ref, stats_ref, table_ref, rl_ref, ro_ref, rt_ref, rs_ref, rc_ref
):
    heads = k_ref.shape[1] // WIDTH
    per_head = q_ref.shape[1] // PAIR // heads
    reads = ro_ref.shape[1]
    slots = table_ref.shape[0]
    for copy in copies[:4]:
        copy.wait()
    row_list = rl_ref[...]
    owner = ro_ref[...] - lax.axis_index("ctx")
    owner = jnp.where(owner < 0, owner + ctx, owner)
    wanted = owner * own + rt_ref[...]
    live = lax.broadcasted_iota(jnp.int32, (1, reads), 1) < rc_ref[0]
    wanted = jnp.where(live, wanted, -1)
    hit = lax.broadcasted_iota(jnp.int32, (slots, reads), 0) == wanted
    first = rs_ref[...] == 0
    count0 = jnp.sum(jnp.where(hit & first, 1.0, 0.0), axis=1, keepdims=True)
    count1 = jnp.sum(jnp.where(hit & jnp.logical_not(first), 1.0, 0.0), axis=1, keepdims=True)
    count = jnp.where(row_list == 0, count0, count1)
    table = jnp.where(count > 0.5, jnp.log2(jnp.maximum(count, 1.0)), NEG)
    table_ref[...] = table
    biases = [tail_bias(row_list)] + tile_bias(table, 0, own)
    for copy in copies[4:7]:
        copy.wait()
    for head in range(heads):
        cols = slice(head * WIDTH, (head + 1) * WIDTH)
        for i in range(per_head):
            pair = head * per_head + i
            at = columns(pair, PAIR)
            s = add_tiles(dot_nt(k_ref[:, cols], pair_rows(q_ref, pair)), biases)
            top = jnp.max(s, axis=0, keepdims=True)
            p = jnp.exp2(s - top)
            p_ref[head, :, columns(i, PAIR)] = p
            stats_ref[0:1, at] = top
            stats_ref[1:2, at] = jnp.sum(p, axis=0, keepdims=True)


def near_value_work(g_ref, v_ref, p_ref, d_ref, stats_ref):
    heads = v_ref.shape[1] // WIDTH
    per_head = g_ref.shape[1] // PAIR // heads
    for head in range(heads):
        cols = slice(head * WIDTH, (head + 1) * WIDTH)
        for i in range(per_head):
            pair = head * per_head + i
            here = columns(i, PAIR)
            d = dot_nt(v_ref[:, cols], pair_rows(g_ref, pair))
            d_ref[head, :, here] = d
            cross = jnp.sum(p_ref[head, :, here] * d, axis=0, keepdims=True)
            stats_ref[2:3, columns(pair, PAIR)] = cross


def near_kernel(ctx, early, *refs):
    ins, rc_ref, rest = refs[:10], refs[10], refs[11 if early else 11 + NEAR_OUTS :]
    q_ref, g_ref, k_ref, v_ref, p_ref, d_ref, stats_ref, table_ref = rest[:NEAR_OUTS]
    small_refs, sems = rest[NEAR_OUTS:-1], rest[-1]
    own = ins[4].shape[0] // TILE

    def key_part():
        copies = load_copies(ins, q_ref, g_ref, k_ref, v_ref, small_refs, sems)
        near_key_work(
            ctx, own, copies, q_ref, k_ref, p_ref, stats_ref, table_ref, *small_refs, rc_ref
        )
        for copy in copies[7:]:
            copy.wait()

    if early:
        pl.when(is_odd())(key_part)
    else:
        pl.when(jnp.logical_not(is_odd()))(key_part)

        @pl.when(jnp.logical_not(value_part_late()))
        def value_part():
            near_value_work(g_ref, v_ref, p_ref, d_ref, stats_ref)


def far_key_kernel(
    unroll, q_ref, g_ref, k_ref, stats_ref, table_ref, back_ref, p_ref, fin_ref, *total_ref
):
    far_tiles = k_ref.shape[0] // TILE
    heads = k_ref.shape[1] // WIDTH
    per_head = q_ref.shape[1] // PAIR // heads
    shifts, own_keys, _ = back_ref.shape
    biases = tile_bias(table_ref[...], own_keys // TILE, far_tiles)
    for head in range(heads):
        cols = slice(head * WIDTH, (head + 1) * WIDTH)

        def step(i):
            pair = head * per_head + i
            at = columns(pair, PAIR)
            here = columns(i, PAIR)
            s = add_tiles(dot_nt(k_ref[:, cols], pair_rows(q_ref, pair)), biases)
            near_top = stats_ref[0:1, at]
            top = jnp.maximum(near_top, jnp.max(s, axis=0, keepdims=True))
            p = jnp.exp2(s - top)
            fade = jnp.exp2(near_top - top)
            inverse = 1.0 / (stats_ref[1:2, at] * fade + jnp.sum(p, axis=0, keepdims=True))
            fin_ref[0:1, at] = fade * inverse
            p = (p * inverse).astype(BF16)
            p_ref[head, :, here] = p
            return dot_nn(p, pair_rows(g_ref, pair))

        dv = added(per_head, unroll, step, total_ref).astype(BF16)
        for shift in range(shifts):
            back_ref[shift, :, cols] = dv[shift * own_keys : (shift + 1) * own_keys]


def far_value_kernel(
    unroll, q_ref, g_ref, v_ref, p_ref, fin_ref, near_v_ref, near_p_ref, *refs
):
    d_ref, stats_ref, back_ref, ds_ref, delta_ref, terms_ref, low_ref, *total_ref = refs[2:]
    heads = v_ref.shape[1] // WIDTH
    per_head = q_ref.shape[1] // PAIR // heads
    shifts, own_keys, _ = back_ref.shape

    @pl.when(value_part_late())
    def value_part():
        near_value_work(g_ref, near_v_ref, near_p_ref, d_ref, stats_ref)

    for head in range(heads):
        cols = slice(head * WIDTH, (head + 1) * WIDTH)

        def step(i):
            pair = head * per_head + i
            at = columns(pair, PAIR)
            here = columns(i, PAIR)
            d = dot_nt(v_ref[:, cols], pair_rows(g_ref, pair))
            p = p_ref[head, :, here].astype(F32)
            delta = stats_ref[2:3, at] * fin_ref[0:1, at] + jnp.sum(p * d, axis=0, keepdims=True)
            delta_ref[0:1, at] = delta
            ds = (p * (d - delta)).astype(BF16)
            ds_ref[head, :, here] = ds
            return dot_nn(ds, pair_rows(q_ref, pair))

        dk = (added(per_head, unroll, step, total_ref) * SCALE).astype(BF16)
        for shift in range(shifts):
            back_ref[shift, :, cols] = dk[shift * own_keys : (shift + 1) * own_keys]

    @pl.when(is_odd())
    def near_terms():
        for head in range(heads):

            def fill(i):
                here = columns(i, PAIR)
                p = near_p_ref[head, :, here] * fin_ref[0:1, columns(head * per_head + i, PAIR)]
                low_ref[head, :, here] = p.astype(BF16)

            repeat(per_head, unroll, fill)
            rows = stacked_rows(g_ref, head, 2 * per_head)
            terms_ref[:, head * WIDTH : (head + 1) * WIDTH] = dot_nn(low_ref[head], rows)


def sum_kernel(after_ref, own_ref, *refs):
    total = own_ref[...]
    for ref in refs[:-1]:
        total = total + ref[...].astype(F32)
    refs[-1][...] = total


def last_kernel(unroll, *refs):
    @pl.when(jnp.logical_not(is_odd()))
    def all_terms():
        last_work(unroll, False, *refs)

    @pl.when(is_odd())
    def other_terms():
        last_work(unroll, True, *refs)


def last_work(
    unroll, made, q_ref, g_ref, k_ref, p_ref, d_ref, fin_ref, delta_ref, fk_ref, fds_ref, terms_ref,
    dq_ref, dtk_ref, dtv_ref, dok_ref, dov_ref, low_ref, ds_ref,
):
    tail = dtk_ref.shape[0]
    heads = k_ref.shape[1] // WIDTH
    per_head = q_ref.shape[1] // PAIR // heads
    for head in range(heads):
        cols = slice(head * WIDTH, (head + 1) * WIDTH)

        def step(i):
            pair = head * per_head + i
            at = columns(pair, PAIR)
            here = columns(i, PAIR)
            p = p_ref[head, :, here] * fin_ref[0:1, at]
            ds = (p * (d_ref[head, :, here] - delta_ref[0:1, at])).astype(BF16)
            if not made:
                low_ref[head, :, here] = p.astype(BF16)
            ds_ref[head, :, here] = ds
            dq = dot_tn(k_ref[:, cols], ds) + dot_tn(fk_ref[:, cols], fds_ref[head, :, here])
            dq = dq * SCALE
            dq = jnp.concatenate([dq[:, :WIDTH].T, dq[:, WIDTH:].T], axis=1)
            dq_ref[:, at] = dq.astype(BF16)

        repeat(per_head, unroll, step)
        dk = dot_nn(ds_ref[head], stacked_rows(q_ref, head, 2 * per_head)) * SCALE
        if made:
            dv = terms_ref[:, cols]
        else:
            dv = dot_nn(low_ref[head], stacked_rows(g_ref, head, 2 * per_head))
        dtk_ref[:, cols] = dk[:tail].astype(BF16)
        dtv_ref[:, cols] = dv[:tail].astype(BF16)
        dok_ref[:, cols] = dk[tail:]
        dov_ref[:, cols] = dv[tail:]


def call(kernel, spaces, outs, scratch, flops, mib, *args, aliases={}):
    vmem = pl.BlockSpec(memory_space=pltpu.VMEM)
    moved = sum(a.size * a.dtype.itemsize for a in args) + sum(
        math.prod(o.shape) * jnp.dtype(o.dtype).itemsize for o in outs
    )
    return pl.pallas_call(
        kernel,
        out_shape=outs,
        in_specs=[pl.BlockSpec(memory_space=space) for space in spaces],
        out_specs=[vmem] * len(outs),
        scratch_shapes=scratch,
        input_output_aliases=aliases,
        compiler_params=pltpu.CompilerParams(vmem_limit_bytes=mib * 2**20),
        cost_estimate=pl.CostEstimate(flops=flops, bytes_accessed=moved, transcendentals=0),
    )(*args)


def body(q, g, tk, tv, ck, cv, row_list, read_owner, read_tile, read_list, read_count):
    ctx = lax.axis_size("ctx")
    rows, q_width = q.shape
    kv_width = tk.shape[1]
    heads = kv_width // WIDTH
    group_rows = rows * (q_width // kv_width)
    own_keys = ck.shape[0]
    own = own_keys // TILE
    far_keys = (ctx - 1) * own_keys
    near_keys = rows + own_keys
    slots = -(-ctx * own // 8) * 8
    unroll = ctx <= 2
    row_list = row_list.reshape(1, rows)

    def shifted(x, shift):
        return lax.ppermute(x, "ctx", [(o, (o - shift) % ctx) for o in range(ctx)])

    far_k = [shifted(ck, s) for s in range(1, ctx)]
    shape = jax.ShapeDtypeStruct
    product = 2 * q_width * rows * WIDTH
    small = read_owner.shape
    here = [
        pltpu.with_memory_space_constraint(a, pltpu.HBM)
        for a in (q, g, tk, tv, ck, cv, row_list, read_owner, read_tile, read_list)
    ]
    near_outs = [
        pltpu.VMEM(q.shape, BF16),
        pltpu.VMEM(g.shape, BF16),
        pltpu.VMEM((near_keys, kv_width), BF16),
        pltpu.VMEM((near_keys, kv_width), BF16),
        pltpu.VMEM((heads, near_keys, group_rows), F32),
        pltpu.VMEM((heads, near_keys, group_rows), F32),
        pltpu.VMEM((8, heads * group_rows), F32),
        pltpu.VMEM((slots, rows), F32),
    ]
    near = [
        [pltpu.HBM] * len(here) + [pltpu.SMEM],
        near_outs,
        [
            pltpu.VMEM(row_list.shape, jnp.int32),
            pltpu.VMEM(small, jnp.int32),
            pltpu.VMEM(small, jnp.int32),
            pltpu.VMEM(small, jnp.int32),
            pltpu.SemaphoreType.DMA((10,)),
        ],
        2 * product * near_keys // WIDTH,
        32,
        *here, read_count,
    ]
    early = list(call(functools.partial(near_kernel, ctx, True), *near))
    own_v, early[-1] = lax.optimization_barrier((cv, early[-1]))
    far_v = [shifted(own_v, s) for s in range(1, ctx)]
    near[0] = near[0] + [pltpu.VMEM] * NEAR_OUTS
    first = len(here) + 1
    early = [pltpu.with_memory_space_constraint(a, pltpu.VMEM) for a in early]
    q, g, near_k, near_v, near_p, near_d, stats, table = call(
        functools.partial(near_kernel, ctx, False), *near, *early,
        aliases={first + i: i for i in range(NEAR_OUTS)},
    )
    mib = 32 if unroll else 60
    total = [] if unroll else [pltpu.VMEM((far_keys, WIDTH), F32)]
    far_k = far_k[0] if ctx == 2 else jnp.concatenate(far_k, axis=0)
    back_v, far_p, fin = call(
        functools.partial(far_key_kernel, unroll),
        [pltpu.VMEM] * 5,
        [
            shape((ctx - 1, own_keys, kv_width), BF16),
            shape((heads, far_keys, group_rows), BF16),
            shape((8, heads * group_rows), F32),
        ],
        total,
        2 * product * far_keys // WIDTH,
        mib,
        q, g, far_k, stats, table,
    )
    returned_v = [shifted(back_v[s - 1], -s) for s in range(1, ctx)]
    far_v = far_v[0] if ctx == 2 else jnp.concatenate(far_v, axis=0)
    near_d, stats = (pltpu.with_memory_space_constraint(a, pltpu.VMEM) for a in (near_d, stats))
    near_d, stats, back_k, far_ds, delta, terms = call(
        functools.partial(far_value_kernel, unroll),
        [pltpu.VMEM] * 9,
        [
            pltpu.VMEM(near_d.shape, F32),
            pltpu.VMEM(stats.shape, F32),
            shape((ctx - 1, own_keys, kv_width), BF16),
            shape((heads, far_keys, group_rows), BF16),
            shape((8, heads * group_rows), F32),
            shape((near_keys, kv_width), F32),
        ],
        [pltpu.VMEM((heads, near_keys, group_rows), BF16)] + total,
        2 * product * far_keys // WIDTH,
        mib,
        q, g, far_v, far_p, fin, near_v, near_p, near_d, stats,
        aliases={7: 0, 8: 1},
    )
    returned_k = [shifted(back_k[s - 1], -s) for s in range(1, ctx)]
    dq, dtk, dtv, dok, dov = call(
        functools.partial(last_kernel, unroll),
        [pltpu.VMEM] * 10,
        [
            shape(q.shape, BF16),
            shape(tk.shape, BF16),
            shape(tv.shape, BF16),
            shape(ck.shape, F32),
            shape(cv.shape, F32),
        ],
        [pltpu.VMEM((heads, near_keys, group_rows), BF16)] * 2,
        product * (3 * near_keys + far_keys) // WIDTH,
        mib,
        q, g, near_k, near_p, near_d, fin, delta, far_k, far_ds, terms,
    )

    def summed(after, own_sum, returned):
        return call(
            sum_kernel,
            [pltpu.HBM] + [pltpu.VMEM] * (1 + len(returned)),
            [shape(own_sum.shape, F32)],
            [],
            0,
            mib,
            pltpu.with_memory_space_constraint(after, pltpu.HBM), own_sum, *returned,
        )[0]

    dov = summed(dq, dov, returned_v)
    dok = summed(dov, dok, returned_k)
    return dq, dtk, dtv, dok, dov


def solution(mesh):
    wide = P(("dp", "ctx"), "tp")
    lone = P(("dp", "ctx"))
    flat = P(("dp", "ctx"), None)
    return jax.shard_map(
        body,
        mesh=mesh,
        in_specs=(wide,) * 6 + (lone, flat, flat, flat, lone),
        out_specs=(wide,) * 5,
        check_vma=False,
    )
```

```python
import functools
import math

import jax
import jax.numpy as jnp
from jax import lax
from jax.experimental import pallas as pl
from jax.experimental.pallas import tpu as pltpu
from jax.sharding import PartitionSpec as P

WIDTH = 128
TILE = 128
PAIR = 2 * WIDTH
SUM_PARTS = 4
NEAR_OUTS = 10
NEG = -1e30
SCALE = 1.0 / math.sqrt(WIDTH)
SCALE2 = SCALE * math.log2(math.e)
F32 = jnp.float32
BF16 = jnp.bfloat16


def dot_nt(a, b):
    return lax.dot_general(a, b, (((1,), (1,)), ((), ())), preferred_element_type=F32)


def dot_nn(a, b):
    return lax.dot_general(a, b, (((1,), (0,)), ((), ())), preferred_element_type=F32)


def dot_tn(a, b):
    return lax.dot_general(a, b, (((0,), (0,)), ((), ())), preferred_element_type=F32)


def repeat(steps, unroll, step):
    if unroll:
        for i in range(steps):
            step(i)
    else:

        def one(i, carry):
            step(i)
            return carry

        lax.fori_loop(0, steps, one, 0)


def added(steps, unroll, step, total_ref):
    if unroll:
        return functools.reduce(jnp.add, [step(i) for i in range(steps)])
    (total_ref,) = total_ref
    total_ref[...] = jnp.zeros_like(total_ref)

    def one(i):
        total_ref[...] += step(i)

    repeat(steps, unroll, one)
    return total_ref[...]


def columns(i, width):
    if isinstance(i, int):
        return pl.ds(i * width, width)
    return pl.ds(pl.multiple_of(i * width, width), width)


def pair_rows(ref, i):
    block = ref[:, columns(i, PAIR)]
    return jnp.concatenate([block[:, :WIDTH], block[:, WIDTH:]], axis=0)


def stacked_rows(ref, head, group):
    first = head * group
    return jnp.concatenate(
        [ref[:, (first + g) * WIDTH : (first + g + 1) * WIDTH] for g in range(group)], axis=0
    )


def twice(row):
    return jnp.concatenate([row, row], axis=1)


def tile_bias(table, first, tiles):
    return [twice(table[first + t : first + t + 1, :]) for t in range(tiles)]


def add_tiles(scores, biases):
    parts = [
        scores[t * TILE : (t + 1) * TILE, :] * SCALE2 + bias for t, bias in enumerate(biases)
    ]
    return parts[0] if len(parts) == 1 else jnp.concatenate(parts, axis=0)


def tail_bias(row_list):
    rows = row_list.shape[1]
    cut = jnp.sum((row_list == 0).astype(jnp.int32), axis=1, keepdims=True)
    key_at = lax.broadcasted_iota(jnp.int32, (rows, rows), 0)
    row_at = lax.broadcasted_iota(jnp.int32, (rows, rows), 1)
    allowed = ((key_at < cut) == (row_at < cut)) & (key_at <= row_at)
    return twice(jnp.where(allowed, 0.0, NEG).astype(F32))


def is_odd():
    return lax.rem(lax.axis_index("dp"), 2) == 1


def value_part_late():
    return jnp.logical_and(jnp.logical_not(is_odd()), lax.axis_index("ctx") > 0)


def load_copies(ins, q_ref, g_ref, k_ref, v_ref, small_refs, sems):
    q_in, g_in, tk_in, tv_in, ok_in, ov_in, *small_ins = ins
    tail = tk_in.shape[0]
    moves = list(zip(small_ins, small_refs)) + [
        (tk_in, k_ref.at[:tail]), (ok_in, k_ref.at[tail:]), (q_in, q_ref),
        (tv_in, v_ref.at[:tail]), (ov_in, v_ref.at[tail:]), (g_in, g_ref),
    ]
    copies = [pltpu.make_async_copy(a, b, sems.at[i]) for i, (a, b) in enumerate(moves)]
    for copy in copies:
        copy.start()
    return copies


def near_key_work(
    ctx, own, copies, q_ref, k_ref, qt_ref, p_ref, stats_ref, table_ref,
    rl_ref, ro_ref, rt_ref, rs_ref, rc_ref,
):
    heads = k_ref.shape[1] // WIDTH
    per_head = q_ref.shape[1] // PAIR // heads
    reads = ro_ref.shape[1]
    slots = table_ref.shape[0]
    for copy in copies[:4]:
        copy.wait()
    row_list = rl_ref[...]
    owner = ro_ref[...] - lax.axis_index("ctx")
    owner = jnp.where(owner < 0, owner + ctx, owner)
    wanted = owner * own + rt_ref[...]
    live = lax.broadcasted_iota(jnp.int32, (1, reads), 1) < rc_ref[0]
    wanted = jnp.where(live, wanted, -1)
    hit = lax.broadcasted_iota(jnp.int32, (slots, reads), 0) == wanted
    first = rs_ref[...] == 0
    count0 = jnp.sum(jnp.where(hit & first, 1.0, 0.0), axis=1, keepdims=True)
    count1 = jnp.sum(jnp.where(hit & jnp.logical_not(first), 1.0, 0.0), axis=1, keepdims=True)
    count = jnp.where(row_list == 0, count0, count1)
    table = jnp.where(count > 0.5, jnp.log2(jnp.maximum(count, 1.0)), NEG)
    table_ref[...] = table
    biases = [tail_bias(row_list)] + tile_bias(table, 0, own)
    for copy in copies[4:7]:
        copy.wait()
    for head in range(heads):
        cols = slice(head * WIDTH, (head + 1) * WIDTH)
        for i in range(per_head):
            pair = head * per_head + i
            at = columns(pair, PAIR)
            qt = pair_rows(q_ref, pair).T
            qt_ref[columns(pair, WIDTH), :] = qt
            s = add_tiles(dot_nn(k_ref[:, cols], qt), biases)
            top = jnp.max(s, axis=0, keepdims=True)
            p = jnp.exp2(s - top)
            p_ref[head, :, columns(i, PAIR)] = p
            stats_ref[0:1, at] = top
            stats_ref[1:2, at] = jnp.sum(p, axis=0, keepdims=True)


def near_value_work(g_ref, v_ref, gt_ref, p_ref, d_ref, stats_ref):
    heads = v_ref.shape[1] // WIDTH
    per_head = g_ref.shape[1] // PAIR // heads
    for head in range(heads):
        cols = slice(head * WIDTH, (head + 1) * WIDTH)
        for i in range(per_head):
            pair = head * per_head + i
            here = columns(i, PAIR)
            gt = pair_rows(g_ref, pair).T
            gt_ref[columns(pair, WIDTH), :] = gt
            d = dot_nn(v_ref[:, cols], gt)
            d_ref[head, :, here] = d
            cross = jnp.sum(p_ref[head, :, here] * d, axis=0, keepdims=True)
            stats_ref[2:3, columns(pair, PAIR)] = cross


def near_kernel(ctx, early, *refs):
    ins, rc_ref, rest = refs[:10], refs[10], refs[11 if early else 11 + NEAR_OUTS :]
    q_ref, g_ref, k_ref, v_ref, qt_ref, gt_ref, p_ref, d_ref, stats_ref, table_ref = rest[:NEAR_OUTS]
    small_refs, sems = rest[NEAR_OUTS:-1], rest[-1]
    own = ins[4].shape[0] // TILE

    def key_part():
        copies = load_copies(ins, q_ref, g_ref, k_ref, v_ref, small_refs, sems)
        near_key_work(
            ctx, own, copies, q_ref, k_ref, qt_ref, p_ref, stats_ref, table_ref, *small_refs, rc_ref
        )
        for copy in copies[7:]:
            copy.wait()

    if early:
        pl.when(is_odd())(key_part)
    else:
        pl.when(jnp.logical_not(is_odd()))(key_part)

        @pl.when(jnp.logical_not(value_part_late()))
        def value_part():
            near_value_work(g_ref, v_ref, gt_ref, p_ref, d_ref, stats_ref)


def far_key_kernel(
    unroll, qt_ref, g_ref, k_ref, stats_ref, table_ref, back_ref, p_ref, fin_ref, *total_ref
):
    far_tiles = k_ref.shape[0] // TILE
    heads = k_ref.shape[1] // WIDTH
    per_head = g_ref.shape[1] // PAIR // heads
    shifts, own_keys, _ = back_ref.shape
    biases = tile_bias(table_ref[...], own_keys // TILE, far_tiles)
    for head in range(heads):
        cols = slice(head * WIDTH, (head + 1) * WIDTH)

        def step(i):
            pair = head * per_head + i
            at = columns(pair, PAIR)
            here = columns(i, PAIR)
            s = add_tiles(dot_nn(k_ref[:, cols], qt_ref[columns(pair, WIDTH), :]), biases)
            near_top = stats_ref[0:1, at]
            top = jnp.maximum(near_top, jnp.max(s, axis=0, keepdims=True))
            p = jnp.exp2(s - top)
            fade = jnp.exp2(near_top - top)
            inverse = 1.0 / (stats_ref[1:2, at] * fade + jnp.sum(p, axis=0, keepdims=True))
            fin_ref[0:1, at] = fade * inverse
            p = (p * inverse).astype(BF16)
            p_ref[head, :, here] = p
            return dot_nn(p, pair_rows(g_ref, pair))

        dv = added(per_head, unroll, step, total_ref).astype(BF16)
        for shift in range(shifts):
            back_ref[shift, :, cols] = dv[shift * own_keys : (shift + 1) * own_keys]


def far_value_kernel(
    unroll, q_ref, g_ref, v_ref, p_ref, fin_ref, near_v_ref, near_p_ref, *refs
):
    gt_ref, d_ref, stats_ref, back_ref, ds_ref, delta_ref, *total_ref = refs[3:]
    heads = v_ref.shape[1] // WIDTH
    per_head = q_ref.shape[1] // PAIR // heads
    shifts, own_keys, _ = back_ref.shape

    @pl.when(value_part_late())
    def value_part():
        near_value_work(g_ref, near_v_ref, gt_ref, near_p_ref, d_ref, stats_ref)

    for head in range(heads):
        cols = slice(head * WIDTH, (head + 1) * WIDTH)

        def step(i):
            pair = head * per_head + i
            at = columns(pair, PAIR)
            here = columns(i, PAIR)
            d = dot_nn(v_ref[:, cols], gt_ref[columns(pair, WIDTH), :])
            p = p_ref[head, :, here].astype(F32)
            delta = stats_ref[2:3, at] * fin_ref[0:1, at] + jnp.sum(p * d, axis=0, keepdims=True)
            delta_ref[0:1, at] = delta
            ds = (p * (d - delta)).astype(BF16)
            ds_ref[head, :, here] = ds
            return dot_nn(ds, pair_rows(q_ref, pair))

        dk = (added(per_head, unroll, step, total_ref) * SCALE).astype(BF16)
        for shift in range(shifts):
            back_ref[shift, :, cols] = dk[shift * own_keys : (shift + 1) * own_keys]


def sum_kernel(after_ref, own_ref, *refs):
    *terms, out_ref, total_ref, sems = refs
    keys = own_ref.shape[0] // SUM_PARTS
    copies = []
    for part in range(SUM_PARTS):
        rows = slice(part * keys, (part + 1) * keys)
        total = own_ref[rows, :]
        for ref in terms:
            total = total + ref[rows, :].astype(F32)
        total_ref[rows, :] = total
        copies.append(
            pltpu.make_async_copy(total_ref.at[rows], out_ref.at[rows], sems.at[part])
        )
        copies[-1].start()
    for copy in copies:
        copy.wait()


def last_kernel(
    unroll, q_ref, g_ref, k_ref, p_ref, d_ref, fin_ref, delta_ref, fk_ref, fds_ref,
    dq_ref, dtk_ref, dtv_ref, dok_ref, dov_ref, low_ref, ds_ref,
):
    tail = dtk_ref.shape[0]
    heads = k_ref.shape[1] // WIDTH
    per_head = q_ref.shape[1] // PAIR // heads
    for head in range(heads):
        cols = slice(head * WIDTH, (head + 1) * WIDTH)

        def step(i):
            pair = head * per_head + i
            at = columns(pair, PAIR)
            here = columns(i, PAIR)
            p = p_ref[head, :, here] * fin_ref[0:1, at]
            ds = (p * (d_ref[head, :, here] - delta_ref[0:1, at])).astype(BF16)
            low_ref[head, :, here] = p.astype(BF16)
            ds_ref[head, :, here] = ds
            dq = dot_tn(k_ref[:, cols], ds) + dot_tn(fk_ref[:, cols], fds_ref[head, :, here])
            dq = dq * SCALE
            dq = jnp.concatenate([dq[:, :WIDTH].T, dq[:, WIDTH:].T], axis=1)
            dq_ref[:, at] = dq.astype(BF16)

        repeat(per_head, unroll, step)
        dk = dot_nn(ds_ref[head], stacked_rows(q_ref, head, 2 * per_head)) * SCALE
        dv = dot_nn(low_ref[head], stacked_rows(g_ref, head, 2 * per_head))
        dtk_ref[:, cols] = dk[:tail].astype(BF16)
        dtv_ref[:, cols] = dv[:tail].astype(BF16)
        dok_ref[:, cols] = dk[tail:]
        dov_ref[:, cols] = dv[tail:]


def call(kernel, spaces, outs, scratch, flops, mib, *args, aliases={}, out=pltpu.VMEM):
    moved = sum(a.size * a.dtype.itemsize for a in args) + sum(
        math.prod(o.shape) * jnp.dtype(o.dtype).itemsize for o in outs
    )
    return pl.pallas_call(
        kernel,
        out_shape=outs,
        in_specs=[pl.BlockSpec(memory_space=space) for space in spaces],
        out_specs=[pl.BlockSpec(memory_space=out)] * len(outs),
        scratch_shapes=scratch,
        input_output_aliases=aliases,
        compiler_params=pltpu.CompilerParams(vmem_limit_bytes=mib * 2**20),
        cost_estimate=pl.CostEstimate(flops=flops, bytes_accessed=moved, transcendentals=0),
    )(*args)


def body(q, g, tk, tv, ck, cv, row_list, read_owner, read_tile, read_list, read_count):
    ctx = lax.axis_size("ctx")
    rows, q_width = q.shape
    kv_width = tk.shape[1]
    heads = kv_width // WIDTH
    group_rows = rows * (q_width // kv_width)
    own_keys = ck.shape[0]
    own = own_keys // TILE
    far_keys = (ctx - 1) * own_keys
    near_keys = rows + own_keys
    slots = -(-ctx * own // 8) * 8
    unroll = ctx <= 2
    row_list = row_list.reshape(1, rows)

    def shifted(x, shift):
        return lax.ppermute(x, "ctx", [(o, (o - shift) % ctx) for o in range(ctx)])

    far_k = [shifted(ck, s) for s in range(1, ctx)]
    shape = jax.ShapeDtypeStruct
    product = 2 * q_width * rows * WIDTH
    small = read_owner.shape
    here = [
        pltpu.with_memory_space_constraint(a, pltpu.HBM)
        for a in (q, g, tk, tv, ck, cv, row_list, read_owner, read_tile, read_list)
    ]
    near_outs = [
        pltpu.VMEM(q.shape, BF16),
        pltpu.VMEM(g.shape, BF16),
        pltpu.VMEM((near_keys, kv_width), BF16),
        pltpu.VMEM((near_keys, kv_width), BF16),
        pltpu.VMEM((q_width // 2, PAIR), BF16),
        pltpu.VMEM((q_width // 2, PAIR), BF16),
        pltpu.VMEM((heads, near_keys, group_rows), F32),
        pltpu.VMEM((heads, near_keys, group_rows), F32),
        pltpu.VMEM((8, heads * group_rows), F32),
        pltpu.VMEM((slots, rows), F32),
    ]
    near = [
        [pltpu.HBM] * len(here) + [pltpu.SMEM],
        near_outs,
        [
            pltpu.VMEM(row_list.shape, jnp.int32),
            pltpu.VMEM(small, jnp.int32),
            pltpu.VMEM(small, jnp.int32),
            pltpu.VMEM(small, jnp.int32),
            pltpu.SemaphoreType.DMA((10,)),
        ],
        2 * product * near_keys // WIDTH,
        32,
        *here, read_count,
    ]
    early = list(call(functools.partial(near_kernel, ctx, True), *near))
    own_v, early[-1] = lax.optimization_barrier((cv, early[-1]))
    far_v = [shifted(own_v, s) for s in range(1, ctx)]
    near[0] = near[0] + [pltpu.VMEM] * NEAR_OUTS
    first = len(here) + 1
    early = [pltpu.with_memory_space_constraint(a, pltpu.VMEM) for a in early]
    q, g, near_k, near_v, qt, gt, near_p, near_d, stats, table = call(
        functools.partial(near_kernel, ctx, False), *near, *early,
        aliases={first + i: i for i in range(NEAR_OUTS)},
    )
    mib = 32 if unroll else 60
    total = [] if unroll else [pltpu.VMEM((far_keys, WIDTH), F32)]
    far_k = far_k[0] if ctx == 2 else jnp.concatenate(far_k, axis=0)
    back_v, far_p, fin = call(
        functools.partial(far_key_kernel, unroll),
        [pltpu.VMEM] * 5,
        [
            shape((ctx - 1, own_keys, kv_width), BF16),
            shape((heads, far_keys, group_rows), BF16),
            shape((8, heads * group_rows), F32),
        ],
        total,
        2 * product * far_keys // WIDTH,
        mib,
        qt, g, far_k, stats, table,
    )
    returned_v = [shifted(back_v[s - 1], -s) for s in range(1, ctx)]
    far_v = far_v[0] if ctx == 2 else jnp.concatenate(far_v, axis=0)
    gt, near_d, stats = (
        pltpu.with_memory_space_constraint(a, pltpu.VMEM) for a in (gt, near_d, stats)
    )
    _, near_d, stats, back_k, far_ds, delta = call(
        functools.partial(far_value_kernel, unroll),
        [pltpu.VMEM] * 10,
        [
            pltpu.VMEM(gt.shape, BF16),
            pltpu.VMEM(near_d.shape, F32),
            pltpu.VMEM(stats.shape, F32),
            shape((ctx - 1, own_keys, kv_width), BF16),
            shape((heads, far_keys, group_rows), BF16),
            shape((8, heads * group_rows), F32),
        ],
        total,
        2 * product * far_keys // WIDTH,
        mib,
        q, g, far_v, far_p, fin, near_v, near_p, gt, near_d, stats,
        aliases={7: 0, 8: 1, 9: 2},
    )
    returned_k = [shifted(back_k[s - 1], -s) for s in range(1, ctx)]
    dq, dtk, dtv, dok, dov = call(
        functools.partial(last_kernel, unroll),
        [pltpu.VMEM] * 9,
        [
            shape(q.shape, BF16),
            shape(tk.shape, BF16),
            shape(tv.shape, BF16),
            shape(ck.shape, F32),
            shape(cv.shape, F32),
        ],
        [pltpu.VMEM((heads, near_keys, group_rows), BF16)] * 2,
        product * (3 * near_keys + far_keys) // WIDTH,
        mib,
        q, g, near_k, near_p, near_d, fin, delta, far_k, far_ds,
    )

    def summed(after, own_sum, returned):
        return call(
            sum_kernel,
            [pltpu.HBM] + [pltpu.VMEM] * (1 + len(returned)),
            [pltpu.HBM(own_sum.shape, F32)],
            [pltpu.VMEM(own_sum.shape, F32), pltpu.SemaphoreType.DMA((SUM_PARTS,))],
            0,
            mib,
            pltpu.with_memory_space_constraint(after, pltpu.HBM), own_sum, *returned,
            out=pltpu.HBM,
        )[0]

    dov = summed(dq, dov, returned_v)
    dok = summed(dov, dok, returned_k)
    return dq, dtk, dtv, dok, dov


def solution(mesh):
    wide = P(("dp", "ctx"), "tp")
    lone = P(("dp", "ctx"))
    flat = P(("dp", "ctx"), None)
    return jax.shard_map(
        body,
        mesh=mesh,
        in_specs=(wide,) * 6 + (lone, flat, flat, flat, lone),
        out_specs=(wide,) * 5,
        check_vma=False,
    )
```

```python
import functools
import math

import jax
import jax.numpy as jnp
from jax import lax
from jax.experimental import pallas as pl
from jax.experimental.pallas import tpu as pltpu
from jax.sharding import PartitionSpec as P

WIDTH = 128
TILE = 128
PAIR = 2 * WIDTH
NEAR_OUTS = 12
NEG = -1e30
SCALE = 1.0 / math.sqrt(WIDTH)
SCALE2 = SCALE * math.log2(math.e)
F32 = jnp.float32
BF16 = jnp.bfloat16


def dot_nt(a, b):
    return lax.dot_general(a, b, (((1,), (1,)), ((), ())), preferred_element_type=F32)


def dot_nn(a, b):
    return lax.dot_general(a, b, (((1,), (0,)), ((), ())), preferred_element_type=F32)


def dot_tn(a, b):
    return lax.dot_general(a, b, (((0,), (0,)), ((), ())), preferred_element_type=F32)


def repeat(steps, unroll, step):
    if unroll:
        for i in range(steps):
            step(i)
    else:

        def one(i, carry):
            step(i)
            return carry

        lax.fori_loop(0, steps, one, 0)


def added(steps, unroll, step, total_ref):
    if unroll:
        return functools.reduce(jnp.add, [step(i) for i in range(steps)])
    (total_ref,) = total_ref
    total_ref[...] = jnp.zeros_like(total_ref)

    def one(i):
        total_ref[...] += step(i)

    repeat(steps, unroll, one)
    return total_ref[...]


def columns(i, width):
    if isinstance(i, int):
        return pl.ds(i * width, width)
    return pl.ds(pl.multiple_of(i * width, width), width)


def pair_rows(ref, i):
    block = ref[:, columns(i, PAIR)]
    return jnp.concatenate([block[:, :WIDTH], block[:, WIDTH:]], axis=0)


def stacked_rows(ref, head, group):
    first = head * group
    return jnp.concatenate(
        [ref[:, (first + g) * WIDTH : (first + g + 1) * WIDTH] for g in range(group)], axis=0
    )


def twice(row):
    return jnp.concatenate([row, row], axis=1)


def tile_bias(table, first, tiles):
    return [twice(table[first + t : first + t + 1, :]) for t in range(tiles)]


def add_tiles(scores, biases):
    parts = [
        scores[t * TILE : (t + 1) * TILE, :] * SCALE2 + bias for t, bias in enumerate(biases)
    ]
    return parts[0] if len(parts) == 1 else jnp.concatenate(parts, axis=0)


def tail_bias(row_list):
    rows = row_list.shape[1]
    cut = jnp.sum((row_list == 0).astype(jnp.int32), axis=1, keepdims=True)
    key_at = lax.broadcasted_iota(jnp.int32, (rows, rows), 0)
    row_at = lax.broadcasted_iota(jnp.int32, (rows, rows), 1)
    allowed = ((key_at < cut) == (row_at < cut)) & (key_at <= row_at)
    return twice(jnp.where(allowed, 0.0, NEG).astype(F32))


def is_odd():
    return lax.rem(lax.axis_index("dp"), 2) == 1


def value_part_late():
    return jnp.logical_and(jnp.logical_not(is_odd()), lax.axis_index("ctx") > 0)


def load_copies(ins, q_ref, g_ref, k_ref, v_ref, small_refs, sems):
    q_in, g_in, tk_in, tv_in, ok_in, ov_in, *small_ins = ins
    tail = tk_in.shape[0]
    moves = list(zip(small_ins, small_refs)) + [
        (tk_in, k_ref.at[:tail]), (ok_in, k_ref.at[tail:]), (q_in, q_ref),
        (tv_in, v_ref.at[:tail]), (ov_in, v_ref.at[tail:]), (g_in, g_ref),
    ]
    copies = [pltpu.make_async_copy(a, b, sems.at[i]) for i, (a, b) in enumerate(moves)]
    for copy in copies:
        copy.start()
    return copies


def raw_scores(q_ref, k_ref, head, i, per_head):
    cols = slice(head * WIDTH, (head + 1) * WIDTH)
    return dot_nt(k_ref[:, cols], pair_rows(q_ref, head * per_head + i))


def near_raw_work(q_ref, k_ref, p_ref):
    heads = k_ref.shape[1] // WIDTH
    per_head = q_ref.shape[1] // PAIR // heads
    for head in range(heads):
        for i in range(per_head):
            p_ref[head, :, columns(i, PAIR)] = raw_scores(q_ref, k_ref, head, i, per_head)


def near_key_work(
    ctx, own, raw_made, q_ref, k_ref, p_ref, stats_ref, table_ref,
    rl_ref, ro_ref, rt_ref, rs_ref, rc_ref,
):
    heads = k_ref.shape[1] // WIDTH
    per_head = q_ref.shape[1] // PAIR // heads
    reads = ro_ref.shape[1]
    slots = table_ref.shape[0]
    row_list = rl_ref[...]
    owner = ro_ref[...] - lax.axis_index("ctx")
    owner = jnp.where(owner < 0, owner + ctx, owner)
    wanted = owner * own + rt_ref[...]
    live = lax.broadcasted_iota(jnp.int32, (1, reads), 1) < rc_ref[0]
    wanted = jnp.where(live, wanted, -1)
    hit = lax.broadcasted_iota(jnp.int32, (slots, reads), 0) == wanted
    first = rs_ref[...] == 0
    count0 = jnp.sum(jnp.where(hit & first, 1.0, 0.0), axis=1, keepdims=True)
    count1 = jnp.sum(jnp.where(hit & jnp.logical_not(first), 1.0, 0.0), axis=1, keepdims=True)
    count = jnp.where(row_list == 0, count0, count1)
    table = jnp.where(count > 0.5, jnp.log2(jnp.maximum(count, 1.0)), NEG)
    table_ref[...] = table
    biases = [tail_bias(row_list)] + tile_bias(table, 0, own)
    for head in range(heads):
        for i in range(per_head):
            at = columns(head * per_head + i, PAIR)
            here = columns(i, PAIR)
            if raw_made:
                raw = p_ref[head, :, here]
            else:
                raw = raw_scores(q_ref, k_ref, head, i, per_head)
            s = add_tiles(raw, biases)
            top = jnp.max(s, axis=0, keepdims=True)
            p = jnp.exp2(s - top)
            p_ref[head, :, here] = p
            stats_ref[0:1, at] = top
            stats_ref[1:2, at] = jnp.sum(p, axis=0, keepdims=True)


def near_dprob_work(g_ref, v_ref, d_ref):
    heads = v_ref.shape[1] // WIDTH
    per_head = g_ref.shape[1] // PAIR // heads
    for head in range(heads):
        for i in range(per_head):
            d_ref[head, :, columns(i, PAIR)] = raw_scores(g_ref, v_ref, head, i, per_head)


def near_cross_work(p_ref, d_ref, stats_ref):
    heads, _, group_rows = p_ref.shape
    for head in range(heads):
        for i in range(group_rows // PAIR):
            here = columns(i, PAIR)
            cross = jnp.sum(p_ref[head, :, here] * d_ref[head, :, here], axis=0, keepdims=True)
            stats_ref[2:3, columns(head * group_rows // PAIR + i, PAIR)] = cross


def near_value_work(g_ref, v_ref, p_ref, d_ref, stats_ref):
    heads = v_ref.shape[1] // WIDTH
    per_head = g_ref.shape[1] // PAIR // heads
    for head in range(heads):
        cols = slice(head * WIDTH, (head + 1) * WIDTH)
        for i in range(per_head):
            pair = head * per_head + i
            here = columns(i, PAIR)
            d = dot_nt(v_ref[:, cols], pair_rows(g_ref, pair))
            d_ref[head, :, here] = d
            cross = jnp.sum(p_ref[head, :, here] * d, axis=0, keepdims=True)
            stats_ref[2:3, columns(pair, PAIR)] = cross


def near_kernel(ctx, early, *refs):
    ins, rest = refs[:10], refs[10 if early else 11 + NEAR_OUTS :]
    q_ref, g_ref, k_ref, v_ref, *small_refs = rest[:8]
    p_ref, d_ref, stats_ref, table_ref, sems = rest[8:]

    def load():
        copies = load_copies(ins, q_ref, g_ref, k_ref, v_ref, small_refs, sems)
        for copy in copies:
            copy.wait()

    if early:

        @pl.when(is_odd())
        def first_part():
            load()
            near_raw_work(q_ref, k_ref, p_ref)
            near_dprob_work(g_ref, v_ref, d_ref)

        return
    own = ins[4].shape[0] // TILE
    refs_of_keys = (q_ref, k_ref, p_ref, stats_ref, table_ref, *small_refs, refs[10])

    @pl.when(is_odd())
    def rest_of_it():
        near_key_work(ctx, own, True, *refs_of_keys)
        near_cross_work(p_ref, d_ref, stats_ref)

    @pl.when(jnp.logical_not(is_odd()))
    def key_part():
        load()
        near_key_work(ctx, own, False, *refs_of_keys)

    @pl.when(jnp.logical_not(jnp.logical_or(is_odd(), value_part_late())))
    def value_part():
        near_value_work(g_ref, v_ref, p_ref, d_ref, stats_ref)


def far_key_kernel(
    unroll, q_ref, g_ref, k_ref, stats_ref, table_ref, back_ref, p_ref, fin_ref, *total_ref
):
    far_tiles = k_ref.shape[0] // TILE
    heads = k_ref.shape[1] // WIDTH
    per_head = q_ref.shape[1] // PAIR // heads
    shifts, own_keys, _ = back_ref.shape
    biases = tile_bias(table_ref[...], own_keys // TILE, far_tiles)
    for head in range(heads):
        cols = slice(head * WIDTH, (head + 1) * WIDTH)

        def step(i):
            pair = head * per_head + i
            at = columns(pair, PAIR)
            here = columns(i, PAIR)
            s = add_tiles(dot_nt(k_ref[:, cols], pair_rows(q_ref, pair)), biases)
            near_top = stats_ref[0:1, at]
            top = jnp.maximum(near_top, jnp.max(s, axis=0, keepdims=True))
            p = jnp.exp2(s - top)
            fade = jnp.exp2(near_top - top)
            inverse = 1.0 / (stats_ref[1:2, at] * fade + jnp.sum(p, axis=0, keepdims=True))
            fin_ref[0:1, at] = fade * inverse
            p = (p * inverse).astype(BF16)
            p_ref[head, :, here] = p
            return dot_nn(p, pair_rows(g_ref, pair))

        dv = added(per_head, unroll, step, total_ref).astype(BF16)
        for shift in range(shifts):
            back_ref[shift, :, cols] = dv[shift * own_keys : (shift + 1) * own_keys]


def far_value_kernel(
    unroll, q_ref, g_ref, v_ref, p_ref, fin_ref, near_v_ref, near_p_ref, *refs
):
    d_ref, stats_ref, back_ref, ds_ref, delta_ref, *total_ref = refs[2:]
    heads = v_ref.shape[1] // WIDTH
    per_head = q_ref.shape[1] // PAIR // heads
    shifts, own_keys, _ = back_ref.shape

    @pl.when(value_part_late())
    def value_part():
        near_value_work(g_ref, near_v_ref, near_p_ref, d_ref, stats_ref)

    for head in range(heads):
        cols = slice(head * WIDTH, (head + 1) * WIDTH)

        def step(i):
            pair = head * per_head + i
            at = columns(pair, PAIR)
            here = columns(i, PAIR)
            d = dot_nt(v_ref[:, cols], pair_rows(g_ref, pair))
            p = p_ref[head, :, here].astype(F32)
            delta = stats_ref[2:3, at] * fin_ref[0:1, at] + jnp.sum(p * d, axis=0, keepdims=True)
            delta_ref[0:1, at] = delta
            ds = (p * (d - delta)).astype(BF16)
            ds_ref[head, :, here] = ds
            return dot_nn(ds, pair_rows(q_ref, pair))

        dk = (added(per_head, unroll, step, total_ref) * SCALE).astype(BF16)
        for shift in range(shifts):
            back_ref[shift, :, cols] = dk[shift * own_keys : (shift + 1) * own_keys]


def sum_kernel(after_ref, own_ref, *refs):
    total = own_ref[...]
    for ref in refs[:-1]:
        total = total + ref[...].astype(F32)
    refs[-1][...] = total


def last_kernel(
    unroll, q_ref, g_ref, k_ref, p_ref, d_ref, fin_ref, delta_ref, fk_ref, fds_ref,
    dq_ref, dtk_ref, dtv_ref, dok_ref, dov_ref, low_ref, ds_ref,
):
    tail = dtk_ref.shape[0]
    heads = k_ref.shape[1] // WIDTH
    per_head = q_ref.shape[1] // PAIR // heads
    for head in range(heads):
        cols = slice(head * WIDTH, (head + 1) * WIDTH)

        def step(i):
            pair = head * per_head + i
            at = columns(pair, PAIR)
            here = columns(i, PAIR)
            p = p_ref[head, :, here] * fin_ref[0:1, at]
            ds = (p * (d_ref[head, :, here] - delta_ref[0:1, at])).astype(BF16)
            low_ref[head, :, here] = p.astype(BF16)
            ds_ref[head, :, here] = ds
            dq = dot_tn(k_ref[:, cols], ds) + dot_tn(fk_ref[:, cols], fds_ref[head, :, here])
            dq = dq * SCALE
            dq = jnp.concatenate([dq[:, :WIDTH].T, dq[:, WIDTH:].T], axis=1)
            dq_ref[:, at] = dq.astype(BF16)

        repeat(per_head, unroll, step)
        dk = dot_nn(ds_ref[head], stacked_rows(q_ref, head, 2 * per_head)) * SCALE
        dv = dot_nn(low_ref[head], stacked_rows(g_ref, head, 2 * per_head))
        dtk_ref[:, cols] = dk[:tail].astype(BF16)
        dtv_ref[:, cols] = dv[:tail].astype(BF16)
        dok_ref[:, cols] = dk[tail:]
        dov_ref[:, cols] = dv[tail:]


def call(kernel, spaces, outs, scratch, flops, mib, *args, aliases={}):
    vmem = pl.BlockSpec(memory_space=pltpu.VMEM)
    moved = sum(a.size * a.dtype.itemsize for a in args) + sum(
        math.prod(o.shape) * jnp.dtype(o.dtype).itemsize for o in outs
    )
    return pl.pallas_call(
        kernel,
        out_shape=outs,
        in_specs=[pl.BlockSpec(memory_space=space) for space in spaces],
        out_specs=[vmem] * len(outs),
        scratch_shapes=scratch,
        input_output_aliases=aliases,
        compiler_params=pltpu.CompilerParams(vmem_limit_bytes=mib * 2**20),
        cost_estimate=pl.CostEstimate(flops=flops, bytes_accessed=moved, transcendentals=0),
    )(*args)


def body(q, g, tk, tv, ck, cv, row_list, read_owner, read_tile, read_list, read_count):
    ctx = lax.axis_size("ctx")
    rows, q_width = q.shape
    kv_width = tk.shape[1]
    heads = kv_width // WIDTH
    group_rows = rows * (q_width // kv_width)
    own_keys = ck.shape[0]
    own = own_keys // TILE
    far_keys = (ctx - 1) * own_keys
    near_keys = rows + own_keys
    slots = -(-ctx * own // 8) * 8
    unroll = ctx <= 2
    row_list = row_list.reshape(1, rows)

    def shifted(x, shift):
        return lax.ppermute(x, "ctx", [(o, (o - shift) % ctx) for o in range(ctx)])

    far_k = [shifted(ck, s) for s in range(1, ctx)]
    shape = jax.ShapeDtypeStruct
    product = 2 * q_width * rows * WIDTH
    small = read_owner.shape
    here = [
        pltpu.with_memory_space_constraint(a, pltpu.HBM)
        for a in (q, g, tk, tv, ck, cv, row_list, read_owner, read_tile, read_list)
    ]
    near_outs = [
        pltpu.VMEM(q.shape, BF16),
        pltpu.VMEM(g.shape, BF16),
        pltpu.VMEM((near_keys, kv_width), BF16),
        pltpu.VMEM((near_keys, kv_width), BF16),
        pltpu.VMEM(row_list.shape, jnp.int32),
        pltpu.VMEM(small, jnp.int32),
        pltpu.VMEM(small, jnp.int32),
        pltpu.VMEM(small, jnp.int32),
        pltpu.VMEM((heads, near_keys, group_rows), F32),
        pltpu.VMEM((heads, near_keys, group_rows), F32),
        pltpu.VMEM((8, heads * group_rows), F32),
        pltpu.VMEM((slots, rows), F32),
    ]
    sems = [pltpu.SemaphoreType.DMA((10,))]
    flops = product * near_keys // WIDTH
    hbm = [pltpu.HBM] * len(here)
    early = list(
        call(functools.partial(near_kernel, ctx, True), hbm, near_outs, sems, flops, 32, *here)
    )
    own_v, early[-1] = lax.optimization_barrier((cv, early[-1]))
    far_v = [shifted(own_v, s) for s in range(1, ctx)]
    early = [pltpu.with_memory_space_constraint(a, pltpu.VMEM) for a in early]
    q, g, near_k, near_v, _, _, _, _, near_p, near_d, stats, table = call(
        functools.partial(near_kernel, ctx, False),
        hbm + [pltpu.SMEM] + [pltpu.VMEM] * NEAR_OUTS,
        near_outs,
        sems,
        flops,
        32,
        *here, read_count, *early,
        aliases={len(here) + 1 + i: i for i in range(NEAR_OUTS)},
    )
    mib = 32 if unroll else 60
    total = [] if unroll else [pltpu.VMEM((far_keys, WIDTH), F32)]
    far_k = far_k[0] if ctx == 2 else jnp.concatenate(far_k, axis=0)
    back_v, far_p, fin = call(
        functools.partial(far_key_kernel, unroll),
        [pltpu.VMEM] * 5,
        [
            shape((ctx - 1, own_keys, kv_width), BF16),
            shape((heads, far_keys, group_rows), BF16),
            shape((8, heads * group_rows), F32),
        ],
        total,
        2 * product * far_keys // WIDTH,
        mib,
        q, g, far_k, stats, table,
    )
    returned_v = [shifted(back_v[s - 1], -s) for s in range(1, ctx)]
    far_v = far_v[0] if ctx == 2 else jnp.concatenate(far_v, axis=0)
    near_d, stats = (pltpu.with_memory_space_constraint(a, pltpu.VMEM) for a in (near_d, stats))
    near_d, stats, back_k, far_ds, delta = call(
        functools.partial(far_value_kernel, unroll),
        [pltpu.VMEM] * 9,
        [
            pltpu.VMEM(near_d.shape, F32),
            pltpu.VMEM(stats.shape, F32),
            shape((ctx - 1, own_keys, kv_width), BF16),
            shape((heads, far_keys, group_rows), BF16),
            shape((8, heads * group_rows), F32),
        ],
        total,
        2 * product * far_keys // WIDTH,
        mib,
        q, g, far_v, far_p, fin, near_v, near_p, near_d, stats,
        aliases={7: 0, 8: 1},
    )
    returned_k = [shifted(back_k[s - 1], -s) for s in range(1, ctx)]
    dq, dtk, dtv, dok, dov = call(
        functools.partial(last_kernel, unroll),
        [pltpu.VMEM] * 9,
        [
            shape(q.shape, BF16),
            shape(tk.shape, BF16),
            shape(tv.shape, BF16),
            shape(ck.shape, F32),
            shape(cv.shape, F32),
        ],
        [pltpu.VMEM((heads, near_keys, group_rows), BF16)] * 2,
        product * (3 * near_keys + far_keys) // WIDTH,
        mib,
        q, g, near_k, near_p, near_d, fin, delta, far_k, far_ds,
    )

    def summed(after, own_sum, returned):
        return call(
            sum_kernel,
            [pltpu.HBM] + [pltpu.VMEM] * (1 + len(returned)),
            [shape(own_sum.shape, F32)],
            [],
            0,
            mib,
            pltpu.with_memory_space_constraint(after, pltpu.HBM), own_sum, *returned,
        )[0]

    dov = summed(dq, dov, returned_v)
    dok = summed(dov, dok, returned_k)
    return dq, dtk, dtv, dok, dov


def solution(mesh):
    wide = P(("dp", "ctx"), "tp")
    lone = P(("dp", "ctx"))
    flat = P(("dp", "ctx"), None)
    return jax.shard_map(
        body,
        mesh=mesh,
        in_specs=(wide,) * 6 + (lone, flat, flat, flat, lone),
        out_specs=(wide,) * 5,
        check_vma=False,
    )
```

```python
import functools
import math

import jax
import jax.numpy as jnp
from jax import lax
from jax.experimental import pallas as pl
from jax.experimental.pallas import tpu as pltpu
from jax.sharding import PartitionSpec as P

WIDTH = 128
TILE = 128
PAIR = 2 * WIDTH
NEAR_OUTS = 12
NEG = -1e30
SCALE = 1.0 / math.sqrt(WIDTH)
SCALE2 = SCALE * math.log2(math.e)
F32 = jnp.float32
BF16 = jnp.bfloat16


def dot_nt(a, b):
    return lax.dot_general(a, b, (((1,), (1,)), ((), ())), preferred_element_type=F32)


def dot_nn(a, b):
    return lax.dot_general(a, b, (((1,), (0,)), ((), ())), preferred_element_type=F32)


def dot_tn(a, b):
    return lax.dot_general(a, b, (((0,), (0,)), ((), ())), preferred_element_type=F32)


def repeat(steps, unroll, step):
    if unroll:
        for i in range(steps):
            step(i)
    else:

        def one(i, carry):
            step(i)
            return carry

        lax.fori_loop(0, steps, one, 0)


def added(steps, unroll, step, total_ref):
    if unroll:
        return functools.reduce(jnp.add, [step(i) for i in range(steps)])
    (total_ref,) = total_ref
    total_ref[...] = jnp.zeros_like(total_ref)

    def one(i):
        total_ref[...] += step(i)

    repeat(steps, unroll, one)
    return total_ref[...]


def columns(i, width):
    if isinstance(i, int):
        return pl.ds(i * width, width)
    return pl.ds(pl.multiple_of(i * width, width), width)


def pair_rows(ref, i):
    block = ref[:, columns(i, PAIR)]
    return jnp.concatenate([block[:, :WIDTH], block[:, WIDTH:]], axis=0)


def stacked_rows(ref, head, group):
    first = head * group
    return jnp.concatenate(
        [ref[:, (first + g) * WIDTH : (first + g + 1) * WIDTH] for g in range(group)], axis=0
    )


def twice(row):
    return jnp.concatenate([row, row], axis=1)


def tile_bias(table, first, tiles):
    return [twice(table[first + t : first + t + 1, :]) for t in range(tiles)]


def add_tiles(scores, biases):
    parts = [
        scores[t * TILE : (t + 1) * TILE, :] * SCALE2 + bias for t, bias in enumerate(biases)
    ]
    return parts[0] if len(parts) == 1 else jnp.concatenate(parts, axis=0)


def tail_bias(row_list):
    rows = row_list.shape[1]
    cut = jnp.sum((row_list == 0).astype(jnp.int32), axis=1, keepdims=True)
    key_at = lax.broadcasted_iota(jnp.int32, (rows, rows), 0)
    row_at = lax.broadcasted_iota(jnp.int32, (rows, rows), 1)
    allowed = ((key_at < cut) == (row_at < cut)) & (key_at <= row_at)
    return twice(jnp.where(allowed, 0.0, NEG).astype(F32))


def is_odd():
    return lax.rem(lax.axis_index("dp"), 2) == 1


def value_part_late():
    return jnp.logical_and(jnp.logical_not(is_odd()), lax.axis_index("ctx") > 0)


def load_copies(ins, q_ref, g_ref, k_ref, v_ref, small_refs, sems):
    q_in, g_in, tk_in, tv_in, ok_in, ov_in, *small_ins = ins
    tail = tk_in.shape[0]
    moves = list(zip(small_ins, small_refs)) + [
        (tk_in, k_ref.at[:tail]), (ok_in, k_ref.at[tail:]), (q_in, q_ref),
        (tv_in, v_ref.at[:tail]), (ov_in, v_ref.at[tail:]), (g_in, g_ref),
    ]
    copies = [pltpu.make_async_copy(a, b, sems.at[i]) for i, (a, b) in enumerate(moves)]
    for copy in copies:
        copy.start()
    return copies


def raw_scores(q_ref, k_ref, head, i, per_head):
    cols = slice(head * WIDTH, (head + 1) * WIDTH)
    return dot_nt(k_ref[:, cols], pair_rows(q_ref, head * per_head + i))


def near_raw_work(q_ref, k_ref, p_ref):
    heads = k_ref.shape[1] // WIDTH
    per_head = q_ref.shape[1] // PAIR // heads
    for head in range(heads):
        for i in range(per_head):
            p_ref[head, :, columns(i, PAIR)] = raw_scores(q_ref, k_ref, head, i, per_head)


def near_key_work(
    ctx, own, copies, q_ref, k_ref, p_ref, stats_ref, table_ref,
    rl_ref, ro_ref, rt_ref, rs_ref, rc_ref,
):
    for copy in copies[:4]:
        copy.wait()
    heads = k_ref.shape[1] // WIDTH
    per_head = q_ref.shape[1] // PAIR // heads
    reads = ro_ref.shape[1]
    slots = table_ref.shape[0]
    row_list = rl_ref[...]
    owner = ro_ref[...] - lax.axis_index("ctx")
    owner = jnp.where(owner < 0, owner + ctx, owner)
    wanted = owner * own + rt_ref[...]
    live = lax.broadcasted_iota(jnp.int32, (1, reads), 1) < rc_ref[0]
    wanted = jnp.where(live, wanted, -1)
    hit = lax.broadcasted_iota(jnp.int32, (slots, reads), 0) == wanted
    first = rs_ref[...] == 0
    count0 = jnp.sum(jnp.where(hit & first, 1.0, 0.0), axis=1, keepdims=True)
    count1 = jnp.sum(jnp.where(hit & jnp.logical_not(first), 1.0, 0.0), axis=1, keepdims=True)
    count = jnp.where(row_list == 0, count0, count1)
    table = jnp.where(count > 0.5, jnp.log2(jnp.maximum(count, 1.0)), NEG)
    table_ref[...] = table
    biases = [tail_bias(row_list)] + tile_bias(table, 0, own)
    for copy in copies[4:7]:
        copy.wait()
    for head in range(heads):
        for i in range(per_head):
            at = columns(head * per_head + i, PAIR)
            here = columns(i, PAIR)
            if copies:
                raw = raw_scores(q_ref, k_ref, head, i, per_head)
            else:
                raw = p_ref[head, :, here]
            s = add_tiles(raw, biases)
            top = jnp.max(s, axis=0, keepdims=True)
            p = jnp.exp2(s - top)
            p_ref[head, :, here] = p
            stats_ref[0:1, at] = top
            stats_ref[1:2, at] = jnp.sum(p, axis=0, keepdims=True)
    for copy in copies[7:]:
        copy.wait()


def near_dprob_work(g_ref, v_ref, d_ref):
    heads = v_ref.shape[1] // WIDTH
    per_head = g_ref.shape[1] // PAIR // heads
    for head in range(heads):
        for i in range(per_head):
            d_ref[head, :, columns(i, PAIR)] = raw_scores(g_ref, v_ref, head, i, per_head)


def near_cross_work(p_ref, d_ref, stats_ref):
    heads, _, group_rows = p_ref.shape
    for head in range(heads):
        for i in range(group_rows // PAIR):
            here = columns(i, PAIR)
            cross = jnp.sum(p_ref[head, :, here] * d_ref[head, :, here], axis=0, keepdims=True)
            stats_ref[2:3, columns(head * group_rows // PAIR + i, PAIR)] = cross


def near_value_work(g_ref, v_ref, p_ref, d_ref, stats_ref):
    heads = v_ref.shape[1] // WIDTH
    per_head = g_ref.shape[1] // PAIR // heads
    for head in range(heads):
        cols = slice(head * WIDTH, (head + 1) * WIDTH)
        for i in range(per_head):
            pair = head * per_head + i
            here = columns(i, PAIR)
            d = dot_nt(v_ref[:, cols], pair_rows(g_ref, pair))
            d_ref[head, :, here] = d
            cross = jnp.sum(p_ref[head, :, here] * d, axis=0, keepdims=True)
            stats_ref[2:3, columns(pair, PAIR)] = cross


def near_kernel(ctx, early, *refs):
    ins, rest = refs[:10], refs[10 if early else 11 + NEAR_OUTS :]
    q_ref, g_ref, k_ref, v_ref, *small_refs = rest[:8]
    p_ref, d_ref, stats_ref, table_ref, sems = rest[8:]

    def load():
        return load_copies(ins, q_ref, g_ref, k_ref, v_ref, small_refs, sems)

    if early:

        @pl.when(is_odd())
        def first_part():
            for copy in load():
                copy.wait()
            near_raw_work(q_ref, k_ref, p_ref)
            near_dprob_work(g_ref, v_ref, d_ref)

        return
    own = ins[4].shape[0] // TILE
    refs_of_keys = (q_ref, k_ref, p_ref, stats_ref, table_ref, *small_refs, refs[10])

    @pl.when(is_odd())
    def rest_of_it():
        near_key_work(ctx, own, [], *refs_of_keys)
        near_cross_work(p_ref, d_ref, stats_ref)

    @pl.when(jnp.logical_not(is_odd()))
    def key_part():
        near_key_work(ctx, own, load(), *refs_of_keys)

    @pl.when(jnp.logical_not(jnp.logical_or(is_odd(), value_part_late())))
    def value_part():
        near_value_work(g_ref, v_ref, p_ref, d_ref, stats_ref)


def far_key_kernel(
    unroll, q_ref, g_ref, k_ref, stats_ref, table_ref, back_ref, p_ref, fin_ref, *total_ref
):
    far_tiles = k_ref.shape[0] // TILE
    heads = k_ref.shape[1] // WIDTH
    per_head = q_ref.shape[1] // PAIR // heads
    shifts, own_keys, _ = back_ref.shape
    biases = tile_bias(table_ref[...], own_keys // TILE, far_tiles)
    for head in range(heads):
        cols = slice(head * WIDTH, (head + 1) * WIDTH)

        def step(i):
            pair = head * per_head + i
            at = columns(pair, PAIR)
            here = columns(i, PAIR)
            s = add_tiles(dot_nt(k_ref[:, cols], pair_rows(q_ref, pair)), biases)
            near_top = stats_ref[0:1, at]
            top = jnp.maximum(near_top, jnp.max(s, axis=0, keepdims=True))
            p = jnp.exp2(s - top)
            fade = jnp.exp2(near_top - top)
            inverse = 1.0 / (stats_ref[1:2, at] * fade + jnp.sum(p, axis=0, keepdims=True))
            fin_ref[0:1, at] = fade * inverse
            p = (p * inverse).astype(BF16)
            p_ref[head, :, here] = p
            return dot_nn(p, pair_rows(g_ref, pair))

        dv = added(per_head, unroll, step, total_ref).astype(BF16)
        for shift in range(shifts):
            back_ref[shift, :, cols] = dv[shift * own_keys : (shift + 1) * own_keys]


def late_near_kernel(after_ref, g_ref, v_ref, p_ref, d_in, stats_in, d_ref, stats_ref):
    @pl.when(value_part_late())
    def value_part():
        near_value_work(g_ref, v_ref, p_ref, d_ref, stats_ref)


def far_value_kernel(
    unroll, q_ref, g_ref, v_ref, p_ref, fin_ref, stats_ref, back_ref, ds_ref, delta_ref, *total_ref
):
    heads = v_ref.shape[1] // WIDTH
    per_head = q_ref.shape[1] // PAIR // heads
    shifts, own_keys, _ = back_ref.shape

    for head in range(heads):
        cols = slice(head * WIDTH, (head + 1) * WIDTH)

        def step(i):
            pair = head * per_head + i
            at = columns(pair, PAIR)
            here = columns(i, PAIR)
            d = dot_nt(v_ref[:, cols], pair_rows(g_ref, pair))
            p = p_ref[head, :, here].astype(F32)
            delta = stats_ref[2:3, at] * fin_ref[0:1, at] + jnp.sum(p * d, axis=0, keepdims=True)
            delta_ref[0:1, at] = delta
            ds = (p * (d - delta)).astype(BF16)
            ds_ref[head, :, here] = ds
            return dot_nn(ds, pair_rows(q_ref, pair))

        dk = (added(per_head, unroll, step, total_ref) * SCALE).astype(BF16)
        for shift in range(shifts):
            back_ref[shift, :, cols] = dk[shift * own_keys : (shift + 1) * own_keys]


def sum_kernel(after_ref, own_ref, *refs):
    total = own_ref[...]
    for ref in refs[:-1]:
        total = total + ref[...].astype(F32)
    refs[-1][...] = total


def last_kernel(
    unroll, q_ref, g_ref, k_ref, p_ref, d_ref, fin_ref, delta_ref, fk_ref, fds_ref,
    dq_ref, dtk_ref, dtv_ref, dok_ref, dov_ref, low_ref, ds_ref,
):
    tail = dtk_ref.shape[0]
    heads = k_ref.shape[1] // WIDTH
    per_head = q_ref.shape[1] // PAIR // heads
    for head in range(heads):
        cols = slice(head * WIDTH, (head + 1) * WIDTH)

        def step(i):
            pair = head * per_head + i
            at = columns(pair, PAIR)
            here = columns(i, PAIR)
            p = p_ref[head, :, here] * fin_ref[0:1, at]
            ds = (p * (d_ref[head, :, here] - delta_ref[0:1, at])).astype(BF16)
            low_ref[head, :, here] = p.astype(BF16)
            ds_ref[head, :, here] = ds
            dq = dot_tn(k_ref[:, cols], ds) + dot_tn(fk_ref[:, cols], fds_ref[head, :, here])
            dq = dq * SCALE
            dq = jnp.concatenate([dq[:, :WIDTH].T, dq[:, WIDTH:].T], axis=1)
            dq_ref[:, at] = dq.astype(BF16)

        repeat(per_head, unroll, step)
        dk = dot_nn(ds_ref[head], stacked_rows(q_ref, head, 2 * per_head)) * SCALE
        dv = dot_nn(low_ref[head], stacked_rows(g_ref, head, 2 * per_head))
        dtk_ref[:, cols] = dk[:tail].astype(BF16)
        dtv_ref[:, cols] = dv[:tail].astype(BF16)
        dok_ref[:, cols] = dk[tail:]
        dov_ref[:, cols] = dv[tail:]


def call(kernel, spaces, outs, scratch, flops, mib, *args, aliases={}):
    vmem = pl.BlockSpec(memory_space=pltpu.VMEM)
    moved = sum(a.size * a.dtype.itemsize for a in args) + sum(
        math.prod(o.shape) * jnp.dtype(o.dtype).itemsize for o in outs
    )
    return pl.pallas_call(
        kernel,
        out_shape=outs,
        in_specs=[pl.BlockSpec(memory_space=space) for space in spaces],
        out_specs=[vmem] * len(outs),
        scratch_shapes=scratch,
        input_output_aliases=aliases,
        compiler_params=pltpu.CompilerParams(vmem_limit_bytes=mib * 2**20),
        cost_estimate=pl.CostEstimate(flops=flops, bytes_accessed=moved, transcendentals=0),
    )(*args)


def body(q, g, tk, tv, ck, cv, row_list, read_owner, read_tile, read_list, read_count):
    ctx = lax.axis_size("ctx")
    rows, q_width = q.shape
    kv_width = tk.shape[1]
    heads = kv_width // WIDTH
    group_rows = rows * (q_width // kv_width)
    own_keys = ck.shape[0]
    own = own_keys // TILE
    far_keys = (ctx - 1) * own_keys
    near_keys = rows + own_keys
    slots = -(-ctx * own // 8) * 8
    unroll = ctx <= 2
    row_list = row_list.reshape(1, rows)

    def shifted(x, shift):
        return lax.ppermute(x, "ctx", [(o, (o - shift) % ctx) for o in range(ctx)])

    far_k = [shifted(ck, s) for s in range(1, ctx)]
    shape = jax.ShapeDtypeStruct
    product = 2 * q_width * rows * WIDTH
    small = read_owner.shape
    here = [
        pltpu.with_memory_space_constraint(a, pltpu.HBM)
        for a in (q, g, tk, tv, ck, cv, row_list, read_owner, read_tile, read_list)
    ]
    near_outs = [
        pltpu.VMEM(q.shape, BF16),
        pltpu.VMEM(g.shape, BF16),
        pltpu.VMEM((near_keys, kv_width), BF16),
        pltpu.VMEM((near_keys, kv_width), BF16),
        pltpu.VMEM(row_list.shape, jnp.int32),
        pltpu.VMEM(small, jnp.int32),
        pltpu.VMEM(small, jnp.int32),
        pltpu.VMEM(small, jnp.int32),
        pltpu.VMEM((heads, near_keys, group_rows), F32),
        pltpu.VMEM((heads, near_keys, group_rows), F32),
        pltpu.VMEM((8, heads * group_rows), F32),
        pltpu.VMEM((slots, rows), F32),
    ]
    sems = [pltpu.SemaphoreType.DMA((10,))]
    flops = product * near_keys // WIDTH
    hbm = [pltpu.HBM] * len(here)
    early = list(
        call(functools.partial(near_kernel, ctx, True), hbm, near_outs, sems, flops, 32, *here)
    )
    own_v, early[-1] = lax.optimization_barrier((cv, early[-1]))
    far_v = [shifted(own_v, s) for s in range(1, ctx)]
    early = [pltpu.with_memory_space_constraint(a, pltpu.VMEM) for a in early]
    q, g, near_k, near_v, _, _, _, _, near_p, near_d, stats, table = call(
        functools.partial(near_kernel, ctx, False),
        hbm + [pltpu.SMEM] + [pltpu.VMEM] * NEAR_OUTS,
        near_outs,
        sems,
        flops,
        32,
        *here, read_count, *early,
        aliases={len(here) + 1 + i: i for i in range(NEAR_OUTS)},
    )
    mib = 32 if unroll else 60
    total = [] if unroll else [pltpu.VMEM((far_keys, WIDTH), F32)]
    far_k = far_k[0] if ctx == 2 else jnp.concatenate(far_k, axis=0)
    back_v, far_p, fin = call(
        functools.partial(far_key_kernel, unroll),
        [pltpu.VMEM] * 5,
        [
            shape((ctx - 1, own_keys, kv_width), BF16),
            shape((heads, far_keys, group_rows), BF16),
            shape((8, heads * group_rows), F32),
        ],
        total,
        2 * product * far_keys // WIDTH,
        mib,
        q, g, far_k, stats, table,
    )
    returned_v = [shifted(back_v[s - 1], -s) for s in range(1, ctx)]
    far_v = far_v[0] if ctx == 2 else jnp.concatenate(far_v, axis=0)
    near_d, stats = (pltpu.with_memory_space_constraint(a, pltpu.VMEM) for a in (near_d, stats))
    near_d, stats = call(
        late_near_kernel,
        [pltpu.VMEM] * 6,
        [pltpu.VMEM(near_d.shape, F32), pltpu.VMEM(stats.shape, F32)],
        [],
        flops,
        32,
        fin, g, near_v, near_p, near_d, stats,
        aliases={4: 0, 5: 1},
    )
    back_k, far_ds, delta = call(
        functools.partial(far_value_kernel, unroll),
        [pltpu.VMEM] * 6,
        [
            shape((ctx - 1, own_keys, kv_width), BF16),
            shape((heads, far_keys, group_rows), BF16),
            shape((8, heads * group_rows), F32),
        ],
        total,
        2 * product * far_keys // WIDTH,
        mib,
        q, g, far_v, far_p, fin, stats,
    )
    returned_k = [shifted(back_k[s - 1], -s) for s in range(1, ctx)]
    dq, dtk, dtv, dok, dov = call(
        functools.partial(last_kernel, unroll),
        [pltpu.VMEM] * 9,
        [
            shape(q.shape, BF16),
            shape(tk.shape, BF16),
            shape(tv.shape, BF16),
            shape(ck.shape, F32),
            shape(cv.shape, F32),
        ],
        [pltpu.VMEM((heads, near_keys, group_rows), BF16)] * 2,
        product * (3 * near_keys + far_keys) // WIDTH,
        mib,
        q, g, near_k, near_p, near_d, fin, delta, far_k, far_ds,
    )

    def summed(after, own_sum, returned):
        return call(
            sum_kernel,
            [pltpu.HBM] + [pltpu.VMEM] * (1 + len(returned)),
            [shape(own_sum.shape, F32)],
            [],
            0,
            mib,
            pltpu.with_memory_space_constraint(after, pltpu.HBM), own_sum, *returned,
        )[0]

    dov = summed(dq, dov, returned_v)
    dok = summed(dov, dok, returned_k)
    return dq, dtk, dtv, dok, dov


def solution(mesh):
    wide = P(("dp", "ctx"), "tp")
    lone = P(("dp", "ctx"))
    flat = P(("dp", "ctx"), None)
    return jax.shard_map(
        body,
        mesh=mesh,
        in_specs=(wide,) * 6 + (lone, flat, flat, flat, lone),
        out_specs=(wide,) * 5,
        check_vma=False,
    )
```

```python
import functools
import math

import jax
import jax.numpy as jnp
from jax import lax
from jax.experimental import pallas as pl
from jax.experimental.pallas import tpu as pltpu
from jax.sharding import PartitionSpec as P

WIDTH = 128
TILE = 128
PAIR = 2 * WIDTH
NEAR_OUTS = 12
NEG = -1e30
SCALE = 1.0 / math.sqrt(WIDTH)
SCALE2 = SCALE * math.log2(math.e)
F32 = jnp.float32
BF16 = jnp.bfloat16


def dot_nt(a, b):
    return lax.dot_general(a, b, (((1,), (1,)), ((), ())), preferred_element_type=F32)


def dot_nn(a, b):
    return lax.dot_general(a, b, (((1,), (0,)), ((), ())), preferred_element_type=F32)


def dot_tn(a, b):
    return lax.dot_general(a, b, (((0,), (0,)), ((), ())), preferred_element_type=F32)


def repeat(steps, unroll, step):
    if unroll:
        for i in range(steps):
            step(i)
    else:

        def one(i, carry):
            step(i)
            return carry

        lax.fori_loop(0, steps, one, 0)


def added(steps, unroll, step, total_ref):
    if unroll:
        return functools.reduce(jnp.add, [step(i) for i in range(steps)])
    (total_ref,) = total_ref
    total_ref[...] = jnp.zeros_like(total_ref)

    def one(i):
        total_ref[...] += step(i)

    repeat(steps, unroll, one)
    return total_ref[...]


def columns(i, width):
    if isinstance(i, int):
        return pl.ds(i * width, width)
    return pl.ds(pl.multiple_of(i * width, width), width)


def pair_rows(ref, i):
    block = ref[:, columns(i, PAIR)]
    return jnp.concatenate([block[:, :WIDTH], block[:, WIDTH:]], axis=0)


def stacked_rows(ref, head, group):
    first = head * group
    return jnp.concatenate(
        [ref[:, (first + g) * WIDTH : (first + g + 1) * WIDTH] for g in range(group)], axis=0
    )


def twice(row):
    return jnp.concatenate([row, row], axis=1)


def tile_bias(table, first, tiles):
    return [twice(table[first + t : first + t + 1, :]) for t in range(tiles)]


def add_tiles(scores, biases):
    parts = [
        scores[t * TILE : (t + 1) * TILE, :] * SCALE2 + bias for t, bias in enumerate(biases)
    ]
    return parts[0] if len(parts) == 1 else jnp.concatenate(parts, axis=0)


def tail_bias(row_list):
    rows = row_list.shape[1]
    cut = jnp.sum((row_list == 0).astype(jnp.int32), axis=1, keepdims=True)
    key_at = lax.broadcasted_iota(jnp.int32, (rows, rows), 0)
    row_at = lax.broadcasted_iota(jnp.int32, (rows, rows), 1)
    allowed = ((key_at < cut) == (row_at < cut)) & (key_at <= row_at)
    return twice(jnp.where(allowed, 0.0, NEG).astype(F32))


def is_odd():
    return lax.rem(lax.axis_index("dp"), 2) == 1


def value_part_late():
    return jnp.logical_and(jnp.logical_not(is_odd()), lax.axis_index("ctx") > 0)


def load_copies(which, ins, q_ref, g_ref, k_ref, v_ref, small_refs, sems):
    q_in, g_in, tk_in, tv_in, ok_in, ov_in, *small_ins = ins
    tail = tk_in.shape[0]
    moves = list(zip(small_ins, small_refs)) + [
        (tk_in, k_ref.at[:tail]), (ok_in, k_ref.at[tail:]), (q_in, q_ref),
        (tv_in, v_ref.at[:tail]), (ov_in, v_ref.at[tail:]), (g_in, g_ref),
    ]
    copies = [pltpu.make_async_copy(*moves[i], sems.at[i]) for i in which]
    for copy in copies:
        copy.start()
    return copies


def raw_scores(q_ref, k_ref, head, i, per_head):
    cols = slice(head * WIDTH, (head + 1) * WIDTH)
    return dot_nt(k_ref[:, cols], pair_rows(q_ref, head * per_head + i))


def near_raw_work(q_ref, k_ref, p_ref):
    heads = k_ref.shape[1] // WIDTH
    per_head = q_ref.shape[1] // PAIR // heads
    for head in range(heads):
        for i in range(per_head):
            p_ref[head, :, columns(i, PAIR)] = raw_scores(q_ref, k_ref, head, i, per_head)


def near_key_work(
    ctx, own, copies, q_ref, k_ref, p_ref, stats_ref, table_ref,
    rl_ref, ro_ref, rt_ref, rs_ref, rc_ref,
):
    for copy in copies[:4]:
        copy.wait()
    heads = k_ref.shape[1] // WIDTH
    per_head = q_ref.shape[1] // PAIR // heads
    reads = ro_ref.shape[1]
    slots = table_ref.shape[0]
    row_list = rl_ref[...]
    owner = ro_ref[...] - lax.axis_index("ctx")
    owner = jnp.where(owner < 0, owner + ctx, owner)
    wanted = owner * own + rt_ref[...]
    live = lax.broadcasted_iota(jnp.int32, (1, reads), 1) < rc_ref[0]
    wanted = jnp.where(live, wanted, -1)
    hit = lax.broadcasted_iota(jnp.int32, (slots, reads), 0) == wanted
    first = rs_ref[...] == 0
    count0 = jnp.sum(jnp.where(hit & first, 1.0, 0.0), axis=1, keepdims=True)
    count1 = jnp.sum(jnp.where(hit & jnp.logical_not(first), 1.0, 0.0), axis=1, keepdims=True)
    count = jnp.where(row_list == 0, count0, count1)
    table = jnp.where(count > 0.5, jnp.log2(jnp.maximum(count, 1.0)), NEG)
    table_ref[...] = table
    biases = [tail_bias(row_list)] + tile_bias(table, 0, own)
    for head in range(heads):
        for i in range(per_head):
            at = columns(head * per_head + i, PAIR)
            here = columns(i, PAIR)
            if copies:
                raw = raw_scores(q_ref, k_ref, head, i, per_head)
            else:
                raw = p_ref[head, :, here]
            s = add_tiles(raw, biases)
            top = jnp.max(s, axis=0, keepdims=True)
            p = jnp.exp2(s - top)
            p_ref[head, :, here] = p
            stats_ref[0:1, at] = top
            stats_ref[1:2, at] = jnp.sum(p, axis=0, keepdims=True)
    for copy in copies[4:]:
        copy.wait()


def near_dprob_work(g_ref, v_ref, d_ref):
    heads = v_ref.shape[1] // WIDTH
    per_head = g_ref.shape[1] // PAIR // heads
    for head in range(heads):
        for i in range(per_head):
            d_ref[head, :, columns(i, PAIR)] = raw_scores(g_ref, v_ref, head, i, per_head)


def near_cross_work(p_ref, d_ref, stats_ref):
    heads, _, group_rows = p_ref.shape
    for head in range(heads):
        for i in range(group_rows // PAIR):
            here = columns(i, PAIR)
            cross = jnp.sum(p_ref[head, :, here] * d_ref[head, :, here], axis=0, keepdims=True)
            stats_ref[2:3, columns(head * group_rows // PAIR + i, PAIR)] = cross


def near_value_work(g_ref, v_ref, p_ref, d_ref, stats_ref):
    heads = v_ref.shape[1] // WIDTH
    per_head = g_ref.shape[1] // PAIR // heads
    for head in range(heads):
        cols = slice(head * WIDTH, (head + 1) * WIDTH)
        for i in range(per_head):
            pair = head * per_head + i
            here = columns(i, PAIR)
            d = dot_nt(v_ref[:, cols], pair_rows(g_ref, pair))
            d_ref[head, :, here] = d
            cross = jnp.sum(p_ref[head, :, here] * d, axis=0, keepdims=True)
            stats_ref[2:3, columns(pair, PAIR)] = cross


def near_kernel(ctx, early, *refs):
    ins, rest = refs[:10], refs[10 if early else 11 + NEAR_OUTS :]
    q_ref, g_ref, k_ref, v_ref, *small_refs = rest[:8]
    p_ref, d_ref, stats_ref, table_ref, sems = rest[8:]

    def load(which):
        return load_copies(which, ins, q_ref, g_ref, k_ref, v_ref, small_refs, sems)

    if early:

        @pl.when(is_odd())
        def first_part():
            for copy in load(range(10)):
                copy.wait()
            near_raw_work(q_ref, k_ref, p_ref)
            near_dprob_work(g_ref, v_ref, d_ref)

        @pl.when(jnp.logical_not(is_odd()))
        def keys_only():
            for copy in load((4, 5, 6)):
                copy.wait()

        return
    own = ins[4].shape[0] // TILE
    refs_of_keys = (q_ref, k_ref, p_ref, stats_ref, table_ref, *small_refs, refs[10])

    @pl.when(is_odd())
    def rest_of_it():
        near_key_work(ctx, own, [], *refs_of_keys)
        near_cross_work(p_ref, d_ref, stats_ref)

    @pl.when(jnp.logical_not(is_odd()))
    def key_part():
        near_key_work(ctx, own, load((0, 1, 2, 3, 7, 8, 9)), *refs_of_keys)

    @pl.when(jnp.logical_not(jnp.logical_or(is_odd(), value_part_late())))
    def value_part():
        near_value_work(g_ref, v_ref, p_ref, d_ref, stats_ref)


def far_key_kernel(
    unroll, q_ref, g_ref, k_ref, stats_ref, table_ref, back_ref, p_ref, fin_ref, *total_ref
):
    far_tiles = k_ref.shape[0] // TILE
    heads = k_ref.shape[1] // WIDTH
    per_head = q_ref.shape[1] // PAIR // heads
    shifts, own_keys, _ = back_ref.shape
    biases = tile_bias(table_ref[...], own_keys // TILE, far_tiles)
    for head in range(heads):
        cols = slice(head * WIDTH, (head + 1) * WIDTH)

        def step(i):
            pair = head * per_head + i
            at = columns(pair, PAIR)
            here = columns(i, PAIR)
            s = add_tiles(dot_nt(k_ref[:, cols], pair_rows(q_ref, pair)), biases)
            near_top = stats_ref[0:1, at]
            top = jnp.maximum(near_top, jnp.max(s, axis=0, keepdims=True))
            p = jnp.exp2(s - top)
            fade = jnp.exp2(near_top - top)
            inverse = 1.0 / (stats_ref[1:2, at] * fade + jnp.sum(p, axis=0, keepdims=True))
            fin_ref[0:1, at] = fade * inverse
            p = (p * inverse).astype(BF16)
            p_ref[head, :, here] = p
            return dot_nn(p, pair_rows(g_ref, pair))

        dv = added(per_head, unroll, step, total_ref).astype(BF16)
        for shift in range(shifts):
            back_ref[shift, :, cols] = dv[shift * own_keys : (shift + 1) * own_keys]


def late_near_kernel(after_ref, g_ref, v_ref, p_ref, d_in, stats_in, d_ref, stats_ref):
    @pl.when(value_part_late())
    def value_part():
        near_value_work(g_ref, v_ref, p_ref, d_ref, stats_ref)


def far_value_kernel(
    unroll, q_ref, g_ref, v_ref, p_ref, fin_ref, stats_ref, back_ref, ds_ref, delta_ref, *total_ref
):
    heads = v_ref.shape[1] // WIDTH
    per_head = q_ref.shape[1] // PAIR // heads
    shifts, own_keys, _ = back_ref.shape

    for head in range(heads):
        cols = slice(head * WIDTH, (head + 1) * WIDTH)

        def step(i):
            pair = head * per_head + i
            at = columns(pair, PAIR)
            here = columns(i, PAIR)
            d = dot_nt(v_ref[:, cols], pair_rows(g_ref, pair))
            p = p_ref[head, :, here].astype(F32)
            delta = stats_ref[2:3, at] * fin_ref[0:1, at] + jnp.sum(p * d, axis=0, keepdims=True)
            delta_ref[0:1, at] = delta
            ds = (p * (d - delta)).astype(BF16)
            ds_ref[head, :, here] = ds
            return dot_nn(ds, pair_rows(q_ref, pair))

        dk = (added(per_head, unroll, step, total_ref) * SCALE).astype(BF16)
        for shift in range(shifts):
            back_ref[shift, :, cols] = dk[shift * own_keys : (shift + 1) * own_keys]


def sum_kernel(after_ref, own_ref, *refs):
    total = own_ref[...]
    for ref in refs[:-1]:
        total = total + ref[...].astype(F32)
    refs[-1][...] = total


def last_kernel(
    unroll, q_ref, g_ref, k_ref, p_ref, d_ref, fin_ref, delta_ref, fk_ref, fds_ref,
    dq_ref, dtk_ref, dtv_ref, dok_ref, dov_ref, low_ref, ds_ref,
):
    tail = dtk_ref.shape[0]
    heads = k_ref.shape[1] // WIDTH
    per_head = q_ref.shape[1] // PAIR // heads
    for head in range(heads):
        cols = slice(head * WIDTH, (head + 1) * WIDTH)

        def step(i):
            pair = head * per_head + i
            at = columns(pair, PAIR)
            here = columns(i, PAIR)
            p = p_ref[head, :, here] * fin_ref[0:1, at]
            ds = (p * (d_ref[head, :, here] - delta_ref[0:1, at])).astype(BF16)
            low_ref[head, :, here] = p.astype(BF16)
            ds_ref[head, :, here] = ds
            dq = dot_tn(k_ref[:, cols], ds) + dot_tn(fk_ref[:, cols], fds_ref[head, :, here])
            dq = dq * SCALE
            dq = jnp.concatenate([dq[:, :WIDTH].T, dq[:, WIDTH:].T], axis=1)
            dq_ref[:, at] = dq.astype(BF16)

        repeat(per_head, unroll, step)
        dk = dot_nn(ds_ref[head], stacked_rows(q_ref, head, 2 * per_head)) * SCALE
        dv = dot_nn(low_ref[head], stacked_rows(g_ref, head, 2 * per_head))
        dtk_ref[:, cols] = dk[:tail].astype(BF16)
        dtv_ref[:, cols] = dv[:tail].astype(BF16)
        dok_ref[:, cols] = dk[tail:]
        dov_ref[:, cols] = dv[tail:]


def call(kernel, spaces, outs, scratch, flops, mib, *args, aliases={}):
    vmem = pl.BlockSpec(memory_space=pltpu.VMEM)
    moved = sum(a.size * a.dtype.itemsize for a in args) + sum(
        math.prod(o.shape) * jnp.dtype(o.dtype).itemsize for o in outs
    )
    return pl.pallas_call(
        kernel,
        out_shape=outs,
        in_specs=[pl.BlockSpec(memory_space=space) for space in spaces],
        out_specs=[vmem] * len(outs),
        scratch_shapes=scratch,
        input_output_aliases=aliases,
        compiler_params=pltpu.CompilerParams(vmem_limit_bytes=mib * 2**20),
        cost_estimate=pl.CostEstimate(flops=flops, bytes_accessed=moved, transcendentals=0),
    )(*args)


def body(q, g, tk, tv, ck, cv, row_list, read_owner, read_tile, read_list, read_count):
    ctx = lax.axis_size("ctx")
    rows, q_width = q.shape
    kv_width = tk.shape[1]
    heads = kv_width // WIDTH
    group_rows = rows * (q_width // kv_width)
    own_keys = ck.shape[0]
    own = own_keys // TILE
    far_keys = (ctx - 1) * own_keys
    near_keys = rows + own_keys
    slots = -(-ctx * own // 8) * 8
    unroll = ctx <= 2
    row_list = row_list.reshape(1, rows)

    def shifted(x, shift):
        return lax.ppermute(x, "ctx", [(o, (o - shift) % ctx) for o in range(ctx)])

    far_k = [shifted(ck, s) for s in range(1, ctx)]
    shape = jax.ShapeDtypeStruct
    product = 2 * q_width * rows * WIDTH
    small = read_owner.shape
    here = [
        pltpu.with_memory_space_constraint(a, pltpu.HBM)
        for a in (q, g, tk, tv, ck, cv, row_list, read_owner, read_tile, read_list)
    ]
    near_outs = [
        pltpu.VMEM(q.shape, BF16),
        pltpu.VMEM(g.shape, BF16),
        pltpu.VMEM((near_keys, kv_width), BF16),
        pltpu.VMEM((near_keys, kv_width), BF16),
        pltpu.VMEM(row_list.shape, jnp.int32),
        pltpu.VMEM(small, jnp.int32),
        pltpu.VMEM(small, jnp.int32),
        pltpu.VMEM(small, jnp.int32),
        pltpu.VMEM((heads, near_keys, group_rows), F32),
        pltpu.VMEM((heads, near_keys, group_rows), F32),
        pltpu.VMEM((8, heads * group_rows), F32),
        pltpu.VMEM((slots, rows), F32),
    ]
    sems = [pltpu.SemaphoreType.DMA((10,))]
    flops = product * near_keys // WIDTH
    hbm = [pltpu.HBM] * len(here)
    early = list(
        call(functools.partial(near_kernel, ctx, True), hbm, near_outs, sems, flops, 32, *here)
    )
    own_v, early[-1] = lax.optimization_barrier((cv, early[-1]))
    far_v = [shifted(own_v, s) for s in range(1, ctx)]
    early = [pltpu.with_memory_space_constraint(a, pltpu.VMEM) for a in early]
    q, g, near_k, near_v, _, _, _, _, near_p, near_d, stats, table = call(
        functools.partial(near_kernel, ctx, False),
        hbm + [pltpu.SMEM] + [pltpu.VMEM] * NEAR_OUTS,
        near_outs,
        sems,
        flops,
        32,
        *here, read_count, *early,
        aliases={len(here) + 1 + i: i for i in range(NEAR_OUTS)},
    )
    mib = 32 if unroll else 60
    total = [] if unroll else [pltpu.VMEM((far_keys, WIDTH), F32)]
    far_k = far_k[0] if ctx == 2 else jnp.concatenate(far_k, axis=0)
    back_v, far_p, fin = call(
        functools.partial(far_key_kernel, unroll),
        [pltpu.VMEM] * 5,
        [
            shape((ctx - 1, own_keys, kv_width), BF16),
            shape((heads, far_keys, group_rows), BF16),
            shape((8, heads * group_rows), F32),
        ],
        total,
        2 * product * far_keys // WIDTH,
        mib,
        q, g, far_k, stats, table,
    )
    returned_v = [shifted(back_v[s - 1], -s) for s in range(1, ctx)]
    far_v = far_v[0] if ctx == 2 else jnp.concatenate(far_v, axis=0)
    near_d, stats = (pltpu.with_memory_space_constraint(a, pltpu.VMEM) for a in (near_d, stats))
    near_d, stats = call(
        late_near_kernel,
        [pltpu.VMEM] * 6,
        [pltpu.VMEM(near_d.shape, F32), pltpu.VMEM(stats.shape, F32)],
        [],
        flops,
        32,
        fin, g, near_v, near_p, near_d, stats,
        aliases={4: 0, 5: 1},
    )
    back_k, far_ds, delta = call(
        functools.partial(far_value_kernel, unroll),
        [pltpu.VMEM] * 6,
        [
            shape((ctx - 1, own_keys, kv_width), BF16),
            shape((heads, far_keys, group_rows), BF16),
            shape((8, heads * group_rows), F32),
        ],
        total,
        2 * product * far_keys // WIDTH,
        mib,
        q, g, far_v, far_p, fin, stats,
    )
    returned_k = [shifted(back_k[s - 1], -s) for s in range(1, ctx)]
    dq, dtk, dtv, dok, dov = call(
        functools.partial(last_kernel, unroll),
        [pltpu.VMEM] * 9,
        [
            shape(q.shape, BF16),
            shape(tk.shape, BF16),
            shape(tv.shape, BF16),
            shape(ck.shape, F32),
            shape(cv.shape, F32),
        ],
        [pltpu.VMEM((heads, near_keys, group_rows), BF16)] * 2,
        product * (3 * near_keys + far_keys) // WIDTH,
        mib,
        q, g, near_k, near_p, near_d, fin, delta, far_k, far_ds,
    )

    def summed(after, own_sum, returned):
        return call(
            sum_kernel,
            [pltpu.HBM] + [pltpu.VMEM] * (1 + len(returned)),
            [shape(own_sum.shape, F32)],
            [],
            0,
            mib,
            pltpu.with_memory_space_constraint(after, pltpu.HBM), own_sum, *returned,
        )[0]

    dov = summed(dq, dov, returned_v)
    dok = summed(dov, dok, returned_k)
    return dq, dtk, dtv, dok, dov


def solution(mesh):
    wide = P(("dp", "ctx"), "tp")
    lone = P(("dp", "ctx"))
    flat = P(("dp", "ctx"), None)
    return jax.shard_map(
        body,
        mesh=mesh,
        in_specs=(wide,) * 6 + (lone, flat, flat, flat, lone),
        out_specs=(wide,) * 5,
        check_vma=False,
    )
```

```python
import functools
import math

import jax
import jax.numpy as jnp
from jax import lax
from jax.experimental import pallas as pl
from jax.experimental.pallas import tpu as pltpu
from jax.sharding import PartitionSpec as P

WIDTH = 128
TILE = 128
PAIR = 2 * WIDTH
NEAR_OUTS = 12
NEG = -1e30
SCALE = 1.0 / math.sqrt(WIDTH)
SCALE2 = SCALE * math.log2(math.e)
F32 = jnp.float32
BF16 = jnp.bfloat16


def dot_nt(a, b):
    return lax.dot_general(a, b, (((1,), (1,)), ((), ())), preferred_element_type=F32)


def dot_nn(a, b):
    return lax.dot_general(a, b, (((1,), (0,)), ((), ())), preferred_element_type=F32)


def dot_tn(a, b):
    return lax.dot_general(a, b, (((0,), (0,)), ((), ())), preferred_element_type=F32)


def repeat(steps, unroll, step):
    if unroll:
        for i in range(steps):
            step(i)
    else:

        def one(i, carry):
            step(i)
            return carry

        lax.fori_loop(0, steps, one, 0)


def columns(i, width):
    if isinstance(i, int):
        return pl.ds(i * width, width)
    return pl.ds(pl.multiple_of(i * width, width), width)


def pair_rows(ref, i):
    block = ref[:, columns(i, PAIR)]
    return jnp.concatenate([block[:, :WIDTH], block[:, WIDTH:]], axis=0)


def stacked_rows(ref, head, group):
    first = head * group
    return jnp.concatenate(
        [ref[:, (first + g) * WIDTH : (first + g + 1) * WIDTH] for g in range(group)], axis=0
    )


def twice(row):
    return jnp.concatenate([row, row], axis=1)


def tile_bias(table, first, tiles):
    return [twice(table[first + t : first + t + 1, :]) for t in range(tiles)]


def add_tiles(scores, biases):
    parts = [
        scores[t * TILE : (t + 1) * TILE, :] * SCALE2 + bias for t, bias in enumerate(biases)
    ]
    return parts[0] if len(parts) == 1 else jnp.concatenate(parts, axis=0)


def tail_bias(row_list):
    rows = row_list.shape[1]
    cut = jnp.sum((row_list == 0).astype(jnp.int32), axis=1, keepdims=True)
    key_at = lax.broadcasted_iota(jnp.int32, (rows, rows), 0)
    row_at = lax.broadcasted_iota(jnp.int32, (rows, rows), 1)
    allowed = ((key_at < cut) == (row_at < cut)) & (key_at <= row_at)
    return twice(jnp.where(allowed, 0.0, NEG).astype(F32))


def is_odd():
    return lax.rem(lax.axis_index("dp"), 2) == 1


def value_part_late():
    return jnp.logical_and(jnp.logical_not(is_odd()), lax.axis_index("ctx") > 0)


def load_copies(ins, q_ref, g_ref, k_ref, v_ref, small_refs, sems):
    q_in, g_in, tk_in, tv_in, ok_in, ov_in, *small_ins = ins
    tail = tk_in.shape[0]
    moves = list(zip(small_ins, small_refs)) + [
        (tk_in, k_ref.at[:tail]), (ok_in, k_ref.at[tail:]), (q_in, q_ref),
        (tv_in, v_ref.at[:tail]), (ov_in, v_ref.at[tail:]), (g_in, g_ref),
    ]
    copies = [pltpu.make_async_copy(a, b, sems.at[i]) for i, (a, b) in enumerate(moves)]
    for copy in copies:
        copy.start()
    return copies


def raw_scores(q_ref, k_ref, head, i, per_head):
    cols = slice(head * WIDTH, (head + 1) * WIDTH)
    return dot_nt(k_ref[:, cols], pair_rows(q_ref, head * per_head + i))


def near_raw_work(q_ref, k_ref, p_ref):
    heads = k_ref.shape[1] // WIDTH
    per_head = q_ref.shape[1] // PAIR // heads
    for head in range(heads):
        for i in range(per_head):
            p_ref[head, :, columns(i, PAIR)] = raw_scores(q_ref, k_ref, head, i, per_head)


def near_key_work(
    ctx, own, raw_made, q_ref, k_ref, p_ref, stats_ref, table_ref,
    rl_ref, ro_ref, rt_ref, rs_ref, rc_ref,
):
    heads = k_ref.shape[1] // WIDTH
    per_head = q_ref.shape[1] // PAIR // heads
    reads = ro_ref.shape[1]
    slots = table_ref.shape[0]
    row_list = rl_ref[...]
    owner = ro_ref[...] - lax.axis_index("ctx")
    owner = jnp.where(owner < 0, owner + ctx, owner)
    wanted = owner * own + rt_ref[...]
    live = lax.broadcasted_iota(jnp.int32, (1, reads), 1) < rc_ref[0]
    wanted = jnp.where(live, wanted, -1)
    hit = lax.broadcasted_iota(jnp.int32, (slots, reads), 0) == wanted
    first = rs_ref[...] == 0
    count0 = jnp.sum(jnp.where(hit & first, 1.0, 0.0), axis=1, keepdims=True)
    count1 = jnp.sum(jnp.where(hit & jnp.logical_not(first), 1.0, 0.0), axis=1, keepdims=True)
    count = jnp.where(row_list == 0, count0, count1)
    table = jnp.where(count > 0.5, jnp.log2(jnp.maximum(count, 1.0)), NEG)
    table_ref[...] = table
    biases = [tail_bias(row_list)] + tile_bias(table, 0, own)
    for head in range(heads):
        for i in range(per_head):
            at = columns(head * per_head + i, PAIR)
            here = columns(i, PAIR)
            if raw_made:
                raw = p_ref[head, :, here]
            else:
                raw = raw_scores(q_ref, k_ref, head, i, per_head)
            s = add_tiles(raw, biases)
            top = jnp.max(s, axis=0, keepdims=True)
            p = jnp.exp2(s - top)
            p_ref[head, :, here] = p
            stats_ref[0:1, at] = top
            stats_ref[1:2, at] = jnp.sum(p, axis=0, keepdims=True)


def near_dprob_work(g_ref, v_ref, d_ref):
    heads = v_ref.shape[1] // WIDTH
    per_head = g_ref.shape[1] // PAIR // heads
    for head in range(heads):
        for i in range(per_head):
            d_ref[head, :, columns(i, PAIR)] = raw_scores(g_ref, v_ref, head, i, per_head)


def near_cross_work(p_ref, d_ref, stats_ref):
    heads, _, group_rows = p_ref.shape
    for head in range(heads):
        for i in range(group_rows // PAIR):
            here = columns(i, PAIR)
            cross = jnp.sum(p_ref[head, :, here] * d_ref[head, :, here], axis=0, keepdims=True)
            stats_ref[2:3, columns(head * group_rows // PAIR + i, PAIR)] = cross


def near_value_work(g_ref, v_ref, p_ref, d_ref, stats_ref):
    heads = v_ref.shape[1] // WIDTH
    per_head = g_ref.shape[1] // PAIR // heads
    for head in range(heads):
        cols = slice(head * WIDTH, (head + 1) * WIDTH)
        for i in range(per_head):
            pair = head * per_head + i
            here = columns(i, PAIR)
            d = dot_nt(v_ref[:, cols], pair_rows(g_ref, pair))
            d_ref[head, :, here] = d
            cross = jnp.sum(p_ref[head, :, here] * d, axis=0, keepdims=True)
            stats_ref[2:3, columns(pair, PAIR)] = cross


def near_kernel(ctx, early, *refs):
    ins, rest = refs[:10], refs[10 if early else 11 + NEAR_OUTS :]
    q_ref, g_ref, k_ref, v_ref, *small_refs = rest[:8]
    p_ref, d_ref, stats_ref, table_ref, sems = rest[8:]

    def load():
        copies = load_copies(ins, q_ref, g_ref, k_ref, v_ref, small_refs, sems)
        for copy in copies:
            copy.wait()

    if early:

        @pl.when(is_odd())
        def first_part():
            load()
            near_raw_work(q_ref, k_ref, p_ref)
            near_dprob_work(g_ref, v_ref, d_ref)

        return
    own = ins[4].shape[0] // TILE
    refs_of_keys = (q_ref, k_ref, p_ref, stats_ref, table_ref, *small_refs, refs[10])

    @pl.when(is_odd())
    def rest_of_it():
        near_key_work(ctx, own, True, *refs_of_keys)
        near_cross_work(p_ref, d_ref, stats_ref)

    @pl.when(jnp.logical_not(is_odd()))
    def key_part():
        load()
        near_key_work(ctx, own, False, *refs_of_keys)

    @pl.when(jnp.logical_not(jnp.logical_or(is_odd(), value_part_late())))
    def value_part():
        near_value_work(g_ref, v_ref, p_ref, d_ref, stats_ref)


def far_key_kernel(
    unroll, q_ref, g_ref, k_ref, stats_ref, table_ref, back_ref, p_ref, fin_ref
):
    far_tiles = k_ref.shape[0] // TILE
    heads = k_ref.shape[1] // WIDTH
    per_head = q_ref.shape[1] // PAIR // heads
    shifts, own_keys, _ = back_ref.shape
    biases = tile_bias(table_ref[...], own_keys // TILE, far_tiles)
    for head in range(heads):
        cols = slice(head * WIDTH, (head + 1) * WIDTH)

        def step(i):
            pair = head * per_head + i
            at = columns(pair, PAIR)
            here = columns(i, PAIR)
            s = add_tiles(dot_nt(k_ref[:, cols], pair_rows(q_ref, pair)), biases)
            near_top = stats_ref[0:1, at]
            top = jnp.maximum(near_top, jnp.max(s, axis=0, keepdims=True))
            p = jnp.exp2(s - top)
            fade = jnp.exp2(near_top - top)
            inverse = 1.0 / (stats_ref[1:2, at] * fade + jnp.sum(p, axis=0, keepdims=True))
            fin_ref[0:1, at] = fade * inverse
            p_ref[head, :, here] = (p * inverse).astype(BF16)

        repeat(per_head, unroll, step)
        dv = dot_nn(p_ref[head], stacked_rows(g_ref, head, 2 * per_head)).astype(BF16)
        for shift in range(shifts):
            back_ref[shift, :, cols] = dv[shift * own_keys : (shift + 1) * own_keys]


def far_value_kernel(
    unroll, q_ref, g_ref, v_ref, p_ref, fin_ref, near_v_ref, near_p_ref, *refs
):
    d_ref, stats_ref, back_ref, ds_ref, delta_ref = refs[2:]
    heads = v_ref.shape[1] // WIDTH
    per_head = q_ref.shape[1] // PAIR // heads
    shifts, own_keys, _ = back_ref.shape

    @pl.when(value_part_late())
    def value_part():
        near_value_work(g_ref, near_v_ref, near_p_ref, d_ref, stats_ref)

    for head in range(heads):
        cols = slice(head * WIDTH, (head + 1) * WIDTH)

        def step(i):
            pair = head * per_head + i
            at = columns(pair, PAIR)
            here = columns(i, PAIR)
            d = dot_nt(v_ref[:, cols], pair_rows(g_ref, pair))
            p = p_ref[head, :, here].astype(F32)
            delta = stats_ref[2:3, at] * fin_ref[0:1, at] + jnp.sum(p * d, axis=0, keepdims=True)
            delta_ref[0:1, at] = delta
            ds_ref[head, :, here] = (p * (d - delta)).astype(BF16)

        repeat(per_head, unroll, step)
        dk = (dot_nn(ds_ref[head], stacked_rows(q_ref, head, 2 * per_head)) * SCALE).astype(BF16)
        for shift in range(shifts):
            back_ref[shift, :, cols] = dk[shift * own_keys : (shift + 1) * own_keys]


def sum_kernel(after_ref, own_ref, *refs):
    total = own_ref[...]
    for ref in refs[:-1]:
        total = total + ref[...].astype(F32)
    refs[-1][...] = total


def last_kernel(
    unroll, q_ref, g_ref, k_ref, p_ref, d_ref, fin_ref, delta_ref, fk_ref, fds_ref,
    dq_ref, dtk_ref, dtv_ref, dok_ref, dov_ref, low_ref, ds_ref,
):
    tail = dtk_ref.shape[0]
    heads = k_ref.shape[1] // WIDTH
    per_head = q_ref.shape[1] // PAIR // heads
    for head in range(heads):
        cols = slice(head * WIDTH, (head + 1) * WIDTH)

        def step(i):
            pair = head * per_head + i
            at = columns(pair, PAIR)
            here = columns(i, PAIR)
            p = p_ref[head, :, here] * fin_ref[0:1, at]
            ds = (p * (d_ref[head, :, here] - delta_ref[0:1, at])).astype(BF16)
            low_ref[head, :, here] = p.astype(BF16)
            ds_ref[head, :, here] = ds
            dq = dot_tn(k_ref[:, cols], ds) + dot_tn(fk_ref[:, cols], fds_ref[head, :, here])
            dq = dq * SCALE
            dq = jnp.concatenate([dq[:, :WIDTH].T, dq[:, WIDTH:].T], axis=1)
            dq_ref[:, at] = dq.astype(BF16)

        repeat(per_head, unroll, step)
        dk = dot_nn(ds_ref[head], stacked_rows(q_ref, head, 2 * per_head)) * SCALE
        dv = dot_nn(low_ref[head], stacked_rows(g_ref, head, 2 * per_head))
        dtk_ref[:, cols] = dk[:tail].astype(BF16)
        dtv_ref[:, cols] = dv[:tail].astype(BF16)
        dok_ref[:, cols] = dk[tail:]
        dov_ref[:, cols] = dv[tail:]


def call(kernel, spaces, outs, scratch, flops, mib, *args, aliases={}):
    vmem = pl.BlockSpec(memory_space=pltpu.VMEM)
    moved = sum(a.size * a.dtype.itemsize for a in args) + sum(
        math.prod(o.shape) * jnp.dtype(o.dtype).itemsize for o in outs
    )
    return pl.pallas_call(
        kernel,
        out_shape=outs,
        in_specs=[pl.BlockSpec(memory_space=space) for space in spaces],
        out_specs=[vmem] * len(outs),
        scratch_shapes=scratch,
        input_output_aliases=aliases,
        compiler_params=pltpu.CompilerParams(vmem_limit_bytes=mib * 2**20),
        cost_estimate=pl.CostEstimate(flops=flops, bytes_accessed=moved, transcendentals=0),
    )(*args)


def body(q, g, tk, tv, ck, cv, row_list, read_owner, read_tile, read_list, read_count):
    ctx = lax.axis_size("ctx")
    rows, q_width = q.shape
    kv_width = tk.shape[1]
    heads = kv_width // WIDTH
    group_rows = rows * (q_width // kv_width)
    own_keys = ck.shape[0]
    own = own_keys // TILE
    far_keys = (ctx - 1) * own_keys
    near_keys = rows + own_keys
    slots = -(-ctx * own // 8) * 8
    unroll = ctx <= 2
    row_list = row_list.reshape(1, rows)

    def shifted(x, shift):
        return lax.ppermute(x, "ctx", [(o, (o - shift) % ctx) for o in range(ctx)])

    far_k = [shifted(ck, s) for s in range(1, ctx)]
    shape = jax.ShapeDtypeStruct
    product = 2 * q_width * rows * WIDTH
    small = read_owner.shape
    here = [
        pltpu.with_memory_space_constraint(a, pltpu.HBM)
        for a in (q, g, tk, tv, ck, cv, row_list, read_owner, read_tile, read_list)
    ]
    near_outs = [
        pltpu.VMEM(q.shape, BF16),
        pltpu.VMEM(g.shape, BF16),
        pltpu.VMEM((near_keys, kv_width), BF16),
        pltpu.VMEM((near_keys, kv_width), BF16),
        pltpu.VMEM(row_list.shape, jnp.int32),
        pltpu.VMEM(small, jnp.int32),
        pltpu.VMEM(small, jnp.int32),
        pltpu.VMEM(small, jnp.int32),
        pltpu.VMEM((heads, near_keys, group_rows), F32),
        pltpu.VMEM((heads, near_keys, group_rows), F32),
        pltpu.VMEM((8, heads * group_rows), F32),
        pltpu.VMEM((slots, rows), F32),
    ]
    sems = [pltpu.SemaphoreType.DMA((10,))]
    flops = product * near_keys // WIDTH
    hbm = [pltpu.HBM] * len(here)
    early = list(
        call(functools.partial(near_kernel, ctx, True), hbm, near_outs, sems, flops, 32, *here)
    )
    own_v, early[-1] = lax.optimization_barrier((cv, early[-1]))
    far_v = [shifted(own_v, s) for s in range(1, ctx)]
    early = [pltpu.with_memory_space_constraint(a, pltpu.VMEM) for a in early]
    q, g, near_k, near_v, _, _, _, _, near_p, near_d, stats, table = call(
        functools.partial(near_kernel, ctx, False),
        hbm + [pltpu.SMEM] + [pltpu.VMEM] * NEAR_OUTS,
        near_outs,
        sems,
        flops,
        32,
        *here, read_count, *early,
        aliases={len(here) + 1 + i: i for i in range(NEAR_OUTS)},
    )
    mib = 32 if unroll else 60
    far_k = far_k[0] if ctx == 2 else jnp.concatenate(far_k, axis=0)
    back_v, far_p, fin = call(
        functools.partial(far_key_kernel, unroll),
        [pltpu.VMEM] * 5,
        [
            shape((ctx - 1, own_keys, kv_width), BF16),
            shape((heads, far_keys, group_rows), BF16),
            shape((8, heads * group_rows), F32),
        ],
        [],
        2 * product * far_keys // WIDTH,
        mib,
        q, g, far_k, stats, table,
    )
    returned_v = [shifted(back_v[s - 1], -s) for s in range(1, ctx)]
    far_v = far_v[0] if ctx == 2 else jnp.concatenate(far_v, axis=0)
    near_d, stats = (pltpu.with_memory_space_constraint(a, pltpu.VMEM) for a in (near_d, stats))
    near_d, stats, back_k, far_ds, delta = call(
        functools.partial(far_value_kernel, unroll),
        [pltpu.VMEM] * 9,
        [
            pltpu.VMEM(near_d.shape, F32),
            pltpu.VMEM(stats.shape, F32),
            shape((ctx - 1, own_keys, kv_width), BF16),
            shape((heads, far_keys, group_rows), BF16),
            shape((8, heads * group_rows), F32),
        ],
        [],
        2 * product * far_keys // WIDTH,
        mib,
        q, g, far_v, far_p, fin, near_v, near_p, near_d, stats,
        aliases={7: 0, 8: 1},
    )
    returned_k = [shifted(back_k[s - 1], -s) for s in range(1, ctx)]
    dq, dtk, dtv, dok, dov = call(
        functools.partial(last_kernel, unroll),
        [pltpu.VMEM] * 9,
        [
            shape(q.shape, BF16),
            shape(tk.shape, BF16),
            shape(tv.shape, BF16),
            shape(ck.shape, F32),
            shape(cv.shape, F32),
        ],
        [pltpu.VMEM((heads, near_keys, group_rows), BF16)] * 2,
        product * (3 * near_keys + far_keys) // WIDTH,
        mib,
        q, g, near_k, near_p, near_d, fin, delta, far_k, far_ds,
    )

    def summed(after, own_sum, returned):
        return call(
            sum_kernel,
            [pltpu.HBM] + [pltpu.VMEM] * (1 + len(returned)),
            [shape(own_sum.shape, F32)],
            [],
            0,
            mib,
            pltpu.with_memory_space_constraint(after, pltpu.HBM), own_sum, *returned,
        )[0]

    dov = summed(dq, dov, returned_v)
    dok = summed(dov, dok, returned_k)
    return dq, dtk, dtv, dok, dov


def solution(mesh):
    wide = P(("dp", "ctx"), "tp")
    lone = P(("dp", "ctx"))
    flat = P(("dp", "ctx"), None)
    return jax.shard_map(
        body,
        mesh=mesh,
        in_specs=(wide,) * 6 + (lone, flat, flat, flat, lone),
        out_specs=(wide,) * 5,
        check_vma=False,
    )
```
